32 devices in a mesh: replica: 2 (over y), shard: 16 (over z, x, core).
Axes of the slice: x: 2, y: 2, z: 4, core: 2. Of those that a mesh axis runs over, the one named last changes fastest.
Arguments:
- tokens: bfloat16 [320, 197, 384], P(('replica', 'shard')), may hold values from -6 to 6
- norm1_gain: bfloat16 [2, 384], P(None, 'shard'), may hold values from 0.5 to 1.5
- norm1_shift: bfloat16 [2, 384], P(None, 'shard'), may hold values from -3 to 3
- qkv_weight: bfloat16 [2, 384, 1152], P(None, 'shard'), may hold values from -0.3125 to 0.3125
- query_bias: bfloat16 [2, 384], P(None, 'shard'), may hold values from -3 to 3
- value_bias: bfloat16 [2, 384], P(None, 'shard'), may hold values from -3 to 3
- proj_weight: bfloat16 [2, 384, 384], P(None, 'shard'), may hold values from -1.25 to 1.25
- proj_bias: bfloat16 [2, 384], P(None, 'shard'), may hold values from -3 to 3
- norm2_gain: bfloat16 [2, 384], P(None, 'shard'), may hold values from 0.5 to 1.5
- norm2_shift: bfloat16 [2, 384], P(None, 'shard'), may hold values from -3 to 3
- fc1_weight: bfloat16 [2, 384, 1536], P(None, 'shard'), may hold values from -0.3125 to 0.3125
- fc1_bias: bfloat16 [2, 1536], P(None, 'shard'), may hold values from -3 to 3
- fc2_weight: bfloat16 [2, 1536, 384], P(None, 'shard'), may hold values from -0.15625 to 0.15625
- fc2_bias: bfloat16 [2, 384], P(None, 'shard'), may hold values from -3 to 3
- cotangent: bfloat16 [320, 197, 384], P(('replica', 'shard')), may hold values from -6 to 6
Outputs:
- layer_one: float32 [320, 197, 384], P(('replica', 'shard'))
- layer_two: float32 [320, 197, 384], P(('replica', 'shard'))
- tokens_grad: float32 [320, 197, 384], P(('replica', 'shard'))
- norm1_gain_grad: float32 [2, 384], P(None, 'shard')
- norm1_shift_grad: float32 [2, 384], P(None, 'shard')
- qkv_weight_grad: float32 [2, 384, 1152], P(None, 'shard')
- query_bias_grad: float32 [2, 384], P(None, 'shard')
- value_bias_grad: float32 [2, 384], P(None, 'shard')
- proj_weight_grad: float32 [2, 384, 384], P(None, 'shard')
- proj_bias_grad: float32 [2, 384], P(None, 'shard')
- norm2_gain_grad: float32 [2, 384], P(None, 'shard')
- norm2_shift_grad: float32 [2, 384], P(None, 'shard')
- fc1_weight_grad: float32 [2, 384, 1536], P(None, 'shard')
- fc1_bias_grad: float32 [2, 1536], P(None, 'shard')
- fc2_weight_grad: float32 [2, 1536, 384], P(None, 'shard')
- fc2_bias_grad: float32 [2, 384], P(None, 'shard')
The draws below stay inside these ranges and needn't reach their ends.
All inputs are finite; a program needn't handle non-finite values.
Results may differ from the reference program's by a relative error of at most 0.02.
Values may be sent and summed in bfloat16 or wider, within the bound.
No kernel may reach another device: no remote copies, remote signals or barrier semaphores. Data moves between devices by JAX's collectives and lax.ppermute only.
A program may use at most 256 MiB of HBM per device.

```python
import jax
import jax.numpy as jnp
from jax import lax

D = 384
HEADS = 6
FF = 1536
SEQ = 197
LAYERS = 2
IMG_DEV = 10
IMAGES = 320


def steps_of(stream_key, dims, shards, least, top_value):
    level, own = 1.0, jax.random.fold_in(stream_key, 6)
    for dim, blocks in shards:
        heights = jnp.exp(jax.random.uniform(jax.random.fold_in(own, dim), (blocks,), jnp.float32, least / len(shards), top_value / len(shards)))
        level = level * jnp.repeat(heights, dims[dim] // blocks).reshape([-1 if axis == dim else 1 for axis in range(len(dims))])
    return level


def scatter_about(own_key, dims, scale, reach, cuts=(), held_as=jnp.bfloat16):
    drawn = jax.random.normal(own_key, dims, jnp.float32) * scale
    if len(cuts) > 0:
        drawn = steps_of(own_key, dims, cuts, -0.22, 0.18) * drawn
    return jnp.clip(drawn, min=-reach, max=reach).astype(held_as)


def setup_inputs(seed: int = 0) -> dict:
    splits = jax.random.split(jax.random.key(seed), 16)
    return {
        "tokens": scatter_about(splits[0], (IMAGES, SEQ, D), 1.0, 6.0, ((0, 32),)),
        "norm1_gain": jnp.clip(0.5 + 1.0 * jax.random.uniform(splits[1], (LAYERS, D), jnp.float32) ** steps_of(splits[1], (LAYERS, D), ((1, 16),), -0.2, 0.2), 0.5, 1.5).astype(jnp.bfloat16),
        "norm1_shift": scatter_about(splits[2], (LAYERS, D), 0.5, 3.0, ((1, 16),)),
        "qkv_weight": scatter_about(splits[3], (LAYERS, D, 3 * D), D ** -0.5, 0.3125, ((1, 16),)),
        "query_bias": scatter_about(splits[4], (LAYERS, D), 0.5, 3.0, ((1, 16),)),
        "value_bias": scatter_about(splits[5], (LAYERS, D), 0.25, 3.0, ((1, 16),)),
        "proj_weight": scatter_about(splits[6], (LAYERS, D, D), (D // 16) ** -0.5, 1.25, ((1, 16),)),
        "proj_bias": scatter_about(splits[7], (LAYERS, D), 0.5, 3.0, ((1, 16),)),
        "norm2_gain": jnp.clip(0.5 + 1.0 * jax.random.uniform(splits[8], (LAYERS, D), jnp.float32) ** steps_of(splits[8], (LAYERS, D), ((1, 16),), -0.2, 0.2), 0.5, 1.5).astype(jnp.bfloat16),
        "norm2_shift": scatter_about(splits[9], (LAYERS, D), 0.5, 3.0, ((1, 16),)),
        "fc1_weight": scatter_about(splits[10], (LAYERS, D, FF), D ** -0.5, 0.3125, ((1, 16),)),
        "fc1_bias": scatter_about(splits[11], (LAYERS, FF), 0.5, 3.0, ((1, 16),)),
        "fc2_weight": scatter_about(splits[12], (LAYERS, FF, D), FF ** -0.5, 0.15625, ((1, 16),)),
        "fc2_bias": scatter_about(splits[13], (LAYERS, D), 0.5, 3.0, ((1, 16),)),
        "cotangent": scatter_about(splits[14], (IMAGES, SEQ, D), 1.0, 6.0, ((0, 32),)),
    }


EPS = 1e-06

@jax.custom_vjp
def low(v):
    return lax.optimization_barrier(v.astype(jnp.bfloat16)).astype(jnp.float32)

@jax.custom_vjp
def low_back(v):
    return v

def low_keep(v):
    return (low(v), None)

def low_pass(kept, grad):
    return (grad,)

def back_keep(v):
    return (v, None)

def back_low(kept, grad):
    return (low(grad),)
low.defvjp(low_keep, low_pass)
low_back.defvjp(back_keep, back_low)

def layer_norm(values, gain_row, shift_row):
    average = lax.optimization_barrier(jnp.mean(values, -1, keepdims=True))
    centred = values - average
    spread = lax.optimization_barrier(jnp.mean(centred * centred, -1, keepdims=True))
    return centred * lax.rsqrt(spread + EPS) * gain_row + shift_row

def project(left, right):
    return jnp.einsum('bsd,de->bse', left, right, precision=lax.Precision.HIGHEST)

def block(inputs, weights):
    gain_one, shift_one, w_qkv, bias_query, bias_value, w_proj, bias_proj, gain_two, shift_two, w_up, bias_up, w_down, bias_down = weights
    images, length, width = inputs.shape
    head_dim = width // HEADS
    normed = low(layer_norm(inputs, gain_one, shift_one))
    mixed = project(normed, w_qkv)
    mixed = mixed + jnp.concatenate([bias_query, jnp.zeros_like(bias_query), bias_value])
    mixed = low(low_back(mixed))
    query_heads = mixed[..., :width].reshape(images, length, HEADS, head_dim)
    key_heads = mixed[..., width:2 * width].reshape(images, length, HEADS, head_dim)
    value_heads = mixed[..., 2 * width:].reshape(images, length, HEADS, head_dim)
    scores = jnp.einsum('bqhd,bkhd->bhqk', query_heads, key_heads, precision=lax.Precision.HIGHEST)
    scores = low_back(scores * head_dim ** (-0.5))
    probs = jax.nn.softmax(scores, axis=-1)
    attended = jnp.einsum('bhqk,bkhd->bqhd', low(probs), value_heads, precision=lax.Precision.HIGHEST)
    attended = low(low_back(attended.reshape(images, length, width)))
    branch = low_back(project(attended, w_proj) + bias_proj)
    middle = inputs + branch
    normed_two = low(layer_norm(middle, gain_two, shift_two))
    hidden = low_back(project(normed_two, w_up) + bias_up)
    active = low(jax.nn.gelu(hidden, approximate=False))
    branch_two = low_back(project(active, w_down) + bias_down)
    return middle + branch_two

def forward(inputs, weights):
    first_out = block(inputs, tuple((weight_arr[0] for weight_arr in weights)))
    second_out = block(first_out, tuple((weight_arr[1] for weight_arr in weights)))
    return (second_out, first_out)

def reference(tokens, norm1_gain, norm1_shift, qkv_weight, query_bias, value_bias, proj_weight, proj_bias, norm2_gain, norm2_shift, fc1_weight, fc1_bias, fc2_weight, fc2_bias, cotangent):
    weights = tuple((weight_arr.astype(jnp.float32) for weight_arr in (norm1_gain, norm1_shift, qkv_weight, query_bias, value_bias, proj_weight, proj_bias, norm2_gain, norm2_shift, fc1_weight, fc1_bias, fc2_weight, fc2_bias)))
    images_all = tokens.shape[0]
    groups = images_all // IMG_DEV
    inputs = tokens.astype(jnp.float32).reshape(groups, IMG_DEV, SEQ, D)
    cotangents = cotangent.astype(jnp.float32).reshape(groups, IMG_DEV, SEQ, D)

    def one_block(totals, block_pair):
        block_in, block_cot = block_pair

        def wrapped(entry_rows, *params):
            return forward(entry_rows, params)
        second_out, pullback, first_out = jax.vjp(wrapped, block_in, *weights, has_aux=True)
        gradients = pullback(block_cot)
        summed = tuple((running + extra for running, extra in zip(totals, gradients[1:])))
        return (summed, (first_out, second_out, gradients[0]))
    start_totals = tuple((jnp.zeros_like(weight_arr) for weight_arr in weights))
    totals, (firsts, seconds, input_grads) = lax.scan(one_block, start_totals, (inputs, cotangents))
    full_shape = (images_all, SEQ, D)
    return (firsts.reshape(full_shape), seconds.reshape(full_shape), input_grads.reshape(full_shape), totals[0], totals[1], totals[2], totals[3], totals[4], totals[5], totals[6], totals[7], totals[8], totals[9], totals[10], totals[11], totals[12])
```

```python
import functools
import jax
import jax.numpy as jnp
from jax import lax
from jax.sharding import PartitionSpec as P
from jax.experimental import pallas as pl
from jax.experimental.pallas import tpu as pltpu

BF = jnp.bfloat16
F32 = jnp.float32
HEADS = 6
EPS = 1e-06
NEG = -1e30
LOG2E = 1.4426950408889634


def dot(a, b):
    return jnp.dot(a, b, preferred_element_type=F32)


def dot_nt(a, b):
    return lax.dot_general(a, b, (((1,), (1,)), ((), ())), preferred_element_type=F32)


def dot_tn(a, b):
    return lax.dot_general(a, b, (((0,), (0,)), ((), ())), preferred_element_type=F32)


def pad_rows(seq):
    return (seq + 15) // 16 * 16


def normalise(x):
    mean = jnp.mean(x, -1, keepdims=True)
    cen = x - mean
    rstd = lax.rsqrt(jnp.mean(cen * cen, -1, keepdims=True) + EPS)
    return cen * rstd, rstd


def norm_back(dxhat, xhat, rstd):
    return rstd * (
        dxhat
        - jnp.mean(dxhat, -1, keepdims=True)
        - xhat * jnp.mean(dxhat * xhat, -1, keepdims=True)
    )


def gelu_both(h):
    ax = jnp.abs(h) * 0.7071067811865476
    t = 1.0 / (1.0 + 0.3275911 * ax)
    e = jnp.exp(h * h * -0.5)
    poly = t * (0.127414796 + t * (-0.142248368 + t * (0.7107068705 + t * (-0.7265760135 + t * 0.5307027145))))
    tail = poly * e
    phi = jnp.where(h >= 0, 1.0 - tail, tail)
    return h * phi, phi + h * e * 0.3989422804014327


def load_padded(dst, src, seq, rows, images):
    for g in range(images):
        dst[g * rows : g * rows + seq] = src[g].astype(F32)
        dst[g * rows + seq : (g + 1) * rows] = jnp.zeros((rows - seq, dst.shape[1]), F32)


def fa_kernel(seq, x_ref, vec, wqkv, wp, m_ref, o_ref, aux_ref, xh_ref, x1_ref, xs):
    images = x_ref.shape[0]
    rows = pad_rows(seq)
    width = x_ref.shape[2]
    load_padded(xs, x_ref, seq, rows, images)
    xhat, rstd = normalise(xs[...])
    xh_ref[...] = xhat.astype(BF).reshape(images, rows, width)
    n1 = (xhat * vec[0:1, :] + vec[1:2, :]).astype(BF)
    for c in range(3):
        cs = slice(c * width, (c + 1) * width)
        mc = dot(n1, wqkv[:, cs])
        if c != 1:
            mc = mc + (vec[2:3, :] if c == 0 else vec[3:4, :])
        m_ref[:, :, cs] = mc.astype(BF).reshape(images, rows, width)
    lane = lax.broadcasted_iota(jnp.int32, (rows, 128), 1)
    row = lax.broadcasted_iota(jnp.int32, (rows, 128), 0)
    low = lane < 64
    kpad = jnp.where(row >= seq, NEG, 0.0).astype(BF)
    ones = jnp.where(row >= seq, 0.0, 1.0).astype(BF)
    qone0 = jnp.where(lane == 64, 1.0, 0.0).astype(BF)
    qone1 = jnp.where(lane == 0, 1.0, 0.0).astype(BF)
    valid = row < seq
    for g in range(images):
        aux = jnp.broadcast_to(rstd[g * rows : (g + 1) * rows], (rows, 128))
        for p in range(width // 128):
            q2 = m_ref[g, :, p * 128 : (p + 1) * 128] * jnp.asarray(0.125, BF)
            k2 = m_ref[g, :, width + p * 128 : width + (p + 1) * 128]
            v2 = m_ref[g, :, 2 * width + p * 128 : 2 * width + (p + 1) * 128]
            v2 = jnp.where(valid, v2, jnp.zeros_like(v2))
            vext = jnp.concatenate([v2, ones], 1)
            parts = []
            for half in range(2):
                mine = low if half == 0 else ~low
                qh = jnp.where(mine, q2, qone0 if half == 0 else qone1)
                kh = jnp.where(mine, k2, kpad)
                s = dot_nt(qh, kh)
                mx = jnp.max(s, -1, keepdims=True)
                pr = jnp.exp(s - mx).astype(BF)
                oe = dot(pr, vext)
                tot = oe[:, 128:]
                parts.append(oe[:, :128] / tot)
                aux = jnp.where(lane == 2 * p + half, mx + jnp.log(tot), aux)
            o_ref[g, :, p * 128 : (p + 1) * 128] = jnp.where(low, parts[0], parts[1]).astype(BF)
        aux_ref[g] = aux
    of = o_ref[...].reshape(images * rows, width)
    x1 = xs[...] + dot(of, wp[...]) + vec[4:5, :]
    x1_ref[...] = x1.reshape(images, rows, width)


def fm_kernel(seq, x1_ref, vec, w1, w2, out_ref, a_ref, d_ref, xh_ref, rs_ref, *, chunk=512):
    images, rows, width = x1_ref.shape
    x1 = x1_ref[...].reshape(images * rows, width)
    xhat, rstd = normalise(x1)
    xh_ref[...] = xhat.astype(BF).reshape(images, rows, width)
    rs_ref[...] = jnp.broadcast_to(rstd, (images * rows, 128)).reshape(images, rows, 128)
    n2 = (xhat * vec[5:6, :] + vec[6:7, :]).astype(BF)
    acc = x1 + vec[7:8, :]
    bias = jnp.concatenate([vec[r : r + 1, :] for r in range(8, 8 + w1.shape[1] // width)], 1)
    for c in range(w1.shape[1] // chunk):
        cs = slice(c * chunk, (c + 1) * chunk)
        h = dot(n2, w1[:, cs]) + bias[:, cs]
        a, d = gelu_both(h)
        a = a.astype(BF)
        a_ref[:, :, cs] = a.reshape(images, rows, chunk)
        d_ref[:, :, cs] = d.astype(BF).reshape(images, rows, chunk)
        acc = acc + dot(a, w2[cs, :])
    acc = acc.reshape(images, rows, width)
    for g in range(images):
        out_ref[g] = acc[g, :seq]


def colsum(x):
    return jnp.sum(x, 0, keepdims=True)


def bm_kernel(seq, gr_ref, a_ref, d_ref, xh_ref, rs_ref, vec, w1, w2,
              dx1_ref, dw1_o, dw2_o, vec_o, db1_o, gs, dw1, dw2, *, chunk=512):
    images, rows, width = xh_ref.shape
    n = images * rows
    step = pl.program_id(0)

    @pl.when(step == 0)
    def _():
        dw1[...] = jnp.zeros_like(dw1)
        dw2[...] = jnp.zeros_like(dw2)
        vec_o[...] = jnp.zeros_like(vec_o)
        db1_o[...] = jnp.zeros_like(db1_o)

    load_padded(gs, gr_ref, seq, rows, images)
    dz = gs[...].astype(BF)
    xhat = xh_ref[...].reshape(n, width).astype(F32)
    n2 = (xhat * vec[5:6, :] + vec[6:7, :]).astype(BF)
    dn2 = jnp.zeros((n, width), F32)
    for c in range(w1.shape[1] // chunk):
        cs = slice(c * chunk, (c + 1) * chunk)
        a = a_ref[:, :, cs].reshape(n, chunk)
        d = d_ref[:, :, cs].reshape(n, chunk)
        da = dot_nt(dz, w2[cs, :])
        dhf = d.astype(F32) * da
        dh = dhf.astype(BF)
        db1_o[:, cs] += colsum(dh.astype(F32))
        dw2[cs, :] += dot_tn(a, dz)
        dw1[:, cs] += dot_tn(n2, dh)
        dn2 = dn2 + dot_nt(dh, w1[:, cs])
    vec_o[0:1, :] += colsum(dz.astype(F32))
    vec_o[1:2, :] += colsum(dn2 * xhat)
    vec_o[2:3, :] += colsum(dn2)
    rs = rs_ref[...].reshape(n, 128)
    rstd = jnp.concatenate([rs] * (width // 128), 1)
    dx1 = gs[...] + norm_back(dn2 * vec[5:6, :], xhat, rstd)
    dx1_ref[...] = dx1.reshape(images, rows, width)

    @pl.when(step == pl.num_programs(0) - 1)
    def _():
        dw1_o[...] = dw1[...].astype(BF)
        dw2_o[...] = dw2[...].astype(BF)


def ba_kernel(seq, dx1_ref, m_ref, o_ref, aux_ref, xh_ref, vec, wqkv, wp,
              dx_ref, dwqkv_o, dwp_o, vec_o, dbm_o, dm, do, dwqkv, dwp):
    images, rows, width = xh_ref.shape
    n = images * rows
    step = pl.program_id(0)

    @pl.when(step == 0)
    def _():
        dwqkv[...] = jnp.zeros_like(dwqkv)
        dwp[...] = jnp.zeros_like(dwp)
        vec_o[...] = jnp.zeros_like(vec_o)
        dbm_o[...] = jnp.zeros_like(dbm_o)

    dx1 = dx1_ref[...].reshape(n, width)
    dy = dx1.astype(BF)
    of = o_ref[...].reshape(n, width)
    vec_o[0:1, :] += colsum(dy.astype(F32))
    dwp[...] += dot_tn(of, dy)
    do[...] = dot_nt(dy, wp[...]).astype(BF)
    lane = lax.broadcasted_iota(jnp.int32, (rows, 128), 1)
    row = lax.broadcasted_iota(jnp.int32, (rows, 128), 0)
    low = lane < 64
    kpad = jnp.where(row >= seq, NEG, 0.0).astype(BF)
    for g in range(images):
        aux = aux_ref[g]
        for p in range(width // 128):
            ps = slice(p * 128, (p + 1) * 128)
            q2 = m_ref[g, :, p * 128 : (p + 1) * 128] * jnp.asarray(0.125, BF)
            k2 = m_ref[g, :, width + p * 128 : width + (p + 1) * 128]
            v2 = m_ref[g, :, 2 * width + p * 128 : 2 * width + (p + 1) * 128]
            do2 = do[g * rows : (g + 1) * rows, ps]
            prod = o_ref[g, :, ps].astype(F32) * do2.astype(F32)
            outs = []
            for half in range(2):
                mine = low if half == 0 else ~low
                base = 64 if half == 0 else 0
                lse = aux[:, 2 * p + half : 2 * p + half + 1]
                l0 = (-lse).astype(BF)
                r1 = -lse - l0.astype(F32)
                l1 = r1.astype(BF)
                l2 = (r1 - l1.astype(F32)).astype(BF)
                dd = -jnp.sum(jnp.where(mine, prod, 0.0), -1, keepdims=True)
                d0 = dd.astype(BF)
                d1 = (dd - d0.astype(F32)).astype(BF)
                zero = jnp.zeros((rows, 128), BF)
                one = jnp.ones((rows, 128), BF)
                qx = jnp.where(lane == base, l0, jnp.where(lane == base + 1, l1, jnp.where(lane == base + 2, l2, jnp.where(lane == base + 3, one, zero))))
                kx = jnp.where((lane >= base) & (lane < base + 3), one, jnp.where(lane == base + 3, kpad, zero))
                dx_ = jnp.where(lane == base, d0, jnp.where(lane == base + 1, d1, zero))
                qh = jnp.where(mine, q2, qx)
                kh = jnp.where(mine, k2, kx)
                doh = jnp.where(mine, do2, dx_)
                vh = jnp.where(mine, v2, jnp.where((lane >= base) & (lane < base + 2), one, zero))
                st = dot_nt(kh, qh)
                pt = jnp.exp(st)
                dpt = dot_nt(vh, doh)
                dst = (pt * dpt).astype(BF)
                dv = dot(pt.astype(BF), do2)
                dk = dot(dst, q2)
                dq = dot_tn(dst, k2) * 0.125
                outs.append((dq, dk, dv))
            for j in range(3):
                val = jnp.where(low, outs[0][j], outs[1][j]).astype(BF)
                dm[g * rows : (g + 1) * rows, j * width + p * 128 : j * width + (p + 1) * 128] = val
    dbm_o[...] += colsum(dm[...].astype(F32))
    xhat = xh_ref[...].reshape(n, width).astype(F32)
    n1 = (xhat * vec[0:1, :] + vec[1:2, :]).astype(BF)
    for c in range(3):
        cs = slice(c * width, (c + 1) * width)
        dwqkv[:, cs] += dot_tn(n1, dm[:, cs])
    dn1 = dot_nt(dm[...], wqkv[...])
    vec_o[1:2, :] += colsum(dn1 * xhat)
    vec_o[2:3, :] += colsum(dn1)
    rstd = aux_ref[...].reshape(n, 128)[:, 127:128]
    dx = dx1 + norm_back(dn1 * vec[0:1, :], xhat, rstd)
    dx = dx.reshape(images, rows, width)
    for g in range(images):
        dx_ref[g] = dx[g, :seq]

    @pl.when(step == pl.num_programs(0) - 1)
    def _():
        dwqkv_o[...] = dwqkv[...].astype(BF)
        dwp_o[...] = dwp[...].astype(BF)


VMEM_LIMIT = 60 * 2**20


def blk(shape):
    nd = len(shape)
    return pl.BlockSpec(shape, lambda i: (i,) + (0,) * (nd - 1))


def whole(arr):
    nd = len(arr.shape)
    return pl.BlockSpec(arr.shape, lambda i: (0,) * nd)


def sds(shape, dt):
    return jax.ShapeDtypeStruct(shape, dt)


def call(kern, grid, blocked_in, whole_in, blocked_out, whole_out, scratch, per, name=None, flops=0):
    in_specs = [blk((per,) + a.shape[1:]) for a in blocked_in] + [whole(a) for a in whole_in]
    out_specs = [blk((per,) + a.shape[1:]) for a in blocked_out] + [whole(a) for a in whole_out]
    return pl.pallas_call(
        kern,
        grid=(grid,),
        in_specs=in_specs,
        out_specs=out_specs,
        out_shape=list(blocked_out) + list(whole_out),
        scratch_shapes=scratch,
        compiler_params=pltpu.CompilerParams(vmem_limit_bytes=VMEM_LIMIT),
        name=name,
        cost_estimate=pl.CostEstimate(flops=flops, bytes_accessed=0, transcendentals=0),
    )(*blocked_in, *whole_in)


def run_fa(x, vec, wqkv, wp, per):
    images, seq, width = x.shape
    rows = pad_rows(seq)
    return call(
        functools.partial(fa_kernel, seq), images // per, [x], [vec, wqkv, wp],
        [sds((images, rows, 3 * width), BF), sds((images, rows, width), BF), sds((images, rows, 128), F32),
         sds((images, rows, width), BF), sds((images, rows, width), F32)], [],
        [pltpu.VMEM((per * rows, width), F32)], per, "fa")


def run_fm(seq, x1, vec, w1, w2, per):
    images, rows, width = x1.shape
    ff = w1.shape[1]
    return call(
        functools.partial(fm_kernel, seq), images // per, [x1], [vec, w1, w2],
        [sds((images, seq, width), F32), sds((images, rows, ff), BF), sds((images, rows, ff), BF),
         sds((images, rows, width), BF), sds((images, rows, 128), F32)], [], [], per, "fm")


def run_bm(gr, a, d, xh, rs, vec, w1, w2, per):
    images, seq, width = gr.shape
    rows = a.shape[1]
    ff = w1.shape[1]
    return call(
        functools.partial(bm_kernel, seq), images // per, [gr, a, d, xh, rs], [vec, w1, w2],
        [sds((images, rows, width), F32)],
        [sds((width, ff), BF), sds((ff, width), BF), sds((8, width), F32), sds((1, ff), F32)],
        [pltpu.VMEM((per * rows, width), F32), pltpu.VMEM((width, ff), F32), pltpu.VMEM((ff, width), F32)], per, "bm")


def run_ba(seq, dx1, m, o, aux, xh, vec, wqkv, wp, per):
    images, rows, width = dx1.shape
    return call(
        functools.partial(ba_kernel, seq), images // per, [dx1, m, o, aux, xh], [vec, wqkv, wp],
        [sds((images, seq, width), F32)],
        [sds((width, 3 * width), BF), sds((width, width), BF), sds((8, width), F32), sds((1, 3 * width), F32)],
        [pltpu.VMEM((per * rows, 3 * width), BF), pltpu.VMEM((per * rows, width), BF),
         pltpu.VMEM((width, 3 * width), F32), pltpu.VMEM((width, width), F32)], per, "ba")


def bits_of(count):
    out = []
    b = 1
    while b < count:
        out.append(b)
        b *= 2
    return out


def xor_pairs(count, b):
    return [(i, i ^ b) for i in range(count)]


def gather(x, n, idx):
    buf = x[None]
    for b in reversed(bits_of(n)):
        recv = lax.ppermute(buf, "shard", xor_pairs(n, b))
        flag = (idx & b) != 0
        low = jnp.where(flag, recv, buf)
        high = jnp.where(flag, buf, recv)
        buf = jnp.stack([low, high], 1).reshape((2 * buf.shape[0],) + x.shape)
    return buf


def reduce_to_owner(x, n, idx, reps):
    buf = x
    for b in bits_of(n):
        half = buf.reshape((buf.shape[0] // 2, 2) + buf.shape[1:])
        flag = ((idx & b) != 0).astype(jnp.int32)
        send = lax.dynamic_index_in_dim(half, 1 - flag, 1, keepdims=False)
        keep = lax.dynamic_index_in_dim(half, flag, 1, keepdims=False)
        recv = lax.ppermute(send, "shard", xor_pairs(n, b))
        buf = (keep.astype(F32) + recv.astype(F32)).astype(BF)
    buf = buf[0]
    for b in bits_of(reps):
        recv = lax.ppermute(buf, "replica", xor_pairs(reps, b))
        buf = (buf.astype(F32) + recv.astype(F32)).astype(BF)
    return buf.astype(F32)


def body(n, reps, tokens, norm1_gain, norm1_shift, qkv_weight, query_bias, value_bias, proj_weight, proj_bias,
         norm2_gain, norm2_shift, fc1_weight, fc1_bias, fc2_weight, fc2_bias, cotangent):
    images, seq, width = tokens.shape
    part = width // n
    ff = fc1_weight.shape[2]
    quart = ff // width
    idx = lax.axis_index("shard")
    per = 2 if images % 2 == 0 else 1
    layers = range(2)

    smalls = [norm1_gain, norm1_shift, query_bias, value_bias, proj_bias, norm2_gain, norm2_shift, fc2_bias]
    small = jnp.concatenate([jnp.stack(smalls, 1), fc1_bias.reshape(2, quart, part)], 1)
    rows_small = small.shape[1]
    small = jnp.pad(small.reshape(2 * rows_small, part).T, ((0, 0), (0, 128 - 2 * rows_small)))

    def full(x):
        g = gather(x, n, idx)
        return g.reshape((n * x.shape[0],) + x.shape[1:])

    def attn_pack(layer):
        parts = [qkv_weight[layer], proj_weight[layer]] + ([small] if layer == 0 else [])
        return jnp.concatenate(parts, 1)

    attn_full, fc1_full, fc2_full = [], [], []
    for layer in layers:
        attn_full.append(full(attn_pack(layer)))
        fc1_full.append(full(fc1_weight[layer]))
        fc2_full.append(full(fc2_weight[layer]))
    sm = attn_full[0][:, 4 * width : 4 * width + 2 * rows_small].astype(F32)
    vec_all = sm.T.reshape(2, rows_small, width)
    vecs = []
    for layer in layers:
        b1 = vec_all[layer, 8:].reshape(quart, n, part).transpose(1, 0, 2).reshape(quart, width)
        vecs.append(jnp.concatenate([vec_all[layer, :8], b1, jnp.zeros((4, width), F32)]))

    current = tokens
    outs, kept = [], []
    for layer in layers:
        vec = vecs[layer]
        wqkv = attn_full[layer][:, : 3 * width]
        wp = attn_full[layer][:, 3 * width : 4 * width]
        m, o, aux, xh1, x1 = run_fa(current, vec, wqkv, wp, per)
        current, a, d, xh2, rs = run_fm(seq, x1, vec, fc1_full[layer], fc2_full[layer], per)
        outs.append(current)
        kept.append((m, o, aux, xh1, a, d, xh2, rs, wqkv, wp))
    grad = cotangent
    grads = [None, None]
    small_grads = [None, None]
    for layer in (1, 0):
        m, o, aux, xh1, a, d, xh2, rs, wqkv, wp = kept[layer]
        vec = vecs[layer]
        dx1, dw1, dw2, v2, db1 = run_bm(grad, a, d, xh2, rs, vec, fc1_full[layer], fc2_full[layer], per)
        g_fc1 = reduce_to_owner(dw1.reshape(n, part, ff), n, idx, reps)
        g_fc2 = reduce_to_owner(dw2.reshape(n, ff // n, width), n, idx, reps)
        grad, dwqkv, dwp, v1, dbm = run_ba(seq, dx1, m, o, aux, xh1, vec, wqkv, wp, per)
        gb1 = db1.reshape(n, quart, part).transpose(1, 0, 2).reshape(quart, width)
        small_grads[layer] = jnp.concatenate(
            [v1[1:3], dbm[:, :width], dbm[:, 2 * width :], v1[0:1], v2[1:3], v2[0:1], gb1])
        parts = [dwqkv, dwp]
        if layer == 0:
            sg = jnp.concatenate(small_grads).astype(BF).T
            parts.append(jnp.pad(sg, ((0, 0), (0, 128 - sg.shape[1]))))
        pack = jnp.concatenate(parts, 1)
        g_attn = reduce_to_owner(pack.reshape(n, part, pack.shape[1]), n, idx, reps)
        grads[layer] = (g_attn, g_fc1, g_fc2)
    g0, g1 = grads[0][0], grads[1][0]
    sgrad = g0[:, 4 * width : 4 * width + 2 * rows_small].T.reshape(2, rows_small, part)
    one = lambda j: sgrad[:, j]
    return (
        outs[0], outs[1], grad,
        one(0), one(1),
        jnp.stack([g0[:, : 3 * width], g1[:, : 3 * width]]),
        one(2), one(3),
        jnp.stack([g0[:, 3 * width : 4 * width], g1[:, 3 * width : 4 * width]]),
        one(4), one(5), one(6),
        jnp.stack([grads[0][1], grads[1][1]]),
        sgrad[:, 8:].reshape(2, ff // n),
        jnp.stack([grads[0][2], grads[1][2]]),
        one(7),
    )


def solution(mesh):
    n = mesh.shape["shard"]
    reps = mesh.shape["replica"]
    batch = P(("replica", "shard"), None, None)
    row2 = P(None, "shard")
    row3 = P(None, "shard", None)
    in_specs = (batch, row2, row2, row3, row2, row2, row3, row2, row2, row2, row3, row2, row3, row2, batch)
    out_specs = (batch, batch, batch, row2, row2, row3, row2, row2, row3, row2, row2, row2, row3, row2, row3, row2)
    return jax.shard_map(
        functools.partial(body, n, reps), mesh=mesh, in_specs=in_specs, out_specs=out_specs, check_vma=False
    )
```

```python
import functools
import jax
import jax.numpy as jnp
from jax import lax
from jax.sharding import PartitionSpec as P
from jax.experimental import pallas as pl
from jax.experimental.pallas import tpu as pltpu

BF = jnp.bfloat16
F32 = jnp.float32
HEADS = 6
EPS = 1e-06
NEG = -1e30
VMEM_LIMIT = 60 * 2**20


def dot(a, b):
    return jnp.dot(a, b, preferred_element_type=F32)


def dot_nt(a, b):
    return lax.dot_general(a, b, (((1,), (1,)), ((), ())), preferred_element_type=F32)


def dot_tn(a, b):
    return lax.dot_general(a, b, (((0,), (0,)), ((), ())), preferred_element_type=F32)


def pad_rows(seq):
    return (seq + 15) // 16 * 16


def colsum(x):
    return jnp.sum(x, 0, keepdims=True)


def slot_masks(n):
    masks = [0]
    b = n // 2
    while b > 1:
        masks = masks + [m ^ b for m in masks]
        b //= 2
    return masks


def start_weights(own, other, dst, sems):
    idx = lax.axis_index("shard")
    for s, mask in enumerate(slot_masks(dst.shape[0])):
        pltpu.make_async_copy(own.at[s], dst.at[jnp.bitwise_xor(idx, mask)], sems.at[2 * s]).start()
        pltpu.make_async_copy(other.at[s], dst.at[jnp.bitwise_xor(idx, mask + 1)], sems.at[2 * s + 1]).start()


def wait_weights(own, other, dst, sems):
    idx = lax.axis_index("shard")
    for s, mask in enumerate(slot_masks(dst.shape[0])):
        pltpu.make_async_copy(own.at[s], dst.at[jnp.bitwise_xor(idx, mask)], sems.at[2 * s]).wait()
        pltpu.make_async_copy(other.at[s], dst.at[jnp.bitwise_xor(idx, mask + 1)], sems.at[2 * s + 1]).wait()


def first_step(*fs):
    @pl.when(pl.program_id(0) == 0)
    def _():
        for f in fs:
            f()


def flat(v):
    return v.reshape(v.shape[0] * v.shape[1], v.shape[2])


def slabs(w, first, count):
    return jnp.concatenate([flat(w[:, k]) for k in range(first, first + count)], 1) if count > 1 else flat(w[:, first])


def tall(w, first, count):
    v = w[:, first : first + count]
    return v.reshape(v.shape[0] * v.shape[1] * v.shape[2], v.shape[3])


def store_slots(keep, send, pieces):
    half = keep.shape[0]
    idx = lax.axis_index("shard")
    for s, mask in enumerate(slot_masks(2 * half)):
        for dst, extra in ((keep, 0), (send, 1)):
            owner = jnp.bitwise_xor(idx, mask + extra)
            for k, piece in enumerate(pieces):
                dst[s, k] = piece(owner).astype(dst.dtype)


def rows_of(ref, part, col, width):
    return lambda owner: ref[pl.ds(pl.multiple_of(owner * part, 8), part), col * width : (col + 1) * width]


def tall_rows_of(ref, part, q, count):
    return lambda owner: ref[pl.ds(pl.multiple_of((owner * count + q) * part, 8), part), :]


def normalise(x):
    mean = jnp.mean(x, -1, keepdims=True)
    cen = x - mean
    rstd = lax.rsqrt(jnp.mean(cen * cen, -1, keepdims=True) + EPS)
    return cen * rstd, rstd


def norm_back(dxhat, xhat, rstd):
    return rstd * (
        dxhat
        - jnp.mean(dxhat, -1, keepdims=True)
        - xhat * jnp.mean(dxhat * xhat, -1, keepdims=True)
    )


def gelu_both(h):
    phi = 0.5 + 0.5 * lax.erf(h * 0.7071067811865476)
    return h * phi, phi + h * (jnp.exp(h * h * -0.5) * 0.3989422804014327)


def to_rows(cols):
    return cols.T[0:8]


def to_column(rows8, r):
    full = jnp.concatenate([rows8, jnp.zeros((120, rows8.shape[1]), F32)], 0)
    return full.T[:, r : r + 1]


def load_padded(dst, src, seq, rows, images):
    for g in range(images):
        dst[g * rows : g * rows + seq] = src[g].astype(F32)
        dst[g * rows + seq : (g + 1) * rows] = jnp.zeros((rows - seq, dst.shape[1]), F32)


def pack_kernel(*refs):
    smalls, (bias_up, w_qkv, w_proj, w_up, w_down) = refs[:8], refs[8:13]
    out_a0, out_m0, out_l1, sq = refs[13:]
    part, width = out_a0.shape[1:]
    sq[...] = jnp.zeros_like(sq)
    for p, ref in enumerate(smalls):
        sq[2 * p : 2 * p + 2, 0:part] = ref[...].astype(F32)
    hid = bias_up.shape[1]
    out_a0[3] = jnp.zeros((part, width), BF)
    out_a0[3, :, 0:128] = sq[...].T[0:part].astype(BF)
    out_a0[3, 0:2, width - hid :] = bias_up[...]
    quart = w_up.shape[2] // width
    for layer in range(2):
        attn = out_a0 if layer == 0 else out_l1
        rest, base = (out_m0, 0) if layer == 0 else (out_l1, 3)
        for k in range(3):
            attn[k] = w_qkv[layer, :, k * width : (k + 1) * width]
        rest[base] = w_proj[layer]
        for q in range(quart):
            rest[base + 1 + q] = w_up[layer, :, q * width : (q + 1) * width]
            rest[base + 1 + quart + q] = w_down[layer, q * part : (q + 1) * part]


def unpack_small(w, vec, tmp):
    shards, _, part, width = w.shape
    hid = tmp.shape[1] // shards
    rows = flat(w[:, 3, :, 0:128]).astype(F32).T
    for j in range(shards):
        tmp[:, j * hid : (j + 1) * hid] = w[j, 3, 0:2, width - hid :].astype(F32)
    quart = tmp.shape[1] // width
    for layer in range(2):
        for p in range(8):
            vec[layer, p : p + 1] = rows[2 * p + layer : 2 * p + layer + 1]
        for q in range(quart):
            vec[layer, 8 + q : 9 + q] = tmp[layer : layer + 1, q * width : (q + 1) * width]
        vec[layer, 8 + quart :] = jnp.zeros((8 - quart, width), F32)


def fa_kernel(seq, layer, x_ref, *refs):
    if layer == 0:
        own, other, m_ref, o_ref, aux_ref, xh_ref, vec_ref, xs, w, sems, tmp = refs
    else:
        vec_ref, own, other, m_ref, o_ref, aux_ref, xh_ref, xs, w, sems = refs
    vec = vec_ref.at[layer]
    first_step(lambda: start_weights(own, other, w, sems))
    images = x_ref.shape[0]
    rows = pad_rows(seq)
    width = x_ref.shape[2]
    load_padded(xs, x_ref, seq, rows, images)
    xhat, rstd = normalise(xs[...])
    xh_ref[...] = xhat.astype(BF).reshape(images, rows, width)
    first_step(lambda: wait_weights(own, other, w, sems))
    if layer == 0:
        first_step(lambda: unpack_small(w, vec_ref, tmp))
    n1 = (xhat * vec[0:1, :] + vec[1:2, :]).astype(BF)
    for c in range(3):
        cs = slice(c * width, (c + 1) * width)
        mc = dot(n1, slabs(w, c, 1))
        if c != 1:
            mc = mc + (vec[2:3, :] if c == 0 else vec[3:4, :])
        m_ref[:, :, cs] = mc.astype(BF).reshape(images, rows, width)
    lane = lax.broadcasted_iota(jnp.int32, (rows, 128), 1)
    row = lax.broadcasted_iota(jnp.int32, (rows, 128), 0)
    low = lane < 64
    kpad = jnp.where(row >= seq, NEG, 0.0).astype(BF)
    ones = jnp.where(row >= seq, 0.0, 1.0).astype(BF)
    qone0 = jnp.where(lane == 64, 1.0, 0.0).astype(BF)
    qone1 = jnp.where(lane == 0, 1.0, 0.0).astype(BF)
    valid = row < seq
    for g in range(images):
        aux = jnp.broadcast_to(rstd[g * rows : (g + 1) * rows], (rows, 128))
        for p in range(width // 128):
            q2 = m_ref[g, :, p * 128 : (p + 1) * 128] * jnp.asarray(0.125, BF)
            k2 = m_ref[g, :, width + p * 128 : width + (p + 1) * 128]
            v2 = m_ref[g, :, 2 * width + p * 128 : 2 * width + (p + 1) * 128]
            v2 = jnp.where(valid, v2, jnp.zeros_like(v2))
            vext = jnp.concatenate([v2, ones], 1)
            parts = []
            for half in range(2):
                mine = low if half == 0 else ~low
                qh = jnp.where(mine, q2, qone0 if half == 0 else qone1)
                kh = jnp.where(mine, k2, kpad)
                s = dot_nt(qh, kh)
                mx = jnp.max(s, -1, keepdims=True)
                pr = jnp.exp(s - mx).astype(BF)
                oe = dot(pr, vext)
                tot = oe[:, 128:]
                parts.append(oe[:, :128] / tot)
                aux = jnp.where(lane == 2 * p + half, mx + jnp.log(tot), aux)
            o_ref[g, :, p * 128 : (p + 1) * 128] = jnp.where(low, parts[0], parts[1]).astype(BF)
        aux_ref[g] = to_rows(aux)


def fm_kernel(seq, layer, x_ref, o_ref, vec_ref, own, other, out_ref, a_ref, d_ref, xh_ref, rs_ref, xs, w, sems):
    vec = vec_ref.at[layer]
    first_step(lambda: start_weights(own, other, w, sems))
    images, rows, width = o_ref.shape
    n = images * rows
    load_padded(xs, x_ref, seq, rows, images)
    first_step(lambda: wait_weights(own, other, w, sems))
    x1 = xs[...] + dot(flat(o_ref[...]), slabs(w, 0, 1)) + vec[4:5, :]
    xhat, rstd = normalise(x1)
    xh_ref[...] = xhat.astype(BF).reshape(images, rows, width)
    for g in range(images):
        rs_ref[g] = to_rows(jnp.broadcast_to(rstd[g * rows : (g + 1) * rows], (rows, 128)))
    n2 = (xhat * vec[5:6, :] + vec[6:7, :]).astype(BF)
    acc = x1 + vec[7:8, :]
    quart = (w.shape[1] - 1) // 2
    w2 = tall(w, 1 + quart, quart)
    for c in range(quart // 2):
        cs = slice(2 * c * width, 2 * (c + 1) * width)
        bias = jnp.concatenate([vec[8 + 2 * c : 9 + 2 * c, :], vec[9 + 2 * c : 10 + 2 * c, :]], 1)
        h = dot(n2, slabs(w, 1 + 2 * c, 2)) + bias
        a, d = gelu_both(h)
        a = a.astype(BF)
        a_ref[:, :, cs] = a.reshape(images, rows, 2 * width)
        d_ref[:, :, cs] = d.astype(BF).reshape(images, rows, 2 * width)
        acc = acc + dot(a, w2[cs, :])
    acc = acc.reshape(images, rows, width)
    for g in range(images):
        out_ref[g] = acc[g, :seq]


def bm_kernel(seq, layer, gr_ref, a_ref, d_ref, xh_ref, rs_ref, o_ref, vec_ref, own, other,
              dx1_ref, do_ref, keep, send, vec_o, db1_o, gs, dwp, dw1, dw2, w, sems):
    vec = vec_ref.at[layer]
    images, rows, width = xh_ref.shape
    n = images * rows
    shards, _, part, _ = w.shape
    step = pl.program_id(0)
    first_step(lambda: start_weights(own, other, w, sems))

    @pl.when(step == 0)
    def _():
        dwp[...] = jnp.zeros_like(dwp)
        dw1[...] = jnp.zeros_like(dw1)
        dw2[...] = jnp.zeros_like(dw2)
        vec_o[...] = jnp.zeros_like(vec_o)
        db1_o[...] = jnp.zeros_like(db1_o)

    load_padded(gs, gr_ref, seq, rows, images)
    dz = gs[...].astype(BF)
    xhat = flat(xh_ref[...]).astype(F32)
    n2 = (xhat * vec[5:6, :] + vec[6:7, :]).astype(BF)
    dn2 = jnp.zeros((n, width), F32)
    first_step(lambda: wait_weights(own, other, w, sems))
    quart = (w.shape[1] - 1) // 2
    w2 = tall(w, 1 + quart, quart)
    for c in range(quart // 2):
        cs = slice(2 * c * width, 2 * (c + 1) * width)
        a = flat(a_ref[:, :, cs])
        d = flat(d_ref[:, :, cs])
        da = dot_nt(dz, w2[cs, :])
        dh = (d.astype(F32) * da).astype(BF)
        db1_o[:, cs] += colsum(dh.astype(F32))
        dw2[cs, :] += dot_tn(a, dz)
        dw1[:, cs] += dot_tn(n2, dh)
        dn2 = dn2 + dot_nt(dh, slabs(w, 1 + 2 * c, 2))
    rstd = jnp.concatenate([to_column(rs_ref[g], 0) for g in range(images)], 0)
    dx1 = gs[...] + norm_back(dn2 * vec[5:6, :], xhat, rstd)
    dx1_ref[...] = dx1.reshape(images, rows, width)
    dy = dx1.astype(BF)
    dwp[...] += dot_tn(flat(o_ref[...]), dy)
    do_ref[...] = dot_nt(dy, slabs(w, 0, 1)).astype(BF).reshape(images, rows, width)
    vec_o[0:1, :] += colsum(dz.astype(F32))
    vec_o[1:2, :] += colsum(dn2 * xhat)
    vec_o[2:3, :] += colsum(dn2)
    vec_o[3:4, :] += colsum(dy.astype(F32))

    @pl.when(step == pl.num_programs(0) - 1)
    def _():
        store_slots(keep, send,
                    [rows_of(dwp, part, 0, width)]
                    + [rows_of(dw1, part, q, width) for q in range(quart)]
                    + [tall_rows_of(dw2, part, q, quart) for q in range(quart)])


def bs_kernel(seq, m_ref, o_ref, do_ref, aux_ref, *rest):
    dm_ref = rest[-1]
    images, rows, width = o_ref.shape
    lane = lax.broadcasted_iota(jnp.int32, (rows, 128), 1)
    low = lane < 64
    last = rows - 16
    valid = lax.broadcasted_iota(jnp.int32, (16, rows), 0) < seq - last
    head = lax.broadcasted_iota(jnp.int32, (8, width), 0)
    pick = jnp.where(lax.broadcasted_iota(jnp.int32, (8, width), 1) // 64 == head, 1.0, 0.0).astype(BF)
    zero = jnp.zeros((rows, 128), BF)
    for g in range(images):
        lse = aux_ref[g]
        inner = dot_nt(pick, (o_ref[g].astype(F32) * do_ref[g].astype(F32)).astype(BF))
        for p in range(width // 128):
            q2 = m_ref[g, :, p * 128 : (p + 1) * 128] * jnp.asarray(0.125, BF)
            k2 = m_ref[g, :, width + p * 128 : width + (p + 1) * 128]
            v2 = m_ref[g, :, 2 * width + p * 128 : 2 * width + (p + 1) * 128]
            do2 = do_ref[g, :, p * 128 : (p + 1) * 128]
            kt = (k2 * jnp.asarray(0.125, BF)).T
            dks, dvs, dqs = [], [], []
            for half in range(2):
                h = 2 * p + half
                kh = jnp.where(low, k2, zero) if half == 0 else jnp.where(low, zero, k2)
                vh = jnp.where(low, v2, zero) if half == 0 else jnp.where(low, zero, v2)
                st = dot_nt(kh, q2) - lse[h : h + 1, :]
                pt = jnp.exp(jnp.concatenate([st[:last], jnp.where(valid, st[last:], NEG)], 0))
                dst = (pt * (dot_nt(vh, do2) - inner[h : h + 1, :])).astype(BF)
                dvs.append(dot(pt.astype(BF), do2))
                dks.append(dot(dst, q2))
                dqs.append(dot(kt[half * 64 : half * 64 + 64], dst))
            dq = jnp.concatenate(dqs, 0).T
            dm_ref[g, :, p * 128 : (p + 1) * 128] = dq.astype(BF)
            dm_ref[g, :, width + p * 128 : width + (p + 1) * 128] = jnp.where(low, dks[0], dks[1]).astype(BF)
            dm_ref[g, :, 2 * width + p * 128 : 2 * width + (p + 1) * 128] = jnp.where(low, dvs[0], dvs[1]).astype(BF)


def bq_kernel(seq, layer, dx1_ref, dm_ref, xh_ref, aux_ref, vec_ref, vec2, db1, own, other,
              dx_ref, keep, send, dwqkv, vec_s, dbm_s, w, sems, sm):
    vec = vec_ref.at[layer]
    images, rows, width = xh_ref.shape
    n = images * rows
    shards, _, part, _ = w.shape
    step = pl.program_id(0)
    first_step(lambda: start_weights(own, other, w, sems))

    @pl.when(step == 0)
    def _():
        dwqkv[...] = jnp.zeros_like(dwqkv)
        vec_s[...] = jnp.zeros_like(vec_s)
        dbm_s[...] = jnp.zeros_like(dbm_s)

    dm = flat(dm_ref[...])
    dbm_s[...] += colsum(dm.astype(F32))
    xhat = flat(xh_ref[...]).astype(F32)
    n1 = (xhat * vec[0:1, :] + vec[1:2, :]).astype(BF)
    dwqkv[...] += dot_tn(n1, dm)
    first_step(lambda: wait_weights(own, other, w, sems))
    dn1 = dot_nt(dm, slabs(w, 0, 3))
    vec_s[0:1, :] += colsum(dn1 * xhat)
    vec_s[1:2, :] += colsum(dn1)
    rstd = jnp.concatenate([to_column(aux_ref[g], 7) for g in range(images)], 0)
    dx = flat(dx1_ref[...]) + norm_back(dn1 * vec[0:1, :], xhat, rstd)
    dx = dx.reshape(images, rows, width)
    for g in range(images):
        dx_ref[g] = dx[g, :seq]

    @pl.when(step == pl.num_programs(0) - 1)
    def _():
        small = jnp.concatenate(
            [vec_s[0:2, :], dbm_s[:, :width], dbm_s[:, 2 * width :], vec2[3:4, :], vec2[1:3, :], vec2[0:1, :],
             jnp.zeros((120, width), F32)], 0)
        sm[...] = jnp.zeros_like(sm)
        sm[:, 0:128] = small.T
        hid = db1.shape[1] // shards
        for j in range(shards):
            sm[j * part : j * part + 1, width - hid :] = db1[:, j * hid : (j + 1) * hid]
        store_slots(keep, send, [rows_of(dwqkv, part, k, width) for k in range(3)] + [rows_of(sm, part, 0, width)])


def finish_kernel(*refs):
    ins, outs = refs[:8], refs[8:]
    o_qkv, o_proj, o_up, o_down, o_bup = outs[:5]
    smalls = outs[5:]
    part, width = ins[0].shape[1:]
    hid = o_bup.shape[1]
    quart = o_up.shape[2] // width
    for layer in range(2):
        a1, a2, m1, m2 = ins[4 * layer : 4 * layer + 4]
        for k in range(3):
            o_qkv[layer, :, k * width : (k + 1) * width] = a1[k].astype(F32) + a2[k].astype(F32)
        small = a1[3].astype(F32) + a2[3].astype(F32)
        o_bup[layer : layer + 1, :] = small[0:1, width - hid :]
        pad = jnp.concatenate([small[:, 0:128], jnp.zeros((128 - part, 128), F32)], 0).T
        for p, ref in enumerate(smalls):
            ref[layer : layer + 1, :] = pad[p : p + 1, 0:part]
        o_proj[layer] = m1[0].astype(F32) + m2[0].astype(F32)
        for q in range(quart):
            o_up[layer, :, q * width : (q + 1) * width] = m1[1 + q].astype(F32) + m2[1 + q].astype(F32)
            o_down[layer, q * part : (q + 1) * part] = m1[1 + quart + q].astype(F32) + m2[1 + quart + q].astype(F32)


def blk(shape):
    nd = len(shape)
    return pl.BlockSpec(shape, lambda i: (i,) + (0,) * (nd - 1))


def whole(arr):
    nd = len(arr.shape)
    return pl.BlockSpec(arr.shape, lambda i: (0,) * nd)


def anyspec():
    return pl.BlockSpec(memory_space=pl.ANY)


def sds(shape, dt):
    return jax.ShapeDtypeStruct(shape, dt)


COST = {"fa": 14, "fm": 18, "bm": 27, "bq": 13}


def call(kern, name, per, blocked_in, whole_in, any_in, blocked_out, whole_out, scratch):
    in_specs = [blk((per,) + a.shape[1:]) for a in blocked_in] + [whole(a) for a in whole_in] + [anyspec() for _ in any_in]
    out_specs = [blk((per,) + a.shape[1:]) for a in blocked_out] + [whole(a) for a in whole_out]
    return pl.pallas_call(
        kern,
        grid=(blocked_in[0].shape[0] // per,),
        in_specs=in_specs,
        out_specs=out_specs,
        out_shape=list(blocked_out) + list(whole_out),
        scratch_shapes=scratch,
        compiler_params=pltpu.CompilerParams(vmem_limit_bytes=VMEM_LIMIT),
        name=name,
        cost_estimate=pl.CostEstimate(flops=COST[name] * 1_150_000_000, bytes_accessed=0, transcendentals=0),
    )(*blocked_in, *whole_in, *any_in)


def wscratch(own):
    return [pltpu.VMEM((2 * own.shape[0],) + own.shape[1:], BF), pltpu.SemaphoreType.DMA((2 * own.shape[0],))]


def run_pack(smalls, bias_up, w_qkv, w_proj, w_up, w_down):
    part, width = w_proj.shape[1:]
    quart = w_up.shape[2] // width
    return pl.pallas_call(
        pack_kernel,
        out_shape=[sds((4, part, width), BF), sds((1 + 2 * quart, part, width), BF), sds((4 + 2 * quart, part, width), BF)],
        scratch_shapes=[pltpu.VMEM((128, 128), F32)],
        name="pack",
    )(*smalls, bias_up, w_qkv, w_proj, w_up, w_down)


def run_fa(x, layer, vec, wa, ff, per):
    images, seq, width = x.shape
    rows = pad_rows(seq)
    outs = [sds((images, rows, 3 * width), BF), sds((images, rows, width), BF), sds((images, 8, rows), F32),
            sds((images, rows, width), BF)]
    scratch = [pltpu.VMEM((per * rows, width), F32)] + wscratch(wa[0])
    if layer == 0:
        return call(functools.partial(fa_kernel, seq, 0), "fa", per, [x], [], wa, outs, [sds((2, 16, width), F32)],
                    scratch + [pltpu.VMEM((2, ff), F32)])
    return call(functools.partial(fa_kernel, seq, 1), "fa", per, [x], [vec], wa, outs, [], scratch)


def run_fm(x, layer, o, vec, wm, per):
    images, seq, width = x.shape
    rows = o.shape[1]
    ff = (wm[0].shape[1] - 1) // 2 * width
    return call(
        functools.partial(fm_kernel, seq, layer), "fm", per, [x, o], [vec], wm,
        [sds((images, seq, width), F32), sds((images, rows, ff), BF), sds((images, rows, ff), BF),
         sds((images, rows, width), BF), sds((images, 8, rows), F32)], [],
        [pltpu.VMEM((per * rows, width), F32)] + wscratch(wm[0]))


def slots(own, count):
    half, _, part, width = own.shape
    return [sds((half, count, part, width), F32), sds((half, count, part, width), BF)]


def run_bm(gr, layer, a, d, xh, rs, o, vec, wm, per):
    images, seq, width = gr.shape
    rows, ff = a.shape[1:]
    return call(
        functools.partial(bm_kernel, seq, layer), "bm", per, [gr, a, d, xh, rs, o], [vec], wm,
        [sds((images, rows, width), F32), sds((images, rows, width), BF)],
        slots(wm[0], wm[0].shape[1]) + [sds((8, width), F32), sds((1, ff), F32)],
        [pltpu.VMEM((per * rows, width), F32), pltpu.VMEM((width, width), F32), pltpu.VMEM((width, ff), F32),
         pltpu.VMEM((ff, width), F32)] + wscratch(wm[0]))


def run_bs(seq, m, o, do, aux, per, first=0, count=None, prev=None):
    count = count or m.shape[0] - first
    base = first // per

    def at(shape):
        nd = len(shape)
        return pl.BlockSpec((per,) + shape[1:], lambda i: (i + base,) + (0,) * (nd - 1))

    more = [] if prev is None else [prev]
    return pl.pallas_call(
        functools.partial(bs_kernel, seq),
        grid=(count // per,),
        in_specs=[at(a.shape) for a in (m, o, do, aux)] + [anyspec() for _ in more],
        out_specs=at(m.shape),
        out_shape=sds(m.shape, BF),
        input_output_aliases={4: 0} if more else {},
        compiler_params=pltpu.CompilerParams(vmem_limit_bytes=VMEM_LIMIT),
        name="bs",
        cost_estimate=pl.CostEstimate(flops=18 * count // m.shape[0] * 1_150_000_000, bytes_accessed=0, transcendentals=0),
    )(m, o, do, aux, *more)


def run_bq(seq, layer, dx1, dm, xh, aux, vec, vec2, db1, wa, per):
    images, rows, width = dx1.shape
    return call(
        functools.partial(bq_kernel, seq, layer), "bq", per, [dx1, dm, xh, aux], [vec, vec2, db1], wa,
        [sds((images, seq, width), F32)], slots(wa[0], 4),
        [pltpu.VMEM((width, 3 * width), F32), pltpu.VMEM((8, width), F32), pltpu.VMEM((1, 3 * width), F32)]
        + wscratch(wa[0]) + [pltpu.VMEM((width, width), F32)])


def run_finish(a0, m0, a1, m1, ff):
    part, width = a0[0].shape[1:]
    return pl.pallas_call(
        finish_kernel,
        out_shape=[sds((2, part, 3 * width), F32), sds((2, part, width), F32), sds((2, part, ff), F32),
                   sds((2, ff // width * part, width), F32), sds((2, ff // width * part), F32)]
        + [sds((2, part), F32)] * 8,
        name="finish",
    )(*a0, *m0, *a1, *m1)


def xor_pairs(count, b):
    return [(i, i ^ b) for i in range(count)]


def tie(value, *others):
    return lax.optimization_barrier((value, *others))[0]


def group(*values):
    return lax.optimization_barrier(values)


def body(n, reps, tokens, norm1_gain, norm1_shift, qkv_weight, query_bias, value_bias, proj_weight, proj_bias,
         norm2_gain, norm2_shift, fc1_weight, fc1_bias, fc2_weight, fc2_bias, cotangent):
    images, seq, width = tokens.shape
    ff = fc1_weight.shape[2]
    per = 2 if images % 2 == 0 else 1
    upper = []
    b = n // 2
    while b > 2:
        upper.append(b)
        b //= 2

    def swap(x, b):
        return lax.ppermute(x, "shard", xor_pairs(n, b))

    def grow(x, b):
        return jnp.concatenate([x, swap(x, b)])

    def direct(x):
        masks = [0]
        for b in upper:
            masks = masks + [m ^ b for m in masks]
        return [x] + [swap(x, m) for m in masks[1:]]

    smalls = [norm1_gain, norm1_shift, query_bias, value_bias, proj_bias, norm2_gain, norm2_shift, fc2_bias]
    a0, m0, l1 = run_pack(smalls, fc1_bias, qkv_weight, proj_weight, fc1_weight, fc2_weight)

    a0 = jnp.stack(direct(a0))
    m0 = direct(tie(m0, a0))
    a0x = swap(a0, 2)
    a0 = jnp.concatenate([a0, a0x])
    a0 = (a0, swap(a0, 1))
    m0 = jnp.stack([m0[0]] + [tie(y, a0x) for y in m0[1:]])
    m0x = swap(m0, 2)
    l1 = direct(tie(l1, m0))
    mix0, o0, aux0, xa0, vec = run_fa(tie(tokens, m0, l1[0]), 0, None, a0, ff, per)
    o0, m0x, *l1 = group(o0, m0x, *l1)
    m0 = jnp.concatenate([m0, m0x])
    l1 = jnp.stack(l1)
    m0 = (m0, swap(tie(m0, l1), 1))
    l1x = swap(l1, 2)
    layer_one, act0, der0, xm0, rs0 = run_fm(tokens, 0, o0, vec, m0, per)
    layer_one, l1x = group(layer_one, l1x)
    a1 = jnp.concatenate([l1[:, :3], l1x[:, :3]])
    m1 = jnp.concatenate([l1[:, 3:], l1x[:, 3:]])
    a1 = (a1, swap(a1, 1))
    m1x = swap(m1, 1)
    mix1, o1, aux1, xa1 = run_fa(tie(layer_one, m1), 1, vec, a1, ff, per)
    o1, m1x = group(o1, m1x)
    m1 = (m1, m1x)
    layer_two, act1, der1, xm1, rs1 = run_fm(layer_one, 1, o1, vec, m1, per)

    class Sum:
        def __init__(self, keep, send):
            self.keep, self.got, self.send = keep, [], send
            self.bits = [1, 2] + upper[::-1]

        def start(self):
            self.flight = swap(self.send, self.bits[len(self.got)])
            return self

        def done(self):
            self.got.append(self.flight)
            size = self.flight.shape[0]
            if len(self.got) < len(self.bits):
                self.send = self.total(size // 2, size).astype(BF)
            else:
                self.send = self.total(0, 1)[0].astype(BF)
            return self

        def total(self, lo, hi):
            t = self.keep[lo:hi]
            for g in self.got:
                t = t + g[lo:hi].astype(F32)
            return t

        def replicas(self):
            mine, b = self.send, 1
            while True:
                other = lax.ppermute(mine, "replica", xor_pairs(reps, b))
                b *= 2
                if b >= reps:
                    return (mine, other)
                mine = (mine.astype(F32) + other.astype(F32)).astype(BF)

    def meet(value, *sums):
        value, *got = group(value, *[s.flight for s in sums])
        for s, g in zip(sums, got):
            s.flight = g
            s.done()
        return value

    def sent(value, *sums):
        return tie(value, *[s.send for s in sums])

    dx1, do, kp, sn, v2, db1 = run_bm(cotangent, 1, act1, der1, xm1, rs1, o1, vec, m1, per)
    gm1 = Sum(kp, sn).start()
    dm = run_bs(seq, mix1, o1, do, aux1, per)
    dm = meet(dm, gm1)
    gm1.start()
    grad, kp, sn = run_bq(seq, 1, dx1, sent(dm, gm1), xa1, aux1, vec, v2, db1, a1, per)
    ga1 = Sum(kp, sn).start()
    grad = meet(grad, gm1)
    gm1.start()
    dx1, do, kp, sn, v2, db1 = run_bm(sent(grad, gm1), 0, act0, der0, xm0, rs0, o0, vec, m0, per)
    gm0 = Sum(kp, sn).start()
    do = meet(do, gm1, ga1)
    gm1.start()
    ga1.start()
    first = images // (2 * per) * per
    dm = run_bs(seq, mix0, o0, sent(do, gm1, ga1), aux0, per, 0, first)
    dm = meet(dm, gm1, ga1, gm0)
    ga1.start()
    gm0.start()
    fin_m1 = gm1.replicas()
    dm = run_bs(seq, mix0, o0, do, aux0, per, first, None, sent(dm, gm1, ga1, gm0))
    dm = meet(dm, ga1, gm0)
    ga1.start()
    gm0.start()
    tokens_grad, kp, sn = run_bq(seq, 0, dx1, sent(dm, ga1, gm0), xa0, aux0, vec, v2, db1, a0, per)
    ga0 = Sum(kp, sn).start()
    tokens_grad = meet(tokens_grad, ga1, gm0)
    fin_a1 = ga1.replicas()
    gm0.start()
    ga0.done().start()
    gm0.flight = tie(gm0.flight, ga0.send)
    gm0.done()
    fin_m0 = gm0.replicas()
    ga0.done().start().done().start().done()
    fin_a0 = ga0.replicas()

    g_qkv, g_proj, g_up, g_down, g_bup, *s = run_finish(fin_a0, fin_m0, fin_a1, fin_m1, ff)
    return (layer_one, layer_two, tokens_grad, s[0], s[1], g_qkv, s[2], s[3], g_proj, s[4], s[5], s[6],
            g_up, g_bup, g_down, s[7])
def solution(mesh):
    n = mesh.shape["shard"]
    reps = mesh.shape["replica"]
    batch = P(("replica", "shard"), None, None)
    row2 = P(None, "shard")
    row3 = P(None, "shard", None)
    in_specs = (batch, row2, row2, row3, row2, row2, row3, row2, row2, row2, row3, row2, row3, row2, batch)
    out_specs = (batch, batch, batch, row2, row2, row3, row2, row2, row3, row2, row2, row2, row3, row2, row3, row2)
    return jax.shard_map(
        functools.partial(body, n, reps), mesh=mesh, in_specs=in_specs, out_specs=out_specs, check_vma=False
    )
```

```python
import functools
import jax
import jax.numpy as jnp
from jax import lax
from jax.sharding import PartitionSpec as P
from jax.experimental import pallas as pl
from jax.experimental.pallas import tpu as pltpu

BF = jnp.bfloat16
F32 = jnp.float32
HEADS = 6
EPS = 1e-06
NEG = -1e30
VMEM_LIMIT = 60 * 2**20


def dot(a, b):
    return jnp.dot(a, b, preferred_element_type=F32)


def dot_nt(a, b):
    return lax.dot_general(a, b, (((1,), (1,)), ((), ())), preferred_element_type=F32)


def dot_tn(a, b):
    return lax.dot_general(a, b, (((0,), (0,)), ((), ())), preferred_element_type=F32)


def pad_rows(seq):
    return (seq + 15) // 16 * 16


def colsum(x):
    return jnp.sum(x, 0, keepdims=True)


def slot_masks(n):
    masks = [0]
    b = n // 2
    while b > 1:
        masks = masks + [m ^ b for m in masks]
        b //= 2
    return masks


def start_weights(own, other, dst, sems):
    idx = lax.axis_index("shard")
    for s, mask in enumerate(slot_masks(dst.shape[0])):
        pltpu.make_async_copy(own.at[s], dst.at[jnp.bitwise_xor(idx, mask)], sems.at[2 * s]).start()
        pltpu.make_async_copy(other.at[s], dst.at[jnp.bitwise_xor(idx, mask + 1)], sems.at[2 * s + 1]).start()


def wait_weights(own, other, dst, sems):
    idx = lax.axis_index("shard")
    for s, mask in enumerate(slot_masks(dst.shape[0])):
        pltpu.make_async_copy(own.at[s], dst.at[jnp.bitwise_xor(idx, mask)], sems.at[2 * s]).wait()
        pltpu.make_async_copy(other.at[s], dst.at[jnp.bitwise_xor(idx, mask + 1)], sems.at[2 * s + 1]).wait()


def first_step(*fs):
    @pl.when(pl.program_id(0) == 0)
    def _():
        for f in fs:
            f()


def flat(v):
    return v.reshape(v.shape[0] * v.shape[1], v.shape[2])


def slabs(w, first, count):
    return jnp.concatenate([flat(w[:, k]) for k in range(first, first + count)], 1) if count > 1 else flat(w[:, first])


def tall(w, first, count):
    v = w[:, first : first + count]
    return v.reshape(v.shape[0] * v.shape[1] * v.shape[2], v.shape[3])


def store_slots(keep, send, pieces):
    half = keep.shape[0]
    idx = lax.axis_index("shard")
    for s, mask in enumerate(slot_masks(2 * half)):
        for dst, extra in ((keep, 0), (send, 1)):
            owner = jnp.bitwise_xor(idx, mask + extra)
            for k, piece in enumerate(pieces):
                dst[s, k] = piece(owner).astype(dst.dtype)


def rows_of(ref, part, col, width):
    return lambda owner: ref[pl.ds(pl.multiple_of(owner * part, 8), part), col * width : (col + 1) * width]


def tall_rows_of(ref, part, q, count):
    return lambda owner: ref[pl.ds(pl.multiple_of((owner * count + q) * part, 8), part), :]


def normalise(x):
    mean = jnp.mean(x, -1, keepdims=True)
    cen = x - mean
    rstd = lax.rsqrt(jnp.mean(cen * cen, -1, keepdims=True) + EPS)
    return cen * rstd, rstd


def norm_back(dxhat, xhat, rstd):
    return rstd * (
        dxhat
        - jnp.mean(dxhat, -1, keepdims=True)
        - xhat * jnp.mean(dxhat * xhat, -1, keepdims=True)
    )


def gelu_both(h):
    phi = 0.5 + 0.5 * lax.erf(h * 0.7071067811865476)
    return h * phi, phi + h * (jnp.exp(h * h * -0.5) * 0.3989422804014327)


def to_rows(cols):
    return cols.T[0:8]


def to_column(rows8, r):
    full = jnp.concatenate([rows8, jnp.zeros((120, rows8.shape[1]), F32)], 0)
    return full.T[:, r : r + 1]


def load_padded(dst, src, seq, rows, images):
    for g in range(images):
        dst[g * rows : g * rows + seq] = src[g].astype(F32)
        dst[g * rows + seq : (g + 1) * rows] = jnp.zeros((rows - seq, dst.shape[1]), F32)


def pack_kernel(*refs):
    smalls, (bias_up, w_qkv, w_proj, w_up, w_down) = refs[:8], refs[8:13]
    out_a0, out_m0, out_l1, sq = refs[13:]
    part, width = out_a0.shape[1:]
    sq[...] = jnp.zeros_like(sq)
    for p, ref in enumerate(smalls):
        sq[2 * p : 2 * p + 2, 0:part] = ref[...].astype(F32)
    hid = bias_up.shape[1]
    out_a0[3] = jnp.zeros((part, width), BF)
    out_a0[3, :, 0:128] = sq[...].T[0:part].astype(BF)
    out_a0[3, 0:2, width - hid :] = bias_up[...]
    quart = w_up.shape[2] // width
    for layer in range(2):
        attn = out_a0 if layer == 0 else out_l1
        rest, base = (out_m0, 0) if layer == 0 else (out_l1, 3)
        for k in range(3):
            attn[k] = w_qkv[layer, :, k * width : (k + 1) * width]
        rest[base] = w_proj[layer]
        for q in range(quart):
            rest[base + 1 + q] = w_up[layer, :, q * width : (q + 1) * width]
            rest[base + 1 + quart + q] = w_down[layer, q * part : (q + 1) * part]


def unpack_small(w, vec, tmp):
    shards, _, part, width = w.shape
    hid = tmp.shape[1] // shards
    rows = flat(w[:, 3, :, 0:128]).astype(F32).T
    for j in range(shards):
        tmp[:, j * hid : (j + 1) * hid] = w[j, 3, 0:2, width - hid :].astype(F32)
    quart = tmp.shape[1] // width
    for layer in range(2):
        for p in range(8):
            vec[layer, p : p + 1] = rows[2 * p + layer : 2 * p + layer + 1]
        for q in range(quart):
            vec[layer, 8 + q : 9 + q] = tmp[layer : layer + 1, q * width : (q + 1) * width]
        vec[layer, 8 + quart :] = jnp.zeros((8 - quart, width), F32)


def attn_forward(seq, xs, vec, w, m_ref, o_ref, aux_ref, xh_ref):
    images, rows, width = o_ref.shape
    xhat, rstd = normalise(xs[...])
    xh_ref[...] = xhat.astype(BF).reshape(images, rows, width)
    n1 = (xhat * vec[0:1, :] + vec[1:2, :]).astype(BF)
    for c in range(3):
        cs = slice(c * width, (c + 1) * width)
        mc = dot(n1, slabs(w, c, 1))
        if c != 1:
            mc = mc + (vec[2:3, :] if c == 0 else vec[3:4, :])
        m_ref[:, :, cs] = mc.astype(BF).reshape(images, rows, width)
    lane = lax.broadcasted_iota(jnp.int32, (rows, 128), 1)
    row = lax.broadcasted_iota(jnp.int32, (rows, 128), 0)
    low = lane < 64
    kpad = jnp.where(row >= seq, NEG, 0.0).astype(BF)
    ones = jnp.where(row >= seq, 0.0, 1.0).astype(BF)
    qone0 = jnp.where(lane == 64, 1.0, 0.0).astype(BF)
    qone1 = jnp.where(lane == 0, 1.0, 0.0).astype(BF)
    valid = row < seq
    for g in range(images):
        aux = jnp.broadcast_to(rstd[g * rows : (g + 1) * rows], (rows, 128))
        for p in range(width // 128):
            q2 = m_ref[g, :, p * 128 : (p + 1) * 128] * jnp.asarray(0.125, BF)
            k2 = m_ref[g, :, width + p * 128 : width + (p + 1) * 128]
            v2 = m_ref[g, :, 2 * width + p * 128 : 2 * width + (p + 1) * 128]
            v2 = jnp.where(valid, v2, jnp.zeros_like(v2))
            vext = jnp.concatenate([v2, ones], 1)
            parts = []
            for half in range(2):
                mine = low if half == 0 else ~low
                qh = jnp.where(mine, q2, qone0 if half == 0 else qone1)
                kh = jnp.where(mine, k2, kpad)
                s = dot_nt(qh, kh)
                mx = jnp.max(s, -1, keepdims=True)
                pr = jnp.exp(s - mx).astype(BF)
                oe = dot(pr, vext)
                tot = oe[:, 128:]
                parts.append(oe[:, :128] / tot)
                aux = jnp.where(lane == 2 * p + half, mx + jnp.log(tot), aux)
            o_ref[g, :, p * 128 : (p + 1) * 128] = jnp.where(low, parts[0], parts[1]).astype(BF)
        aux_ref[g] = to_rows(aux)


def mlp_forward(seq, xs, o_ref, vec, w, base, out_ref, a_ref, d_ref, xh_ref, rs_ref):
    images, rows, width = o_ref.shape
    x1 = xs[...] + dot(flat(o_ref[...]), slabs(w, base, 1)) + vec[4:5, :]
    xhat, rstd = normalise(x1)
    xh_ref[...] = xhat.astype(BF).reshape(images, rows, width)
    for g in range(images):
        rs_ref[g] = to_rows(jnp.broadcast_to(rstd[g * rows : (g + 1) * rows], (rows, 128)))
    n2 = (xhat * vec[5:6, :] + vec[6:7, :]).astype(BF)
    acc = x1 + vec[7:8, :]
    quart = a_ref.shape[2] // width
    w2 = tall(w, base + 1 + quart, quart)
    for c in range(quart // 2):
        cs = slice(2 * c * width, 2 * (c + 1) * width)
        bias = jnp.concatenate([vec[8 + 2 * c : 9 + 2 * c, :], vec[9 + 2 * c : 10 + 2 * c, :]], 1)
        h = dot(n2, slabs(w, base + 1 + 2 * c, 2)) + bias
        a, d = gelu_both(h)
        a = a.astype(BF)
        a_ref[:, :, cs] = a.reshape(images, rows, 2 * width)
        d_ref[:, :, cs] = d.astype(BF).reshape(images, rows, 2 * width)
        acc = acc + dot(a, w2[cs, :])
    acc = acc.reshape(images, rows, width)
    for g in range(images):
        out_ref[g] = acc[g, :seq]


def zero(*refs):
    for r in refs:
        r[...] = jnp.zeros_like(r)


def mlp_backward(gs, a_ref, d_ref, xh_ref, rs_ref, o_ref, vec, w, base, dx1_ref, do_ref, dwp, dw1, dw2, vec_o, db1_o):
    images, rows, width = xh_ref.shape
    n = images * rows
    dz = gs[...].astype(BF)
    xhat = flat(xh_ref[...]).astype(F32)
    n2 = (xhat * vec[5:6, :] + vec[6:7, :]).astype(BF)
    dn2 = jnp.zeros((n, width), F32)
    quart = a_ref.shape[2] // width
    w2 = tall(w, base + 1 + quart, quart)
    for c in range(quart // 2):
        cs = slice(2 * c * width, 2 * (c + 1) * width)
        a = flat(a_ref[:, :, cs])
        d = flat(d_ref[:, :, cs])
        da = dot_nt(dz, w2[cs, :])
        dh = (d.astype(F32) * da).astype(BF)
        db1_o[:, cs] += colsum(dh.astype(F32))
        dw2[cs, :] += dot_tn(a, dz)
        dw1[:, cs] += dot_tn(n2, dh)
        dn2 = dn2 + dot_nt(dh, slabs(w, base + 1 + 2 * c, 2))
    rstd = jnp.concatenate([to_column(rs_ref[g], 0) for g in range(images)], 0)
    dx1 = gs[...] + norm_back(dn2 * vec[5:6, :], xhat, rstd)
    dx1_ref[...] = dx1.reshape(images, rows, width)
    dy = dx1.astype(BF)
    dwp[...] += dot_tn(flat(o_ref[...]), dy)
    do_ref[...] = dot_nt(dy, slabs(w, base, 1)).astype(BF).reshape(images, rows, width)
    vec_o[0:1, :] += colsum(dz.astype(F32))
    vec_o[1:2, :] += colsum(dn2 * xhat)
    vec_o[2:3, :] += colsum(dn2)
    vec_o[3:4, :] += colsum(dy.astype(F32))


def attn_backward(seq, m_ref, do_ref, aux_ref, dm_ref):
    images, rows, width = do_ref.shape
    lane = lax.broadcasted_iota(jnp.int32, (rows, 128), 1)
    low = lane < 64
    last = rows - 16
    valid = lax.broadcasted_iota(jnp.int32, (16, rows), 0) < seq - last
    none = jnp.zeros((rows, 128), BF)
    for g in range(images):
        lse = aux_ref[g]
        for p in range(width // 128):
            q2 = m_ref[g, :, p * 128 : (p + 1) * 128] * jnp.asarray(0.125, BF)
            k2 = m_ref[g, :, width + p * 128 : width + (p + 1) * 128]
            v2 = m_ref[g, :, 2 * width + p * 128 : 2 * width + (p + 1) * 128]
            do2 = do_ref[g, :, p * 128 : (p + 1) * 128]
            kt = (k2 * jnp.asarray(0.125, BF)).T
            dks, dvs, dqs = [], [], []
            for half in range(2):
                h = 2 * p + half
                kh = jnp.where(low, k2, none) if half == 0 else jnp.where(low, none, k2)
                vh = jnp.where(low, v2, none) if half == 0 else jnp.where(low, none, v2)
                st = dot_nt(kh, q2) - lse[h : h + 1, :]
                pt = jnp.exp(jnp.concatenate([st[:last], jnp.where(valid, st[last:], NEG)], 0))
                pd = pt * dot_nt(vh, do2)
                dst = (pd - pt * colsum(pd)).astype(BF)
                dvs.append(dot(pt.astype(BF), do2))
                dks.append(dot(dst, q2))
                dqs.append(dot(kt[half * 64 : half * 64 + 64], dst))
            dq = jnp.concatenate(dqs, 0).T
            dm_ref[g, :, p * 128 : (p + 1) * 128] = dq.astype(BF)
            dm_ref[g, :, width + p * 128 : width + (p + 1) * 128] = jnp.where(low, dks[0], dks[1]).astype(BF)
            dm_ref[g, :, 2 * width + p * 128 : 2 * width + (p + 1) * 128] = jnp.where(low, dvs[0], dvs[1]).astype(BF)


def qkv_backward(seq, dx1_ref, dm_ref, xh_ref, aux_ref, vec, w, dx_ref, dwqkv, vec_s, dbm_s):
    images, rows, width = xh_ref.shape
    dm = flat(dm_ref[...])
    dbm_s[...] += colsum(dm.astype(F32))
    xhat = flat(xh_ref[...]).astype(F32)
    n1 = (xhat * vec[0:1, :] + vec[1:2, :]).astype(BF)
    dwqkv[...] += dot_tn(n1, dm)
    dn1 = dot_nt(dm, slabs(w, 0, 3))
    vec_s[0:1, :] += colsum(dn1 * xhat)
    vec_s[1:2, :] += colsum(dn1)
    rstd = jnp.concatenate([to_column(aux_ref[g], 7) for g in range(images)], 0)
    dx = flat(dx1_ref[...]) + norm_back(dn1 * vec[0:1, :], xhat, rstd)
    dx = dx.reshape(images, rows, width)
    for g in range(images):
        dx_ref[g] = dx[g, :seq]


def small_slab(sm, vec_s, dbm_s, vec2, db1, part):
    width = sm.shape[0]
    small = jnp.concatenate(
        [vec_s[0:2, :], dbm_s[:, :width], dbm_s[:, 2 * width :], vec2[3:4, :], vec2[1:3, :], vec2[0:1, :],
         jnp.zeros((120, width), F32)], 0)
    sm[...] = jnp.zeros_like(sm)
    sm[:, 0:128] = small.T
    shards = width // part
    hid = db1.shape[1] // shards
    for j in range(shards):
        sm[j * part : j * part + 1, width - hid :] = db1[:, j * hid : (j + 1) * hid]


def attn_pieces(dwqkv, sm, part):
    width = sm.shape[0]
    return [rows_of(dwqkv, part, c, width) for c in range(3)] + [rows_of(sm, part, 0, width)]


def mlp_pieces(dwp, dw1, dw2, part):
    width = dwp.shape[0]
    quart = dw1.shape[1] // width
    return ([rows_of(dwp, part, 0, width)] + [rows_of(dw1, part, q, width) for q in range(quart)]
            + [tall_rows_of(dw2, part, q, quart) for q in range(quart)])


def last_step(f):
    pl.when(pl.program_id(0) == pl.num_programs(0) - 1)(f)


def fa_kernel(seq, x_ref, own, other, m_ref, o_ref, aux_ref, xh_ref, vec_ref, xs, w, sems, tmp):
    first_step(lambda: start_weights(own, other, w, sems))
    images, rows, _ = o_ref.shape
    load_padded(xs, x_ref, seq, rows, images)
    first_step(lambda: wait_weights(own, other, w, sems), lambda: unpack_small(w, vec_ref, tmp))
    attn_forward(seq, xs, vec_ref.at[0], w, m_ref, o_ref, aux_ref, xh_ref)


def fm_kernel(seq, x_ref, o_ref, vec_ref, own, other, out_ref, a_ref, d_ref, xh_ref, rs_ref, xs, w, sems):
    first_step(lambda: start_weights(own, other, w, sems))
    images, rows, _ = o_ref.shape
    load_padded(xs, x_ref, seq, rows, images)
    first_step(lambda: wait_weights(own, other, w, sems))
    mlp_forward(seq, xs, o_ref, vec_ref.at[0], w, 0, out_ref, a_ref, d_ref, xh_ref, rs_ref)


def bm_kernel(seq, gr_ref, a_ref, d_ref, xh_ref, rs_ref, o_ref, vec_ref, own, other,
              dx1_ref, do_ref, keep, send, vec_o, db1_o, gs, dwp, dw1, dw2, w, sems):
    images, rows, width = xh_ref.shape
    first_step(lambda: start_weights(own, other, w, sems), lambda: zero(dwp, dw1, dw2, vec_o, db1_o))
    load_padded(gs, gr_ref, seq, rows, images)
    first_step(lambda: wait_weights(own, other, w, sems))
    mlp_backward(gs, a_ref, d_ref, xh_ref, rs_ref, o_ref, vec_ref.at[0], w, 0, dx1_ref, do_ref, dwp, dw1, dw2, vec_o, db1_o)

    @last_step
    def _():
        store_slots(keep, send, mlp_pieces(dwp, dw1, dw2, w.shape[2]))


def ba_kernel(seq, dx1_ref, m_ref, do_ref, xh_ref, aux_ref, vec_ref, vec2, db1, own, other,
              dx_ref, keep, send, dm_s, dwqkv, vec_s, dbm_s, w, sems, sm):
    first_step(lambda: start_weights(own, other, w, sems), lambda: zero(dwqkv, vec_s, dbm_s))
    attn_backward(seq, m_ref, do_ref, aux_ref, dm_s)
    first_step(lambda: wait_weights(own, other, w, sems))
    qkv_backward(seq, dx1_ref, dm_s, xh_ref, aux_ref, vec_ref.at[0], w, dx_ref, dwqkv, vec_s, dbm_s)

    @last_step
    def _():
        part = w.shape[2]
        small_slab(sm, vec_s, dbm_s, vec2, db1, part)
        store_slots(keep, send, attn_pieces(dwqkv, sm, part))


def top_kernel(seq, x_ref, cot_ref, vec_ref, own, other, out_ref, dx_ref, keep, send,
               xs, gs, m_s, o_s, aux_s, xa_s, xm_s, rs_s, a_s, d_s, dx1_s, do_s, dm_s,
               dwqkv, dwp, dw1, dw2, vec_a, vec_m, dbm_s, db1_s, sm, w, sems):
    images, rows, width = o_s.shape
    vec = vec_ref.at[1]
    first_step(lambda: start_weights(own, other, w, sems),
               lambda: zero(dwqkv, dwp, dw1, dw2, vec_a, vec_m, dbm_s, db1_s))
    load_padded(xs, x_ref, seq, rows, images)
    load_padded(gs, cot_ref, seq, rows, images)
    first_step(lambda: wait_weights(own, other, w, sems))
    attn_forward(seq, xs, vec, w, m_s, o_s, aux_s, xa_s)
    mlp_forward(seq, xs, o_s, vec, w, 3, out_ref, a_s, d_s, xm_s, rs_s)
    mlp_backward(gs, a_s, d_s, xm_s, rs_s, o_s, vec, w, 3, dx1_s, do_s, dwp, dw1, dw2, vec_m, db1_s)
    attn_backward(seq, m_s, do_s, aux_s, dm_s)
    qkv_backward(seq, dx1_s, dm_s, xa_s, aux_s, vec, w, dx_ref, dwqkv, vec_a, dbm_s)

    @last_step
    def _():
        part = w.shape[2]
        small_slab(sm, vec_a, dbm_s, vec_m, db1_s, part)
        store_slots(keep, send, attn_pieces(dwqkv, sm, part) + mlp_pieces(dwp, dw1, dw2, part))


def finish_kernel(*refs):
    ins, outs = refs[:6], refs[6:]
    o_qkv, o_proj, o_up, o_down, o_bup = outs[:5]
    smalls = outs[5:]
    part, width = ins[0].shape[1:]
    hid = o_bup.shape[1]
    quart = o_up.shape[2] // width
    for layer in range(2):
        a1, a2 = ins[4:6] if layer == 1 else ins[0:2]
        m1, m2, base = (*ins[4:6], 4) if layer == 1 else (*ins[2:4], 0)
        for k in range(3):
            o_qkv[layer, :, k * width : (k + 1) * width] = a1[k].astype(F32) + a2[k].astype(F32)
        small = a1[3].astype(F32) + a2[3].astype(F32)
        o_bup[layer : layer + 1, :] = small[0:1, width - hid :]
        pad = jnp.concatenate([small[:, 0:128], jnp.zeros((128 - part, 128), F32)], 0).T
        for p, ref in enumerate(smalls):
            ref[layer : layer + 1, :] = pad[p : p + 1, 0:part]

        def both(k):
            return m1[base + k].astype(F32) + m2[base + k].astype(F32)

        o_proj[layer] = both(0)
        for q in range(quart):
            o_up[layer, :, q * width : (q + 1) * width] = both(1 + q)
            o_down[layer, q * part : (q + 1) * part] = both(1 + quart + q)


def blk(shape):
    nd = len(shape)
    return pl.BlockSpec(shape, lambda i: (i,) + (0,) * (nd - 1))


def whole(arr):
    nd = len(arr.shape)
    return pl.BlockSpec(arr.shape, lambda i: (0,) * nd)


def anyspec():
    return pl.BlockSpec(memory_space=pl.ANY)


def sds(shape, dt):
    return jax.ShapeDtypeStruct(shape, dt)


COST = {"fa": 13, "fm": 18, "bm": 26, "ba": 28, "top": 70}


def call(kern, name, per, blocked_in, whole_in, any_in, blocked_out, whole_out, scratch):
    in_specs = [blk((per,) + a.shape[1:]) for a in blocked_in] + [whole(a) for a in whole_in] + [anyspec() for _ in any_in]
    out_specs = [blk((per,) + a.shape[1:]) for a in blocked_out] + [whole(a) for a in whole_out]
    return pl.pallas_call(
        kern,
        grid=(blocked_in[0].shape[0] // per,),
        in_specs=in_specs,
        out_specs=out_specs,
        out_shape=list(blocked_out) + list(whole_out),
        scratch_shapes=scratch,
        compiler_params=pltpu.CompilerParams(vmem_limit_bytes=VMEM_LIMIT),
        name=name,
        cost_estimate=pl.CostEstimate(flops=COST[name] * 1_150_000_000, bytes_accessed=0, transcendentals=0),
    )(*blocked_in, *whole_in, *any_in)


def wscratch(own):
    return [pltpu.VMEM((2 * own.shape[0],) + own.shape[1:], BF), pltpu.SemaphoreType.DMA((2 * own.shape[0],))]


def run_pack(smalls, bias_up, w_qkv, w_proj, w_up, w_down):
    part, width = w_proj.shape[1:]
    quart = w_up.shape[2] // width
    return pl.pallas_call(
        pack_kernel,
        out_shape=[sds((4, part, width), BF), sds((1 + 2 * quart, part, width), BF), sds((4 + 2 * quart, part, width), BF)],
        scratch_shapes=[pltpu.VMEM((128, 128), F32)],
        name="pack",
    )(*smalls, bias_up, w_qkv, w_proj, w_up, w_down)


def run_fa(x, wa, ff, per):
    images, seq, width = x.shape
    rows = pad_rows(seq)
    return call(
        functools.partial(fa_kernel, seq), "fa", per, [x], [], wa,
        [sds((images, rows, 3 * width), BF), sds((images, rows, width), BF), sds((images, 8, rows), F32),
         sds((images, rows, width), BF)], [sds((2, 16, width), F32)],
        [pltpu.VMEM((per * rows, width), F32)] + wscratch(wa[0]) + [pltpu.VMEM((2, ff), F32)])


def run_top(x, cot, vec, wt, per):
    images, seq, width = x.shape
    rows = pad_rows(seq)
    ff = (wt[0].shape[1] - 4) // 2 * width
    n = per * rows
    cells = lambda c: pltpu.VMEM((per, rows, c), BF)
    tall8 = pltpu.VMEM((per, 8, rows), F32)
    full = lambda r, c: pltpu.VMEM((r, c), F32)
    return call(
        functools.partial(top_kernel, seq), "top", per, [x, cot], [vec], wt,
        [sds((images, seq, width), F32), sds((images, seq, width), F32)], slots(wt[0], wt[0].shape[1] + 1),
        [full(n, width), full(n, width), cells(3 * width), cells(width), tall8, cells(width), cells(width), tall8,
         cells(ff), cells(ff), pltpu.VMEM((per, rows, width), F32), cells(width), cells(3 * width),
         full(width, 3 * width), full(width, width), full(width, ff), full(ff, width), full(8, width), full(8, width),
         full(1, 3 * width), full(1, ff), full(width, width)] + wscratch(wt[0]))


def run_fm(x, o, vec, wm, per):
    images, seq, width = x.shape
    rows = o.shape[1]
    ff = (wm[0].shape[1] - 1) // 2 * width
    return call(
        functools.partial(fm_kernel, seq), "fm", per, [x, o], [vec], wm,
        [sds((images, seq, width), F32), sds((images, rows, ff), BF), sds((images, rows, ff), BF),
         sds((images, rows, width), BF), sds((images, 8, rows), F32)], [],
        [pltpu.VMEM((per * rows, width), F32)] + wscratch(wm[0]))


def slots(own, count):
    half, _, part, width = own.shape
    return [sds((half, count, part, width), BF)] * 2


def run_bm(gr, a, d, xh, rs, o, vec, wm, per):
    images, seq, width = gr.shape
    rows, ff = a.shape[1:]
    return call(
        functools.partial(bm_kernel, seq), "bm", per, [gr, a, d, xh, rs, o], [vec], wm,
        [sds((images, rows, width), F32), sds((images, rows, width), BF)],
        slots(wm[0], wm[0].shape[1]) + [sds((8, width), F32), sds((1, ff), F32)],
        [pltpu.VMEM((per * rows, width), F32), pltpu.VMEM((width, width), F32), pltpu.VMEM((width, ff), F32),
         pltpu.VMEM((ff, width), F32)] + wscratch(wm[0]))


def run_ba(seq, dx1, m, do, xh, aux, vec, vec2, db1, wa, per):
    images, rows, width = dx1.shape
    return call(
        functools.partial(ba_kernel, seq), "ba", per, [dx1, m, do, xh, aux], [vec, vec2, db1], wa,
        [sds((images, seq, width), F32)], slots(wa[0], 4),
        [pltpu.VMEM((per, rows, 3 * width), BF), pltpu.VMEM((width, 3 * width), F32), pltpu.VMEM((8, width), F32),
         pltpu.VMEM((1, 3 * width), F32)] + wscratch(wa[0]) + [pltpu.VMEM((width, width), F32)])


def run_finish(a0, m0, l1, ff):
    part, width = a0[0].shape[1:]
    return pl.pallas_call(
        finish_kernel,
        out_shape=[sds((2, part, 3 * width), F32), sds((2, part, width), F32), sds((2, part, ff), F32),
                   sds((2, ff // width * part, width), F32), sds((2, ff // width * part), F32)]
        + [sds((2, part), F32)] * 8,
        name="finish",
    )(*a0, *m0, *l1)


def xor_pairs(count, b):
    return [(i, i ^ b) for i in range(count)]


def tie(value, *others):
    return lax.optimization_barrier((value, *others))[0]


def group(*values):
    return lax.optimization_barrier(values)


def body(n, reps, tokens, norm1_gain, norm1_shift, qkv_weight, query_bias, value_bias, proj_weight, proj_bias,
         norm2_gain, norm2_shift, fc1_weight, fc1_bias, fc2_weight, fc2_bias, cotangent):
    images, seq, width = tokens.shape
    ff = fc1_weight.shape[2]
    per = 2 if images % 2 == 0 else 1
    upper = []
    b = n // 2
    while b > 2:
        upper.append(b)
        b //= 2

    def swap(x, b):
        return lax.ppermute(x, "shard", xor_pairs(n, b))

    def direct(x):
        masks = [0]
        for b in upper:
            masks = masks + [m ^ b for m in masks]
        return [x] + [swap(x, m) for m in masks[1:]]

    smalls = [norm1_gain, norm1_shift, query_bias, value_bias, proj_bias, norm2_gain, norm2_shift, fc2_bias]
    a0, m0, l1 = run_pack(smalls, fc1_bias, qkv_weight, proj_weight, fc1_weight, fc2_weight)

    a0 = jnp.stack(direct(a0))
    m0 = direct(tie(m0, a0))
    a0x = swap(a0, 2)
    a0 = jnp.concatenate([a0, a0x])
    a0 = (a0, swap(a0, 1))
    m0 = jnp.stack([m0[0]] + [tie(y, a0x) for y in m0[1:]])
    m0x = swap(m0, 2)
    l1 = direct(tie(l1, m0))
    mix, o, aux, xa, vec = run_fa(tie(tokens, m0, l1[0]), a0, ff, per)
    o, m0x, *l1 = group(o, m0x, *l1)
    m0 = jnp.concatenate([m0, m0x])
    l1 = jnp.stack(l1)
    m0 = (m0, swap(tie(m0, l1), 1))
    l1x = swap(l1, 2)
    layer_one, act, der, xm, rs = run_fm(tokens, o, vec, m0, per)
    layer_one, l1x = group(layer_one, l1x)
    l1 = jnp.concatenate([l1, l1x])
    l1 = (l1, swap(l1, 1))
    layer_two, grad, kp, sn = run_top(layer_one, cotangent, vec, l1, per)

    class Sum:
        def __init__(self, keep, send):
            self.keep, self.got, self.send = keep, [], send
            self.bits = [1, 2] + upper[::-1]

        def start(self):
            self.flight = swap(self.send, self.bits[len(self.got)])
            return self

        def done(self):
            self.got.append(self.flight)
            size = self.flight.shape[0]
            if len(self.got) < len(self.bits):
                self.send = self.total(size // 2, size).astype(BF)
            else:
                self.send = self.total(0, 1)[0].astype(BF)
            return self

        def total(self, lo, hi):
            t = self.keep[lo:hi].astype(F32)
            for g in self.got:
                t = t + g[lo:hi].astype(F32)
            return t

        def replicas(self):
            mine, b = self.send, 1
            while True:
                other = lax.ppermute(mine, "replica", xor_pairs(reps, b))
                b *= 2
                if b >= reps:
                    return (mine, other)
                mine = (mine.astype(F32) + other.astype(F32)).astype(BF)

    def meet(value, *sums):
        value, *got = group(value, *[s.flight for s in sums])
        for s, g in zip(sums, got):
            s.flight = g
            s.done()
        return value

    def sent(value, *sums):
        return tie(value, *[s.send for s in sums])

    g1 = Sum(kp, sn).start().done().start()
    dx1, do, kp, sn, v2, db1 = run_bm(sent(grad, g1), act, der, xm, rs, o, vec, m0, per)
    do = meet(do, g1)
    g1.start()
    gm0 = Sum(kp, sn).start()
    tokens_grad, kp, sn = run_ba(seq, dx1, mix, sent(do, g1), xa, aux, vec, v2, db1, a0, per)
    sn, g1.flight, gm0.flight = group(sn, g1.flight, gm0.flight)
    ga0 = Sum(kp, sn).start()
    gm0.done().start()
    g1.done().start()
    ga0.flight = tie(ga0.flight, gm0.send)
    ga0.done().start()
    gm0.done().start()
    g1.flight = tie(g1.flight, ga0.send)
    g1.done()
    fin_1 = g1.replicas()
    ga0.done().start()
    gm0.done().start()
    ga0.done().start()
    gm0.done()
    fin_m0 = gm0.replicas()
    ga0.done()
    fin_a0 = ga0.replicas()

    g_qkv, g_proj, g_up, g_down, g_bup, *s = run_finish(fin_a0, fin_m0, fin_1, ff)
    return (layer_one, layer_two, tokens_grad, s[0], s[1], g_qkv, s[2], s[3], g_proj, s[4], s[5], s[6],
            g_up, g_bup, g_down, s[7])
def solution(mesh):
    n = mesh.shape["shard"]
    reps = mesh.shape["replica"]
    batch = P(("replica", "shard"), None, None)
    row2 = P(None, "shard")
    row3 = P(None, "shard", None)
    in_specs = (batch, row2, row2, row3, row2, row2, row3, row2, row2, row2, row3, row2, row3, row2, batch)
    out_specs = (batch, batch, batch, row2, row2, row3, row2, row2, row3, row2, row2, row2, row3, row2, row3, row2)
    return jax.shard_map(
        functools.partial(body, n, reps), mesh=mesh, in_specs=in_specs, out_specs=out_specs, check_vma=False
    )
```

```python
import functools
import jax
import jax.numpy as jnp
from jax import lax
from jax.sharding import PartitionSpec as P
from jax.experimental import pallas as pl
from jax.experimental.pallas import tpu as pltpu

BF = jnp.bfloat16
F32 = jnp.float32
HEADS = 6
EPS = 1e-06
NEG = -1e30
VMEM_LIMIT = 54 * 2**20


def dot(a, b):
    return jnp.dot(a, b, preferred_element_type=F32)


def dot_nt(a, b):
    return lax.dot_general(a, b, (((1,), (1,)), ((), ())), preferred_element_type=F32)


def dot_tn(a, b):
    return lax.dot_general(a, b, (((0,), (0,)), ((), ())), preferred_element_type=F32)


def pad_rows(seq):
    return (seq + 15) // 16 * 16


def colsum(x):
    return jnp.sum(x, 0, keepdims=True)


def slot_masks(n):
    masks = [0]
    b = n // 2
    while b > 1:
        masks = masks + [m ^ b for m in masks]
        b //= 2
    return masks


def start_weights(own, other, dst, sems):
    idx = lax.axis_index("shard")
    for s, mask in enumerate(slot_masks(dst.shape[0])):
        pltpu.make_async_copy(own.at[s], dst.at[jnp.bitwise_xor(idx, mask)], sems.at[2 * s]).start()
        pltpu.make_async_copy(other.at[s], dst.at[jnp.bitwise_xor(idx, mask + 1)], sems.at[2 * s + 1]).start()


def wait_weights(own, other, dst, sems):
    idx = lax.axis_index("shard")
    for s, mask in enumerate(slot_masks(dst.shape[0])):
        pltpu.make_async_copy(own.at[s], dst.at[jnp.bitwise_xor(idx, mask)], sems.at[2 * s]).wait()
        pltpu.make_async_copy(other.at[s], dst.at[jnp.bitwise_xor(idx, mask + 1)], sems.at[2 * s + 1]).wait()


def first_step(*fs):
    @pl.when(pl.program_id(0) == 0)
    def _():
        for f in fs:
            f()


def flat(v):
    return v.reshape(v.shape[0] * v.shape[1], v.shape[2])


def slabs(w, first, count):
    return jnp.concatenate([flat(w[:, k]) for k in range(first, first + count)], 1) if count > 1 else flat(w[:, first])


def tall(w, first, count):
    v = w[:, first : first + count]
    return v.reshape(v.shape[0] * v.shape[1] * v.shape[2], v.shape[3])


def store_slots(keep, send, pieces):
    half = keep.shape[0]
    idx = lax.axis_index("shard")
    for s, mask in enumerate(slot_masks(2 * half)):
        for dst, extra in ((keep, 0), (send, 1)):
            owner = jnp.bitwise_xor(idx, mask + extra)
            for k, piece in enumerate(pieces):
                dst[s, k] = piece(owner).astype(dst.dtype)


def rows_of(ref, part, col, width):
    return lambda owner: ref[pl.ds(pl.multiple_of(owner * part, 8), part), col * width : (col + 1) * width]


def tall_rows_of(ref, part, q, count):
    return lambda owner: ref[pl.ds(pl.multiple_of((owner * count + q) * part, 8), part), :]


def normalise(x):
    mean = jnp.mean(x, -1, keepdims=True)
    cen = x - mean
    rstd = lax.rsqrt(jnp.mean(cen * cen, -1, keepdims=True) + EPS)
    return cen * rstd, rstd


def norm_back(dxhat, xhat, rstd):
    return rstd * (
        dxhat
        - jnp.mean(dxhat, -1, keepdims=True)
        - xhat * jnp.mean(dxhat * xhat, -1, keepdims=True)
    )


def gelu_both(h):
    phi = 0.5 + 0.5 * lax.erf(h * 0.7071067811865476)
    return h * phi, phi + h * (jnp.exp(h * h * -0.5) * 0.3989422804014327)


def to_rows(cols):
    return cols.T[0:8]


def to_column(rows8, r):
    full = jnp.concatenate([rows8, jnp.zeros((120, rows8.shape[1]), F32)], 0)
    return full.T[:, r : r + 1]


def load_padded(dst, src, seq, rows, images):
    for g in range(images):
        dst[g * rows : g * rows + seq] = src[g].astype(F32)
        dst[g * rows + seq : (g + 1) * rows] = jnp.zeros((rows - seq, dst.shape[1]), F32)


def pack_kernel(*refs):
    smalls, (bias_up, w_qkv, w_proj, w_up, w_down) = refs[:8], refs[8:13]
    out_a0, out_l1, sq = refs[13:]
    part, width = out_a0.shape[1:]
    sq[...] = jnp.zeros_like(sq)
    for p, ref in enumerate(smalls):
        sq[2 * p : 2 * p + 2, 0:part] = ref[...].astype(F32)
    hid = bias_up.shape[1]
    out_a0[3] = jnp.zeros((part, width), BF)
    out_a0[3, :, 0:128] = sq[...].T[0:part].astype(BF)
    out_a0[3, 0:2, width - hid :] = bias_up[...]
    quart = w_up.shape[2] // width
    for layer in range(2):
        attn = out_a0 if layer == 0 else out_l1
        rest, base = (out_a0, 4) if layer == 0 else (out_l1, 3)
        for k in range(3):
            attn[k] = w_qkv[layer, :, k * width : (k + 1) * width]
        rest[base] = w_proj[layer]
        for q in range(quart):
            rest[base + 1 + q] = w_up[layer, :, q * width : (q + 1) * width]
            rest[base + 1 + quart + q] = w_down[layer, q * part : (q + 1) * part]


def unpack_small(w, vec, tmp):
    shards, _, part, width = w.shape
    hid = tmp.shape[1] // shards
    rows = flat(w[:, 3, :, 0:128]).astype(F32).T
    for j in range(shards):
        tmp[:, j * hid : (j + 1) * hid] = w[j, 3, 0:2, width - hid :].astype(F32)
    quart = tmp.shape[1] // width
    for layer in range(2):
        for p in range(8):
            vec[layer, p : p + 1] = rows[2 * p + layer : 2 * p + layer + 1]
        for q in range(quart):
            vec[layer, 8 + q : 9 + q] = tmp[layer : layer + 1, q * width : (q + 1) * width]
        vec[layer, 8 + quart :] = jnp.zeros((8 - quart, width), F32)


def attn_forward(seq, xs, vec, w, m_ref, o_ref, aux_ref, xh_ref):
    images, rows, width = o_ref.shape
    xhat, rstd = normalise(xs[...])
    xh_ref[...] = xhat.astype(BF).reshape(images, rows, width)
    n1 = (xhat * vec[0:1, :] + vec[1:2, :]).astype(BF)
    for c in range(3):
        cs = slice(c * width, (c + 1) * width)
        mc = dot(n1, slabs(w, c, 1))
        if c != 1:
            mc = mc + (vec[2:3, :] if c == 0 else vec[3:4, :])
        m_ref[:, :, cs] = mc.astype(BF).reshape(images, rows, width)
    lane = lax.broadcasted_iota(jnp.int32, (rows, 128), 1)
    row = lax.broadcasted_iota(jnp.int32, (rows, 128), 0)
    low = lane < 64
    kpad = jnp.where(row >= seq, NEG, 0.0).astype(BF)
    ones = jnp.where(row >= seq, 0.0, 1.0).astype(BF)
    first = lax.broadcasted_iota(jnp.int32, (1, 128), 1)
    mine = [jnp.where(first < 64, 1.0, 0.0).astype(BF), jnp.where(first < 64, 0.0, 1.0).astype(BF)]
    mark = [jnp.where(first == 64, 1.0, 0.0).astype(BF), jnp.where(first == 0, 1.0, 0.0).astype(BF)]
    kpads = [kpad * mark[0], kpad * mark[1]]
    for g in range(images):
        aux = jnp.broadcast_to(rstd[g * rows : (g + 1) * rows], (rows, 128))
        for p in range(width // 128):
            q2 = m_ref[g, :, p * 128 : (p + 1) * 128] * jnp.asarray(0.125, BF)
            k2 = m_ref[g, :, width + p * 128 : width + (p + 1) * 128]
            v2 = m_ref[g, :, 2 * width + p * 128 : 2 * width + (p + 1) * 128]
            vext = jnp.concatenate([v2 * ones, ones], 1)
            parts = []
            for half in range(2):
                s = dot_nt(q2 * mine[half] + mark[half], k2 * mine[half] + kpads[half])
                mx = jnp.max(s, -1, keepdims=True)
                pr = jnp.exp(s - mx).astype(BF)
                oe = dot(pr, vext)
                tot = oe[:, 128:]
                parts.append(oe[:, :128] / tot)
                aux = jnp.where(lane == 2 * p + half, mx + jnp.log(tot), aux)
            o_ref[g, :, p * 128 : (p + 1) * 128] = jnp.where(low, parts[0], parts[1]).astype(BF)
        aux_ref[g] = to_rows(aux)


def mlp_forward(seq, xs, o_ref, vec, w, base, out_ref, a_ref, d_ref, xh_ref, rs_ref):
    images, rows, width = o_ref.shape
    x1 = xs[...] + dot(flat(o_ref[...]), slabs(w, base, 1)) + vec[4:5, :]
    xhat, rstd = normalise(x1)
    xh_ref[...] = xhat.astype(BF).reshape(images, rows, width)
    for g in range(images):
        rs_ref[g] = to_rows(jnp.broadcast_to(rstd[g * rows : (g + 1) * rows], (rows, 128)))
    n2 = (xhat * vec[5:6, :] + vec[6:7, :]).astype(BF)
    acc = x1 + vec[7:8, :]
    quart = a_ref.shape[2] // width
    w2 = tall(w, base + 1 + quart, quart)
    for c in range(quart // 2):
        cs = slice(2 * c * width, 2 * (c + 1) * width)
        bias = jnp.concatenate([vec[8 + 2 * c : 9 + 2 * c, :], vec[9 + 2 * c : 10 + 2 * c, :]], 1)
        h = dot(n2, slabs(w, base + 1 + 2 * c, 2)) + bias
        a, d = gelu_both(h)
        a = a.astype(BF)
        a_ref[:, :, cs] = a.reshape(images, rows, 2 * width)
        d_ref[:, :, cs] = d.astype(BF).reshape(images, rows, 2 * width)
        acc = acc + dot(a, w2[cs, :])
    acc = acc.reshape(images, rows, width)
    for g in range(images):
        out_ref[g] = acc[g, :seq]


def zero(*refs):
    for r in refs:
        r[...] = jnp.zeros_like(r)


def mlp_backward(gs, a_ref, d_ref, xh_ref, rs_ref, o_ref, vec, w, base, dx1_ref, do_ref, dwp, dw1, dw2, vec_o, db1_o):
    images, rows, width = xh_ref.shape
    n = images * rows
    dz = gs[...].astype(BF)
    xhat = flat(xh_ref[...]).astype(F32)
    n2 = (xhat * vec[5:6, :] + vec[6:7, :]).astype(BF)
    dn2 = jnp.zeros((n, width), F32)
    quart = a_ref.shape[2] // width
    w2 = tall(w, base + 1 + quart, quart)
    for c in range(quart // 2):
        cs = slice(2 * c * width, 2 * (c + 1) * width)
        a = flat(a_ref[:, :, cs])
        d = flat(d_ref[:, :, cs])
        da = dot_nt(dz, w2[cs, :])
        dh = (d.astype(F32) * da).astype(BF)
        db1_o[:, cs] += colsum(dh.astype(F32))
        dw2[cs, :] += dot_tn(a, dz)
        dw1[:, cs] += dot_tn(n2, dh)
        dn2 = dn2 + dot_nt(dh, slabs(w, base + 1 + 2 * c, 2))
    rstd = jnp.concatenate([to_column(rs_ref[g], 0) for g in range(images)], 0)
    dx1 = gs[...] + norm_back(dn2 * vec[5:6, :], xhat, rstd)
    dx1_ref[...] = dx1.reshape(images, rows, width).astype(dx1_ref.dtype)
    dy = dx1.astype(BF)
    dwp[...] += dot_tn(flat(o_ref[...]), dy)
    do_ref[...] = dot_nt(dy, slabs(w, base, 1)).astype(BF).reshape(images, rows, width)
    vec_o[0:1, :] += colsum(dz.astype(F32))
    vec_o[1:2, :] += colsum(dn2 * xhat)
    vec_o[2:3, :] += colsum(dn2)
    vec_o[3:4, :] += colsum(dy.astype(F32))


def attn_backward(seq, m_ref, do_ref, aux_ref, dm_ref):
    images, rows, width = do_ref.shape
    lane = lax.broadcasted_iota(jnp.int32, (rows, 128), 1)
    low = lane < 64
    last = rows - 16
    valid = lax.broadcasted_iota(jnp.int32, (16, rows), 0) < seq - last
    first = lax.broadcasted_iota(jnp.int32, (1, 128), 1)
    mine = [jnp.where(first < 64, 1.0, 0.0).astype(BF), jnp.where(first < 64, 0.0, 1.0).astype(BF)]
    def scores(g, p):
        q2 = m_ref[g, :, p * 128 : (p + 1) * 128] * jnp.asarray(0.125, BF)
        k2 = m_ref[g, :, width + p * 128 : width + (p + 1) * 128]
        v2 = m_ref[g, :, 2 * width + p * 128 : 2 * width + (p + 1) * 128]
        do2 = do_ref[g, :, p * 128 : (p + 1) * 128]
        st = [dot_nt(k2 * mine[half], q2) for half in range(2)]
        dp = [dot_nt(v2 * mine[half], do2) for half in range(2)]
        return q2, k2, do2, st, dp

    def weigh(g, p, got):
        q2, k2, do2, st, dp = got
        pts, dsts = [], []
        for half in range(2):
            h = 2 * p + half
            sh = st[half] - aux_ref[g, h : h + 1, :]
            pt = jnp.exp(jnp.concatenate([sh[:last], jnp.where(valid, sh[last:], NEG)], 0))
            pd = pt * dp[half]
            dsts.append((pd - pt * colsum(pd)).astype(BF))
            pts.append(pt.astype(BF))
        return q2, k2, do2, pts, dsts

    def finish(g, p, got):
        q2, k2, do2, pts, dsts = got
        kt = (k2 * jnp.asarray(0.125, BF)).T
        dvs = [dot(pts[half], do2) for half in range(2)]
        dks = [dot(dsts[half], q2) for half in range(2)]
        dqs = [dot(kt[half * 64 : half * 64 + 64], dsts[half]) for half in range(2)]
        dm_ref[g, :, p * 128 : (p + 1) * 128] = jnp.concatenate(dqs, 0).T.astype(BF)
        dm_ref[g, :, width + p * 128 : width + (p + 1) * 128] = jnp.where(low, dks[0], dks[1]).astype(BF)
        dm_ref[g, :, 2 * width + p * 128 : 2 * width + (p + 1) * 128] = jnp.where(low, dvs[0], dvs[1]).astype(BF)

    items = [(g, p) for g in range(images) for p in range(width // 128)]
    ahead = scores(*items[0])
    for t, item in enumerate(items):
        got = weigh(*item, ahead)
        if t + 1 < len(items):
            ahead = scores(*items[t + 1])
        finish(*item, got)


def qkv_backward(seq, dx1_ref, dm_ref, xh_ref, aux_ref, vec, w, dx_ref, dwqkv, vec_s, dbm_s):
    images, rows, width = xh_ref.shape
    dm = flat(dm_ref[...])
    dbm_s[...] += colsum(dm.astype(F32))
    xhat = flat(xh_ref[...]).astype(F32)
    n1 = (xhat * vec[0:1, :] + vec[1:2, :]).astype(BF)
    dwqkv[...] += dot_tn(n1, dm)
    dn1 = dot_nt(dm, slabs(w, 0, 3))
    vec_s[0:1, :] += colsum(dn1 * xhat)
    vec_s[1:2, :] += colsum(dn1)
    rstd = jnp.concatenate([to_column(aux_ref[g], 7) for g in range(images)], 0)
    dx = flat(dx1_ref[...]).astype(F32) + norm_back(dn1 * vec[0:1, :], xhat, rstd)
    dx = dx.reshape(images, rows, width)
    for g in range(images):
        dx_ref[g] = dx[g, :seq].astype(dx_ref.dtype)


def small_slab(sm, vec_s, dbm_s, vec2, db1, part):
    width = sm.shape[0]
    small = jnp.concatenate(
        [vec_s[0:2, :], dbm_s[:, :width], dbm_s[:, 2 * width :], vec2[3:4, :], vec2[1:3, :], vec2[0:1, :],
         jnp.zeros((120, width), F32)], 0)
    sm[...] = jnp.zeros_like(sm)
    sm[:, 0:128] = small.T
    shards = width // part
    hid = db1.shape[1] // shards
    for j in range(shards):
        sm[j * part : j * part + 1, width - hid :] = db1[:, j * hid : (j + 1) * hid]


def attn_pieces(dwqkv, sm, part):
    width = sm.shape[0]
    return [rows_of(dwqkv, part, c, width) for c in range(3)] + [rows_of(sm, part, 0, width)]


def mlp_pieces(dwp, dw1, dw2, part):
    width = dwp.shape[0]
    quart = dw1.shape[1] // width
    return ([rows_of(dwp, part, 0, width)] + [rows_of(dw1, part, q, width) for q in range(quart)]
            + [tall_rows_of(dw2, part, q, quart) for q in range(quart)])


def last_step(f):
    pl.when(pl.program_id(0) == pl.num_programs(0) - 1)(f)


def fa_kernel(seq, x_ref, own, other, m_ref, o_ref, aux_ref, xh_ref, vec_ref, xs, w, sems, tmp):
    first_step(lambda: start_weights(own, other, w, sems))
    images, rows, _ = o_ref.shape
    load_padded(xs, x_ref, seq, rows, images)
    first_step(lambda: wait_weights(own, other, w, sems), lambda: unpack_small(w, vec_ref, tmp))
    attn_forward(seq, xs, vec_ref.at[0], w, m_ref, o_ref, aux_ref, xh_ref)


def fm_kernel(seq, x_ref, o_ref, vec_ref, own, other, out_ref, a_ref, d_ref, xh_ref, rs_ref, xs, w, sems):
    first_step(lambda: start_weights(own, other, w, sems))
    images, rows, _ = o_ref.shape
    load_padded(xs, x_ref, seq, rows, images)
    first_step(lambda: wait_weights(own, other, w, sems))
    mlp_forward(seq, xs, o_ref, vec_ref.at[0], w, 0, out_ref, a_ref, d_ref, xh_ref, rs_ref)


def bm_kernel(seq, gr_ref, a_ref, d_ref, xh_ref, rs_ref, o_ref, vec_ref, own, other,
              dx1_ref, do_ref, keep, send, vec_o, db1_o, gs, dwp, dw1, dw2, w, sems):
    images, rows, width = xh_ref.shape
    first_step(lambda: start_weights(own, other, w, sems), lambda: zero(dwp, dw1, dw2, vec_o, db1_o))
    load_padded(gs, gr_ref, seq, rows, images)
    first_step(lambda: wait_weights(own, other, w, sems))
    mlp_backward(gs, a_ref, d_ref, xh_ref, rs_ref, o_ref, vec_ref.at[0], w, 0, dx1_ref, do_ref, dwp, dw1, dw2, vec_o, db1_o)

    @last_step
    def _():
        store_slots(keep, send, mlp_pieces(dwp, dw1, dw2, w.shape[2]))


def ba_kernel(seq, dx1_ref, m_ref, do_ref, xh_ref, aux_ref, vec_ref, vec2, db1, own, other,
              dx_ref, keep, send, dm_s, dwqkv, vec_s, dbm_s, w, sems, sm):
    first_step(lambda: start_weights(own, other, w, sems), lambda: zero(dwqkv, vec_s, dbm_s))
    attn_backward(seq, m_ref, do_ref, aux_ref, dm_s)
    first_step(lambda: wait_weights(own, other, w, sems))
    qkv_backward(seq, dx1_ref, dm_s, xh_ref, aux_ref, vec_ref.at[0], w, dx_ref, dwqkv, vec_s, dbm_s)

    @last_step
    def _():
        part = w.shape[2]
        small_slab(sm, vec_s, dbm_s, vec2, db1, part)
        store_slots(keep, send, attn_pieces(dwqkv, sm, part))


def top_kernel(seq, x_ref, cot_ref, vec_ref, own, other, out_ref, dx_ref, keep, send,
               xs, gs, m_s, o_s, aux_s, xa_s, xm_s, rs_s, a_s, d_s, dx1_s, do_s, dm_s,
               dwqkv, dwp, dw1, dw2, vec_a, vec_m, dbm_s, db1_s, sm, w, sems):
    images, rows, width = o_s.shape
    vec = vec_ref.at[1]
    first_step(lambda: start_weights(own, other, w, sems),
               lambda: zero(dwqkv, dwp, dw1, dw2, vec_a, vec_m, dbm_s, db1_s))
    load_padded(xs, x_ref, seq, rows, images)
    load_padded(gs, cot_ref, seq, rows, images)
    first_step(lambda: wait_weights(own, other, w, sems))
    attn_forward(seq, xs, vec, w, m_s, o_s, aux_s, xa_s)
    mlp_forward(seq, xs, o_s, vec, w, 3, out_ref, a_s, d_s, xm_s, rs_s)
    mlp_backward(gs, a_s, d_s, xm_s, rs_s, o_s, vec, w, 3, dx1_s, do_s, dwp, dw1, dw2, vec_m, db1_s)
    attn_backward(seq, m_s, do_s, aux_s, dm_s)
    qkv_backward(seq, dx1_s, dm_s, xa_s, aux_s, vec, w, dx_ref, dwqkv, vec_a, dbm_s)

    @last_step
    def _():
        part = w.shape[2]
        small_slab(sm, vec_a, dbm_s, vec_m, db1_s, part)
        store_slots(keep, send, attn_pieces(dwqkv, sm, part) + mlp_pieces(dwp, dw1, dw2, part))


def finish_kernel(*refs):
    ins, outs = refs[:6], refs[6:]
    o_qkv, o_proj, o_up, o_down, o_bup = outs[:5]
    smalls = outs[5:]
    part, width = ins[0].shape[1:]
    hid = o_bup.shape[1]
    quart = o_up.shape[2] // width
    for layer in range(2):
        a1, a2 = ins[4:6] if layer == 1 else ins[0:2]
        m1, m2, base = (*ins[4:6], 4) if layer == 1 else (*ins[2:4], 0)
        for k in range(3):
            o_qkv[layer, :, k * width : (k + 1) * width] = a1[k].astype(F32) + a2[k].astype(F32)
        small = a1[3].astype(F32) + a2[3].astype(F32)
        o_bup[layer : layer + 1, :] = small[0:1, width - hid :]
        pad = jnp.concatenate([small[:, 0:128], jnp.zeros((128 - part, 128), F32)], 0).T
        for p, ref in enumerate(smalls):
            ref[layer : layer + 1, :] = pad[p : p + 1, 0:part]

        def both(k):
            return m1[base + k].astype(F32) + m2[base + k].astype(F32)

        o_proj[layer] = both(0)
        for q in range(quart):
            o_up[layer, :, q * width : (q + 1) * width] = both(1 + q)
            o_down[layer, q * part : (q + 1) * part] = both(1 + quart + q)


def blk(shape):
    nd = len(shape)
    return pl.BlockSpec(shape, lambda i: (i,) + (0,) * (nd - 1))


def whole(arr):
    nd = len(arr.shape)
    return pl.BlockSpec(arr.shape, lambda i: (0,) * nd)


def anyspec():
    return pl.BlockSpec(memory_space=pl.ANY)


def sds(shape, dt):
    return jax.ShapeDtypeStruct(shape, dt)


COST = {"fa": 13, "fm": 18, "bm": 26, "ba": 28, "top": 70}


def call(kern, name, per, blocked_in, whole_in, any_in, blocked_out, whole_out, scratch):
    in_specs = [blk((per,) + a.shape[1:]) for a in blocked_in] + [whole(a) for a in whole_in] + [anyspec() for _ in any_in]
    out_specs = [blk((per,) + a.shape[1:]) for a in blocked_out] + [whole(a) for a in whole_out]
    return pl.pallas_call(
        kern,
        grid=(blocked_in[0].shape[0] // per,),
        in_specs=in_specs,
        out_specs=out_specs,
        out_shape=list(blocked_out) + list(whole_out),
        scratch_shapes=scratch,
        compiler_params=pltpu.CompilerParams(vmem_limit_bytes=VMEM_LIMIT),
        name=name,
        cost_estimate=pl.CostEstimate(flops=COST[name] * 1_150_000_000, bytes_accessed=0, transcendentals=0),
    )(*blocked_in, *whole_in, *any_in)


def wscratch(own):
    return [pltpu.VMEM((2 * own.shape[0],) + own.shape[1:], BF), pltpu.SemaphoreType.DMA((2 * own.shape[0],))]


def run_pack(smalls, bias_up, w_qkv, w_proj, w_up, w_down):
    part, width = w_proj.shape[1:]
    quart = w_up.shape[2] // width
    return pl.pallas_call(
        pack_kernel,
        out_shape=[sds((5 + 2 * quart, part, width), BF), sds((4 + 2 * quart, part, width), BF)],
        scratch_shapes=[pltpu.VMEM((128, 128), F32)],
        name="pack",
    )(*smalls, bias_up, w_qkv, w_proj, w_up, w_down)


def run_fa(x, wa, ff, per):
    images, seq, width = x.shape
    rows = pad_rows(seq)
    return call(
        functools.partial(fa_kernel, seq), "fa", per, [x], [], wa,
        [sds((images, rows, 3 * width), BF), sds((images, rows, width), BF), sds((images, 8, rows), F32),
         sds((images, rows, width), BF)], [sds((2, 16, width), F32)],
        [pltpu.VMEM((per * rows, width), F32)] + wscratch(wa[0]) + [pltpu.VMEM((2, ff), F32)])


def run_top(x, cot, vec, wt, per):
    images, seq, width = x.shape
    rows = pad_rows(seq)
    ff = (wt[0].shape[1] - 4) // 2 * width
    n = per * rows
    cells = lambda c: pltpu.VMEM((per, rows, c), BF)
    tall8 = pltpu.VMEM((per, 8, rows), F32)
    full = lambda r, c: pltpu.VMEM((r, c), F32)
    return call(
        functools.partial(top_kernel, seq), "top", per, [x, cot], [vec], wt,
        [sds((images, seq, width), F32), sds((images, seq, width), BF)], slots(wt[0], wt[0].shape[1] + 1),
        [full(n, width), full(n, width), cells(3 * width), cells(width), tall8, cells(width), cells(width), tall8,
         cells(ff), cells(ff), pltpu.VMEM((per, rows, width), F32), cells(width), cells(3 * width),
         full(width, 3 * width), full(width, width), full(width, ff), full(ff, width), full(8, width), full(8, width),
         full(1, 3 * width), full(1, ff), full(width, width)] + wscratch(wt[0]))


def run_fm(x, o, vec, wm, per):
    images, seq, width = x.shape
    rows = o.shape[1]
    ff = (wm[0].shape[1] - 1) // 2 * width
    return call(
        functools.partial(fm_kernel, seq), "fm", per, [x, o], [vec], wm,
        [sds((images, seq, width), F32), sds((images, rows, ff), BF), sds((images, rows, ff), BF),
         sds((images, rows, width), BF), sds((images, 8, rows), F32)], [],
        [pltpu.VMEM((per * rows, width), F32)] + wscratch(wm[0]))


def slots(own, count):
    half, _, part, width = own.shape
    return [sds((half, count, part, width), BF)] * 2


def run_bm(gr, a, d, xh, rs, o, vec, wm, per):
    images, seq, width = gr.shape
    rows, ff = a.shape[1:]
    return call(
        functools.partial(bm_kernel, seq), "bm", per, [gr, a, d, xh, rs, o], [vec], wm,
        [sds((images, rows, width), BF), sds((images, rows, width), BF)],
        slots(wm[0], wm[0].shape[1]) + [sds((8, width), F32), sds((1, ff), F32)],
        [pltpu.VMEM((per * rows, width), F32), pltpu.VMEM((width, width), F32), pltpu.VMEM((width, ff), F32),
         pltpu.VMEM((ff, width), F32)] + wscratch(wm[0]))


def run_ba(seq, dx1, m, do, xh, aux, vec, vec2, db1, wa, per):
    images, rows, width = dx1.shape
    return call(
        functools.partial(ba_kernel, seq), "ba", per, [dx1, m, do, xh, aux], [vec, vec2, db1], wa,
        [sds((images, seq, width), F32)], slots(wa[0], 4),
        [pltpu.VMEM((per, rows, 3 * width), BF), pltpu.VMEM((width, 3 * width), F32), pltpu.VMEM((8, width), F32),
         pltpu.VMEM((1, 3 * width), F32)] + wscratch(wa[0]) + [pltpu.VMEM((width, width), F32)])


def run_finish(a0, m0, l1, ff):
    part, width = a0[0].shape[1:]
    return pl.pallas_call(
        finish_kernel,
        out_shape=[sds((2, part, 3 * width), F32), sds((2, part, width), F32), sds((2, part, ff), F32),
                   sds((2, ff // width * part, width), F32), sds((2, ff // width * part), F32)]
        + [sds((2, part), F32)] * 8,
        name="finish",
    )(*a0, *m0, *l1)


def xor_pairs(count, b):
    return [(i, i ^ b) for i in range(count)]


def tie(value, *others):
    return lax.optimization_barrier((value, *others))[0]


def group(*values):
    return lax.optimization_barrier(values)


def body(n, reps, tokens, norm1_gain, norm1_shift, qkv_weight, query_bias, value_bias, proj_weight, proj_bias,
         norm2_gain, norm2_shift, fc1_weight, fc1_bias, fc2_weight, fc2_bias, cotangent):
    images, seq, width = tokens.shape
    ff = fc1_weight.shape[2]
    per = 2 if images % 2 == 0 else 1
    upper = []
    b = n // 2
    while b > 2:
        upper.append(b)
        b //= 2

    def swap(x, b):
        return lax.ppermute(x, "shard", xor_pairs(n, b))

    def direct(x):
        masks = [0]
        for b in upper:
            masks = masks + [m ^ b for m in masks]
        return [x] + [swap(x, m) for m in masks[1:]]

    smalls = [norm1_gain, norm1_shift, query_bias, value_bias, proj_bias, norm2_gain, norm2_shift, fc2_bias]
    am, l1 = run_pack(smalls, fc1_bias, qkv_weight, proj_weight, fc1_weight, fc2_weight)

    am = direct(am)
    a0 = jnp.stack([y[:4] for y in am])
    m0 = jnp.stack([y[4:] for y in am])
    a0x = swap(a0, 2)
    l1 = direct(tie(l1, a0))
    a0 = jnp.concatenate([a0, a0x])
    m0x = swap(tie(m0, a0x), 2)
    a0 = (a0, swap(a0, 1))
    mix, o, aux, xa, vec = run_fa(tie(tokens, m0, l1[0]), a0, ff, per)
    o, m0x, *l1 = group(o, m0x, *l1)
    m0 = jnp.concatenate([m0, m0x])
    l1 = jnp.stack(l1)
    m0 = (m0, swap(tie(m0, l1), 1))
    l1x = swap(l1, 2)
    layer_one, act, der, xm, rs = run_fm(tokens, o, vec, m0, per)
    layer_one, l1x = group(layer_one, l1x)
    l1 = jnp.concatenate([l1, l1x])
    l1 = (l1, swap(l1, 1))
    layer_two, grad, kp, sn = run_top(layer_one, cotangent, vec, l1, per)

    class Sum:
        def __init__(self, keep, send):
            self.keep, self.got, self.send = keep, [], send
            self.bits = [1, 2] + upper[::-1]

        def start(self):
            self.flight = swap(self.send, self.bits[len(self.got)])
            return self

        def done(self):
            self.got.append(self.flight)
            size = self.flight.shape[0]
            if len(self.got) < len(self.bits):
                self.send = self.total(size // 2, size).astype(BF)
            else:
                self.send = self.total(0, 1)[0].astype(BF)
            return self

        def scatter(self):
            self.rest = self.total(0, 1)[0]
            masks = [0]
            for b in upper:
                masks = masks + [m ^ b for m in masks]
            sends = [self.total(z, z + 1)[0].astype(BF) for z in range(1, len(masks))]
            self.send = sends
            self.flight = [swap(s, m) for s, m in zip(sends, masks[1:])]
            return self

        def collect(self):
            total = self.rest
            for f in self.flight:
                total = total + f.astype(F32)
            self.send = total.astype(BF)
            return self

        def total(self, lo, hi):
            t = self.keep[lo:hi].astype(F32)
            for g in self.got:
                t = t + g[lo:hi].astype(F32)
            return t

        def replicas(self):
            mine, b = self.send, 1
            while True:
                other = lax.ppermute(mine, "replica", xor_pairs(reps, b))
                b *= 2
                if b >= reps:
                    return (mine, other)
                mine = (mine.astype(F32) + other.astype(F32)).astype(BF)

    def meet(value, *sums):
        value, *got = group(value, *[s.flight for s in sums])
        for s, g in zip(sums, got):
            s.flight = g
            s.done()
        return value

    def sent(value, *sums):
        return tie(value, *[s.send for s in sums])

    g1 = Sum(kp, sn).start().done().start()
    dx1, do, kp, sn, v2, db1 = run_bm(sent(grad, g1), act, der, xm, rs, o, vec, m0, per)
    do, sn, g1.flight = group(do, sn, g1.flight)
    gm0 = Sum(kp, sn).start()
    g1.got.append(g1.flight)
    g1.scatter()
    gm0.done().start()
    tokens_grad, kp, sn = run_ba(seq, dx1, mix, tie(do, *g1.send, gm0.send), xa, aux, vec, v2, db1, a0, per)
    sn, gm0.flight, *g1.flight = group(sn, gm0.flight, *g1.flight)
    ga0 = Sum(kp, sn).start()
    gm0.done().start()
    g1.collect()
    ga0.flight = tie(ga0.flight, gm0.send)
    ga0.done().start()
    g1.send = tie(g1.send, ga0.send)
    fin_1 = g1.replicas()
    gm0.done().start()
    ga0.done().start()
    gm0.done()
    fin_m0 = gm0.replicas()
    ga0.done().start()
    ga0.done()
    fin_a0 = ga0.replicas()

    g_qkv, g_proj, g_up, g_down, g_bup, *s = run_finish(fin_a0, fin_m0, fin_1, ff)
    return (layer_one, layer_two, tokens_grad, s[0], s[1], g_qkv, s[2], s[3], g_proj, s[4], s[5], s[6],
            g_up, g_bup, g_down, s[7])
def solution(mesh):
    n = mesh.shape["shard"]
    reps = mesh.shape["replica"]
    batch = P(("replica", "shard"), None, None)
    row2 = P(None, "shard")
    row3 = P(None, "shard", None)
    in_specs = (batch, row2, row2, row3, row2, row2, row3, row2, row2, row2, row3, row2, row3, row2, batch)
    out_specs = (batch, batch, batch, row2, row2, row3, row2, row2, row3, row2, row2, row2, row3, row2, row3, row2)
    return jax.shard_map(
        functools.partial(body, n, reps), mesh=mesh, in_specs=in_specs, out_specs=out_specs, check_vma=False
    )
```

```python
import functools
import jax
import jax.numpy as jnp
from jax import lax
from jax.sharding import PartitionSpec as P
from jax.experimental import pallas as pl
from jax.experimental.pallas import tpu as pltpu

BF = jnp.bfloat16
F32 = jnp.float32
HEADS = 6
EPS = 1e-06
NEG = -1e30
VMEM_LIMIT = 54 * 2**20


def dot(a, b):
    return jnp.dot(a, b, preferred_element_type=F32)


def dot_nt(a, b):
    return lax.dot_general(a, b, (((1,), (1,)), ((), ())), preferred_element_type=F32)


def dot_tn(a, b):
    return lax.dot_general(a, b, (((0,), (0,)), ((), ())), preferred_element_type=F32)


def pad_rows(seq):
    return (seq + 15) // 16 * 16


def colsum(x):
    return jnp.sum(x, 0, keepdims=True)


def slot_masks(n):
    masks = [0]
    b = n // 2
    while b > 1:
        masks = masks + [m ^ b for m in masks]
        b //= 2
    return masks


def start_weights(own, other, dst, sems):
    idx = lax.axis_index("shard")
    for s, mask in enumerate(slot_masks(dst.shape[0])):
        pltpu.make_async_copy(own.at[s], dst.at[jnp.bitwise_xor(idx, mask)], sems.at[2 * s]).start()
        pltpu.make_async_copy(other.at[s], dst.at[jnp.bitwise_xor(idx, mask + 1)], sems.at[2 * s + 1]).start()


def wait_weights(own, other, dst, sems):
    idx = lax.axis_index("shard")
    for s, mask in enumerate(slot_masks(dst.shape[0])):
        pltpu.make_async_copy(own.at[s], dst.at[jnp.bitwise_xor(idx, mask)], sems.at[2 * s]).wait()
        pltpu.make_async_copy(other.at[s], dst.at[jnp.bitwise_xor(idx, mask + 1)], sems.at[2 * s + 1]).wait()


def first_step(*fs):
    @pl.when(pl.program_id(0) == 0)
    def _():
        for f in fs:
            f()


def flat(v):
    return v.reshape(v.shape[0] * v.shape[1], v.shape[2])


def slabs(w, first, count):
    return jnp.concatenate([flat(w[:, k]) for k in range(first, first + count)], 1) if count > 1 else flat(w[:, first])


def tall(w, first, count):
    v = w[:, first : first + count]
    return v.reshape(v.shape[0] * v.shape[1] * v.shape[2], v.shape[3])


def store_slots(keep, send, pieces):
    half = keep.shape[0]
    idx = lax.axis_index("shard")
    for s, mask in enumerate(slot_masks(2 * half)):
        for dst, extra in ((keep, 0), (send, 1)):
            owner = jnp.bitwise_xor(idx, mask + extra)
            for k, piece in enumerate(pieces):
                dst[s, k] = piece(owner).astype(dst.dtype)


def rows_of(ref, part, col, width):
    return lambda owner: ref[pl.ds(pl.multiple_of(owner * part, 8), part), col * width : (col + 1) * width]


def tall_rows_of(ref, part, q, count):
    return lambda owner: ref[pl.ds(pl.multiple_of((owner * count + q) * part, 8), part), :]


def normalise(x):
    mean = jnp.mean(x, -1, keepdims=True)
    cen = x - mean
    rstd = lax.rsqrt(jnp.mean(cen * cen, -1, keepdims=True) + EPS)
    return cen * rstd, rstd


def norm_back(dxhat, xhat, rstd):
    return rstd * (
        dxhat
        - jnp.mean(dxhat, -1, keepdims=True)
        - xhat * jnp.mean(dxhat * xhat, -1, keepdims=True)
    )


def gelu_both(h):
    phi = 0.5 + 0.5 * lax.erf(h * 0.7071067811865476)
    return h * phi, phi + h * (jnp.exp(h * h * -0.5) * 0.3989422804014327)


def to_rows(cols):
    return cols.T[0:8]


def to_column(rows8, r):
    full = jnp.concatenate([rows8, jnp.zeros((120, rows8.shape[1]), F32)], 0)
    return full.T[:, r : r + 1]


def load_padded(dst, src, seq, rows, images):
    for g in range(images):
        dst[g * rows : g * rows + seq] = src[g].astype(F32)
        dst[g * rows + seq : (g + 1) * rows] = jnp.zeros((rows - seq, dst.shape[1]), F32)


def pack_kernel(*refs):
    smalls, (bias_up, w_qkv, w_proj, w_up, w_down) = refs[:8], refs[8:13]
    out_a0, out_l1, sq = refs[13:]
    part, width = out_a0.shape[1:]
    sq[...] = jnp.zeros_like(sq)
    for p, ref in enumerate(smalls):
        sq[2 * p : 2 * p + 2, 0:part] = ref[...].astype(F32)
    hid = bias_up.shape[1]
    out_a0[3] = jnp.zeros((part, width), BF)
    out_a0[3, :, 0:128] = sq[...].T[0:part].astype(BF)
    out_a0[3, 0:2, width - hid :] = bias_up[...]
    quart = w_up.shape[2] // width
    for layer in range(2):
        attn = out_a0 if layer == 0 else out_l1
        rest, base = (out_a0, 4) if layer == 0 else (out_l1, 3)
        for k in range(3):
            attn[k] = w_qkv[layer, :, k * width : (k + 1) * width]
        rest[base] = w_proj[layer]
        for q in range(quart):
            rest[base + 1 + q] = w_up[layer, :, q * width : (q + 1) * width]
            rest[base + 1 + quart + q] = w_down[layer, q * part : (q + 1) * part]


def unpack_small(w, vec, tmp):
    shards, _, part, width = w.shape
    hid = tmp.shape[1] // shards
    rows = flat(w[:, 3, :, 0:128]).astype(F32).T
    for j in range(shards):
        tmp[:, j * hid : (j + 1) * hid] = w[j, 3, 0:2, width - hid :].astype(F32)
    quart = tmp.shape[1] // width
    for layer in range(2):
        for p in range(8):
            vec[layer, p : p + 1] = rows[2 * p + layer : 2 * p + layer + 1]
        for q in range(quart):
            vec[layer, 8 + q : 9 + q] = tmp[layer : layer + 1, q * width : (q + 1) * width]
        vec[layer, 8 + quart :] = jnp.zeros((8 - quart, width), F32)


def attn_forward(seq, xs, vec, w, m_ref, o_ref, aux_ref, xh_ref):
    images, rows, width = o_ref.shape
    xhat, rstd = normalise(xs[...])
    xh_ref[...] = xhat.astype(BF).reshape(images, rows, width)
    n1 = (xhat * vec[0:1, :] + vec[1:2, :]).astype(BF)
    for c in range(3):
        cs = slice(c * width, (c + 1) * width)
        mc = dot(n1, slabs(w, c, 1))
        if c != 1:
            mc = mc + (vec[2:3, :] if c == 0 else vec[3:4, :])
        m_ref[:, :, cs] = mc.astype(BF).reshape(images, rows, width)
    lane = lax.broadcasted_iota(jnp.int32, (rows, 128), 1)
    row = lax.broadcasted_iota(jnp.int32, (rows, 128), 0)
    low = lane < 64
    kpad = jnp.where(row >= seq, NEG, 0.0).astype(BF)
    ones = jnp.where(row >= seq, 0.0, 1.0).astype(BF)
    first = lax.broadcasted_iota(jnp.int32, (1, 128), 1)
    mine = [jnp.where(first < 64, 1.0, 0.0).astype(BF), jnp.where(first < 64, 0.0, 1.0).astype(BF)]
    mark = [jnp.where(first == 64, 1.0, 0.0).astype(BF), jnp.where(first == 0, 1.0, 0.0).astype(BF)]
    kpads = [kpad * mark[0], kpad * mark[1]]
    for g in range(images):
        aux = jnp.broadcast_to(rstd[g * rows : (g + 1) * rows], (rows, 128))
        for p in range(width // 128):
            q2 = m_ref[g, :, p * 128 : (p + 1) * 128] * jnp.asarray(0.125, BF)
            k2 = m_ref[g, :, width + p * 128 : width + (p + 1) * 128]
            v2 = m_ref[g, :, 2 * width + p * 128 : 2 * width + (p + 1) * 128]
            vext = jnp.concatenate([v2 * ones, ones], 1)
            parts = []
            for half in range(2):
                s = dot_nt(q2 * mine[half] + mark[half], k2 * mine[half] + kpads[half])
                mx = jnp.max(s, -1, keepdims=True)
                pr = jnp.exp(s - mx).astype(BF)
                oe = dot(pr, vext)
                tot = oe[:, 128:]
                parts.append(oe[:, :128] / tot)
                aux = jnp.where(lane == 2 * p + half, mx + jnp.log(tot), aux)
            o_ref[g, :, p * 128 : (p + 1) * 128] = jnp.where(low, parts[0], parts[1]).astype(BF)
        aux_ref[g] = to_rows(aux)


def mlp_forward(seq, xs, o_ref, vec, w, base, out_ref, a_ref, d_ref, xh_ref, rs_ref):
    images, rows, width = o_ref.shape
    x1 = xs[...] + dot(flat(o_ref[...]), slabs(w, base, 1)) + vec[4:5, :]
    xhat, rstd = normalise(x1)
    xh_ref[...] = xhat.astype(BF).reshape(images, rows, width)
    for g in range(images):
        rs_ref[g] = to_rows(jnp.broadcast_to(rstd[g * rows : (g + 1) * rows], (rows, 128)))
    n2 = (xhat * vec[5:6, :] + vec[6:7, :]).astype(BF)
    acc = x1 + vec[7:8, :]
    quart = a_ref.shape[2] // width
    w2 = tall(w, base + 1 + quart, quart)
    for c in range(quart // 2):
        cs = slice(2 * c * width, 2 * (c + 1) * width)
        bias = jnp.concatenate([vec[8 + 2 * c : 9 + 2 * c, :], vec[9 + 2 * c : 10 + 2 * c, :]], 1)
        h = dot(n2, slabs(w, base + 1 + 2 * c, 2)) + bias
        a, d = gelu_both(h)
        a = a.astype(BF)
        a_ref[:, :, cs] = a.reshape(images, rows, 2 * width)
        d_ref[:, :, cs] = d.astype(BF).reshape(images, rows, 2 * width)
        acc = acc + dot(a, w2[cs, :])
    acc = acc.reshape(images, rows, width)
    for g in range(images):
        out_ref[g] = acc[g, :seq]


def zero(*refs):
    for r in refs:
        r[...] = jnp.zeros_like(r)


def mlp_backward(gs, a_ref, d_ref, xh_ref, rs_ref, o_ref, vec, w, base, dx1_ref, do_ref, dwp, dw1, dw2, vec_o, db1_o):
    images, rows, width = xh_ref.shape
    n = images * rows
    dz = gs[...].astype(BF)
    xhat = flat(xh_ref[...]).astype(F32)
    n2 = (xhat * vec[5:6, :] + vec[6:7, :]).astype(BF)
    dn2 = jnp.zeros((n, width), F32)
    quart = a_ref.shape[2] // width
    w2 = tall(w, base + 1 + quart, quart)
    for c in range(quart // 2):
        cs = slice(2 * c * width, 2 * (c + 1) * width)
        a = flat(a_ref[:, :, cs])
        d = flat(d_ref[:, :, cs])
        da = dot_nt(dz, w2[cs, :])
        dh = (d.astype(F32) * da).astype(BF)
        db1_o[:, cs] += colsum(dh.astype(F32))
        dw2[cs, :] += dot_tn(a, dz)
        dw1[:, cs] += dot_tn(n2, dh)
        dn2 = dn2 + dot_nt(dh, slabs(w, base + 1 + 2 * c, 2))
    rstd = jnp.concatenate([to_column(rs_ref[g], 0) for g in range(images)], 0)
    dx1 = gs[...] + norm_back(dn2 * vec[5:6, :], xhat, rstd)
    dx1_ref[...] = dx1.reshape(images, rows, width).astype(dx1_ref.dtype)
    dy = dx1.astype(BF)
    dwp[...] += dot_tn(flat(o_ref[...]), dy)
    do_ref[...] = dot_nt(dy, slabs(w, base, 1)).astype(BF).reshape(images, rows, width)
    vec_o[0:1, :] += colsum(dz.astype(F32))
    vec_o[1:2, :] += colsum(dn2 * xhat)
    vec_o[2:3, :] += colsum(dn2)
    vec_o[3:4, :] += colsum(dy.astype(F32))


def attn_backward(seq, m_ref, do_ref, aux_ref, dm_ref):
    images, rows, width = do_ref.shape
    lane = lax.broadcasted_iota(jnp.int32, (rows, 128), 1)
    low = lane < 64
    last = rows - 16
    valid = lax.broadcasted_iota(jnp.int32, (16, rows), 0) < seq - last
    first = lax.broadcasted_iota(jnp.int32, (1, 128), 1)
    mine = [jnp.where(first < 64, 1.0, 0.0).astype(BF), jnp.where(first < 64, 0.0, 1.0).astype(BF)]
    def scores(g, p):
        q2 = m_ref[g, :, p * 128 : (p + 1) * 128] * jnp.asarray(0.125, BF)
        k2 = m_ref[g, :, width + p * 128 : width + (p + 1) * 128]
        v2 = m_ref[g, :, 2 * width + p * 128 : 2 * width + (p + 1) * 128]
        do2 = do_ref[g, :, p * 128 : (p + 1) * 128]
        st = [dot_nt(k2 * mine[half], q2) for half in range(2)]
        dp = [dot_nt(v2 * mine[half], do2) for half in range(2)]
        return q2, k2, do2, st, dp

    def weigh(g, p, got):
        q2, k2, do2, st, dp = got
        pts, dsts = [], []
        for half in range(2):
            h = 2 * p + half
            sh = st[half] - aux_ref[g, h : h + 1, :]
            pt = jnp.exp(jnp.concatenate([sh[:last], jnp.where(valid, sh[last:], NEG)], 0))
            pd = pt * dp[half]
            dsts.append((pd - pt * colsum(pd)).astype(BF))
            pts.append(pt.astype(BF))
        return q2, k2, do2, pts, dsts

    def finish(g, p, got):
        q2, k2, do2, pts, dsts = got
        kt = (k2 * jnp.asarray(0.125, BF)).T
        dvs = [dot(pts[half], do2) for half in range(2)]
        dks = [dot(dsts[half], q2) for half in range(2)]
        dqs = [dot(kt[half * 64 : half * 64 + 64], dsts[half]) for half in range(2)]
        dm_ref[g, :, p * 128 : (p + 1) * 128] = jnp.concatenate(dqs, 0).T.astype(BF)
        dm_ref[g, :, width + p * 128 : width + (p + 1) * 128] = jnp.where(low, dks[0], dks[1]).astype(BF)
        dm_ref[g, :, 2 * width + p * 128 : 2 * width + (p + 1) * 128] = jnp.where(low, dvs[0], dvs[1]).astype(BF)

    items = [(g, p) for g in range(images) for p in range(width // 128)]
    ahead = scores(*items[0])
    for t, item in enumerate(items):
        got = weigh(*item, ahead)
        if t + 1 < len(items):
            ahead = scores(*items[t + 1])
        finish(*item, got)


def qkv_backward(seq, dx1_ref, dm_ref, xh_ref, aux_ref, vec, w, dx_ref, dwqkv, vec_s, dbm_s):
    images, rows, width = xh_ref.shape
    dm = flat(dm_ref[...])
    dbm_s[...] += colsum(dm.astype(F32))
    xhat = flat(xh_ref[...]).astype(F32)
    n1 = (xhat * vec[0:1, :] + vec[1:2, :]).astype(BF)
    dwqkv[...] += dot_tn(n1, dm)
    dn1 = dot_nt(dm, slabs(w, 0, 3))
    vec_s[0:1, :] += colsum(dn1 * xhat)
    vec_s[1:2, :] += colsum(dn1)
    rstd = jnp.concatenate([to_column(aux_ref[g], 7) for g in range(images)], 0)
    dx = flat(dx1_ref[...]).astype(F32) + norm_back(dn1 * vec[0:1, :], xhat, rstd)
    dx = dx.reshape(images, rows, width)
    for g in range(images):
        dx_ref[g] = dx[g, :seq].astype(dx_ref.dtype)


def small_slab(sm, vec_s, dbm_s, vec2, db1, part):
    width = sm.shape[0]
    small = jnp.concatenate(
        [vec_s[0:2, :], dbm_s[:, :width], dbm_s[:, 2 * width :], vec2[3:4, :], vec2[1:3, :], vec2[0:1, :],
         jnp.zeros((120, width), F32)], 0)
    sm[...] = jnp.zeros_like(sm)
    sm[:, 0:128] = small.T
    shards = width // part
    hid = db1.shape[1] // shards
    for j in range(shards):
        sm[j * part : j * part + 1, width - hid :] = db1[:, j * hid : (j + 1) * hid]


def attn_pieces(dwqkv, sm, part):
    width = sm.shape[0]
    return [rows_of(dwqkv, part, c, width) for c in range(3)] + [rows_of(sm, part, 0, width)]


def mlp_pieces(dwp, dw1, dw2, part):
    width = dwp.shape[0]
    quart = dw1.shape[1] // width
    return ([rows_of(dwp, part, 0, width)] + [rows_of(dw1, part, q, width) for q in range(quart)]
            + [tall_rows_of(dw2, part, q, quart) for q in range(quart)])


def last_step(f):
    pl.when(pl.program_id(0) == pl.num_programs(0) - 1)(f)


def fa_kernel(seq, x_ref, own, other, m_ref, o_ref, aux_ref, xh_ref, vec_ref, xs, w, sems, tmp):
    first_step(lambda: start_weights(own, other, w, sems))
    images, rows, _ = o_ref.shape
    load_padded(xs, x_ref, seq, rows, images)
    first_step(lambda: wait_weights(own, other, w, sems), lambda: unpack_small(w, vec_ref, tmp))
    attn_forward(seq, xs, vec_ref.at[0], w, m_ref, o_ref, aux_ref, xh_ref)


def fm_kernel(seq, x_ref, o_ref, vec_ref, own, other, out_ref, a_ref, d_ref, xh_ref, rs_ref, xs, w, sems):
    first_step(lambda: start_weights(own, other, w, sems))
    images, rows, _ = o_ref.shape
    load_padded(xs, x_ref, seq, rows, images)
    first_step(lambda: wait_weights(own, other, w, sems))
    mlp_forward(seq, xs, o_ref, vec_ref.at[0], w, 0, out_ref, a_ref, d_ref, xh_ref, rs_ref)


def bm_kernel(seq, gr_ref, a_ref, d_ref, xh_ref, rs_ref, o_ref, vec_ref, own, other,
              dx1_ref, do_ref, keep, send, vec_o, db1_o, gs, dwp, dw1, dw2, w, sems):
    images, rows, width = xh_ref.shape
    first_step(lambda: start_weights(own, other, w, sems), lambda: zero(dwp, dw1, dw2, vec_o, db1_o))
    load_padded(gs, gr_ref, seq, rows, images)
    first_step(lambda: wait_weights(own, other, w, sems))
    mlp_backward(gs, a_ref, d_ref, xh_ref, rs_ref, o_ref, vec_ref.at[0], w, 0, dx1_ref, do_ref, dwp, dw1, dw2, vec_o, db1_o)

    @last_step
    def _():
        store_slots(keep, send, mlp_pieces(dwp, dw1, dw2, w.shape[2]))


def ba_kernel(seq, m_ref, do_ref, xh_ref, aux_ref, vec_ref, vec2, db1, own, other,
              dm_ref, keep, send, dwqkv, dbm_s, w, sems, sm):
    first_step(lambda: start_weights(own, other, w, sems), lambda: zero(dwqkv, dbm_s))
    attn_backward(seq, m_ref, do_ref, aux_ref, dm_ref)
    dm = flat(dm_ref[...])
    dbm_s[...] += colsum(dm.astype(F32))
    dwqkv[...] += dot_tn(flat(xh_ref[...]), dm)
    first_step(lambda: wait_weights(own, other, w, sems))

    @last_step
    def _():
        part = w.shape[2]
        width = sm.shape[0]
        prod = dwqkv[...]
        full = slabs(w, 0, 3).astype(F32)
        gain = jnp.sum(full * prod, 1, keepdims=True)
        shift = jnp.sum(full * dbm_s[...], 1, keepdims=True)
        params = vec_ref[0, 0:8, :]
        dwqkv[...] = to_column(params, 0) * prod + to_column(params, 1) * dbm_s[...]
        small_slab(sm, jnp.zeros((8, width), F32), dbm_s, vec2, db1, part)
        sm[:, 0:1] = gain
        sm[:, 1:2] = shift
        store_slots(keep, send, attn_pieces(dwqkv, sm, part))


def bx_kernel(seq, dx1_ref, dm_ref, xh_ref, aux_ref, vec_ref, own, other, *rest):
    dx_ref, w, sems = rest[-3:]
    vec = vec_ref.at[0]
    images, rows, width = xh_ref.shape
    first_step(lambda: start_weights(own, other, w, sems), lambda: wait_weights(own, other, w, sems))
    dn1 = dot_nt(flat(dm_ref[...]), slabs(w, 0, 3))
    rstd = jnp.concatenate([to_column(aux_ref[g], 7) for g in range(images)], 0)
    dx = flat(dx1_ref[...]).astype(F32) + norm_back(dn1 * vec[0:1, :], flat(xh_ref[...]).astype(F32), rstd)
    dx = dx.reshape(images, rows, width)
    for g in range(images):
        dx_ref[g] = dx[g, :seq]


def top_kernel(seq, x_ref, cot_ref, vec_ref, own, other, out_ref, dx_ref, keep, send,
               xs, gs, m_s, o_s, aux_s, xa_s, xm_s, rs_s, a_s, d_s, dx1_s, do_s, dm_s,
               dwqkv, dwp, dw1, dw2, vec_a, vec_m, dbm_s, db1_s, sm, w, sems):
    images, rows, width = o_s.shape
    vec = vec_ref.at[1]
    first_step(lambda: start_weights(own, other, w, sems),
               lambda: zero(dwqkv, dwp, dw1, dw2, vec_a, vec_m, dbm_s, db1_s))
    load_padded(xs, x_ref, seq, rows, images)
    load_padded(gs, cot_ref, seq, rows, images)
    first_step(lambda: wait_weights(own, other, w, sems))
    attn_forward(seq, xs, vec, w, m_s, o_s, aux_s, xa_s)
    mlp_forward(seq, xs, o_s, vec, w, 3, out_ref, a_s, d_s, xm_s, rs_s)
    mlp_backward(gs, a_s, d_s, xm_s, rs_s, o_s, vec, w, 3, dx1_s, do_s, dwp, dw1, dw2, vec_m, db1_s)
    attn_backward(seq, m_s, do_s, aux_s, dm_s)
    qkv_backward(seq, dx1_s, dm_s, xa_s, aux_s, vec, w, dx_ref, dwqkv, vec_a, dbm_s)

    @last_step
    def _():
        part = w.shape[2]
        small_slab(sm, vec_a, dbm_s, vec_m, db1_s, part)
        store_slots(keep, send, attn_pieces(dwqkv, sm, part) + mlp_pieces(dwp, dw1, dw2, part))


def finish_kernel(*refs):
    ins, outs = refs[:6], refs[6:]
    o_qkv, o_proj, o_up, o_down, o_bup = outs[:5]
    smalls = outs[5:]
    part, width = ins[0].shape[1:]
    hid = o_bup.shape[1]
    quart = o_up.shape[2] // width
    for layer in range(2):
        a1, a2 = ins[4:6] if layer == 1 else ins[0:2]
        m1, m2, base = (*ins[4:6], 4) if layer == 1 else (*ins[2:4], 0)
        for k in range(3):
            o_qkv[layer, :, k * width : (k + 1) * width] = a1[k].astype(F32) + a2[k].astype(F32)
        small = a1[3].astype(F32) + a2[3].astype(F32)
        o_bup[layer : layer + 1, :] = small[0:1, width - hid :]
        pad = jnp.concatenate([small[:, 0:128], jnp.zeros((128 - part, 128), F32)], 0).T
        for p, ref in enumerate(smalls):
            ref[layer : layer + 1, :] = pad[p : p + 1, 0:part]

        def both(k):
            return m1[base + k].astype(F32) + m2[base + k].astype(F32)

        o_proj[layer] = both(0)
        for q in range(quart):
            o_up[layer, :, q * width : (q + 1) * width] = both(1 + q)
            o_down[layer, q * part : (q + 1) * part] = both(1 + quart + q)


def blk(shape):
    nd = len(shape)
    return pl.BlockSpec(shape, lambda i: (i,) + (0,) * (nd - 1))


def whole(arr):
    nd = len(arr.shape)
    return pl.BlockSpec(arr.shape, lambda i: (0,) * nd)


def anyspec():
    return pl.BlockSpec(memory_space=pl.ANY)


def sds(shape, dt):
    return jax.ShapeDtypeStruct(shape, dt)


COST = {"fa": 13, "fm": 18, "bm": 26, "ba": 20, "top": 70}


def call(kern, name, per, blocked_in, whole_in, any_in, blocked_out, whole_out, scratch):
    in_specs = [blk((per,) + a.shape[1:]) for a in blocked_in] + [whole(a) for a in whole_in] + [anyspec() for _ in any_in]
    out_specs = [blk((per,) + a.shape[1:]) for a in blocked_out] + [whole(a) for a in whole_out]
    return pl.pallas_call(
        kern,
        grid=(blocked_in[0].shape[0] // per,),
        in_specs=in_specs,
        out_specs=out_specs,
        out_shape=list(blocked_out) + list(whole_out),
        scratch_shapes=scratch,
        compiler_params=pltpu.CompilerParams(vmem_limit_bytes=VMEM_LIMIT),
        name=name,
        cost_estimate=pl.CostEstimate(flops=COST[name] * 1_150_000_000, bytes_accessed=0, transcendentals=0),
    )(*blocked_in, *whole_in, *any_in)


def wscratch(own):
    return [pltpu.VMEM((2 * own.shape[0],) + own.shape[1:], BF), pltpu.SemaphoreType.DMA((2 * own.shape[0],))]


def run_pack(smalls, bias_up, w_qkv, w_proj, w_up, w_down):
    part, width = w_proj.shape[1:]
    quart = w_up.shape[2] // width
    return pl.pallas_call(
        pack_kernel,
        out_shape=[sds((5 + 2 * quart, part, width), BF), sds((4 + 2 * quart, part, width), BF)],
        scratch_shapes=[pltpu.VMEM((128, 128), F32)],
        name="pack",
    )(*smalls, bias_up, w_qkv, w_proj, w_up, w_down)


def run_fa(x, wa, ff, per):
    images, seq, width = x.shape
    rows = pad_rows(seq)
    return call(
        functools.partial(fa_kernel, seq), "fa", per, [x], [], wa,
        [sds((images, rows, 3 * width), BF), sds((images, rows, width), BF), sds((images, 8, rows), F32),
         sds((images, rows, width), BF)], [sds((2, 16, width), F32)],
        [pltpu.VMEM((per * rows, width), F32)] + wscratch(wa[0]) + [pltpu.VMEM((2, ff), F32)])


def run_top(x, cot, vec, wt, per):
    images, seq, width = x.shape
    rows = pad_rows(seq)
    ff = (wt[0].shape[1] - 4) // 2 * width
    n = per * rows
    cells = lambda c: pltpu.VMEM((per, rows, c), BF)
    tall8 = pltpu.VMEM((per, 8, rows), F32)
    full = lambda r, c: pltpu.VMEM((r, c), F32)
    return call(
        functools.partial(top_kernel, seq), "top", per, [x, cot], [vec], wt,
        [sds((images, seq, width), F32), sds((images, seq, width), BF)], slots(wt[0], wt[0].shape[1] + 1),
        [full(n, width), full(n, width), cells(3 * width), cells(width), tall8, cells(width), cells(width), tall8,
         cells(ff), cells(ff), pltpu.VMEM((per, rows, width), F32), cells(width), cells(3 * width),
         full(width, 3 * width), full(width, width), full(width, ff), full(ff, width), full(8, width), full(8, width),
         full(1, 3 * width), full(1, ff), full(width, width)] + wscratch(wt[0]))


def run_fm(x, o, vec, wm, per):
    images, seq, width = x.shape
    rows = o.shape[1]
    ff = (wm[0].shape[1] - 1) // 2 * width
    return call(
        functools.partial(fm_kernel, seq), "fm", per, [x, o], [vec], wm,
        [sds((images, seq, width), F32), sds((images, rows, ff), BF), sds((images, rows, ff), BF),
         sds((images, rows, width), BF), sds((images, 8, rows), F32)], [],
        [pltpu.VMEM((per * rows, width), F32)] + wscratch(wm[0]))


def slots(own, count):
    half, _, part, width = own.shape
    return [sds((half, count, part, width), BF)] * 2


def run_bm(gr, a, d, xh, rs, o, vec, wm, per):
    images, seq, width = gr.shape
    rows, ff = a.shape[1:]
    return call(
        functools.partial(bm_kernel, seq), "bm", per, [gr, a, d, xh, rs, o], [vec], wm,
        [sds((images, rows, width), BF), sds((images, rows, width), BF)],
        slots(wm[0], wm[0].shape[1]) + [sds((8, width), F32), sds((1, ff), F32)],
        [pltpu.VMEM((per * rows, width), F32), pltpu.VMEM((width, width), F32), pltpu.VMEM((width, ff), F32),
         pltpu.VMEM((ff, width), F32)] + wscratch(wm[0]))


def run_ba(seq, m, do, xh, aux, vec, vec2, db1, wa, per):
    images, rows, width = do.shape
    return call(
        functools.partial(ba_kernel, seq), "ba", per, [m, do, xh, aux], [vec, vec2, db1], wa,
        [sds((images, rows, 3 * width), BF)], slots(wa[0], 4),
        [pltpu.VMEM((width, 3 * width), F32), pltpu.VMEM((1, 3 * width), F32)]
        + wscratch(wa[0]) + [pltpu.VMEM((width, width), F32)])


def run_bx(seq, dx1, dm, xh, aux, vec, wa, per, first, count, prev=None):
    images, rows, width = dx1.shape
    base = first // per

    def at(shape):
        nd = len(shape)
        return pl.BlockSpec((per,) + shape[1:], lambda i: (i + base,) + (0,) * (nd - 1))

    more = [] if prev is None else [prev]
    out = sds((images, seq, width), F32)
    return pl.pallas_call(
        functools.partial(bx_kernel, seq),
        grid=(count // per,),
        in_specs=[at(a.shape) for a in (dx1, dm, xh, aux)] + [whole(vec)] + [anyspec() for _ in [*wa, *more]],
        out_specs=at(out.shape),
        out_shape=out,
        input_output_aliases={7: 0} if more else {},
        scratch_shapes=wscratch(wa[0]),
        compiler_params=pltpu.CompilerParams(vmem_limit_bytes=VMEM_LIMIT),
        name="bx",
        cost_estimate=pl.CostEstimate(flops=count * 1_150_000_000, bytes_accessed=0, transcendentals=0),
    )(dx1, dm, xh, aux, vec, *wa, *more)


def run_finish(a0, m0, l1, ff):
    part, width = a0[0].shape[1:]
    return pl.pallas_call(
        finish_kernel,
        out_shape=[sds((2, part, 3 * width), F32), sds((2, part, width), F32), sds((2, part, ff), F32),
                   sds((2, ff // width * part, width), F32), sds((2, ff // width * part), F32)]
        + [sds((2, part), F32)] * 8,
        name="finish",
    )(*a0, *m0, *l1)


def xor_pairs(count, b):
    return [(i, i ^ b) for i in range(count)]


def tie(value, *others):
    return lax.optimization_barrier((value, *others))[0]


def group(*values):
    return lax.optimization_barrier(values)


def body(n, reps, tokens, norm1_gain, norm1_shift, qkv_weight, query_bias, value_bias, proj_weight, proj_bias,
         norm2_gain, norm2_shift, fc1_weight, fc1_bias, fc2_weight, fc2_bias, cotangent):
    images, seq, width = tokens.shape
    ff = fc1_weight.shape[2]
    per = 2 if images % 2 == 0 else 1
    upper = []
    b = n // 2
    while b > 2:
        upper.append(b)
        b //= 2

    def swap(x, b):
        return lax.ppermute(x, "shard", xor_pairs(n, b))

    def direct(x):
        masks = [0]
        for b in upper:
            masks = masks + [m ^ b for m in masks]
        return [x] + [swap(x, m) for m in masks[1:]]

    smalls = [norm1_gain, norm1_shift, query_bias, value_bias, proj_bias, norm2_gain, norm2_shift, fc2_bias]
    am, l1 = run_pack(smalls, fc1_bias, qkv_weight, proj_weight, fc1_weight, fc2_weight)

    am = direct(am)
    a0 = jnp.stack([y[:4] for y in am])
    m0 = jnp.stack([y[4:] for y in am])
    a0x = swap(a0, 2)
    l1 = direct(tie(l1, a0))
    a0 = jnp.concatenate([a0, a0x])
    m0x = swap(tie(m0, a0x), 2)
    a0 = (a0, swap(a0, 1))
    mix, o, aux, xa, vec = run_fa(tie(tokens, m0, l1[0]), a0, ff, per)
    o, m0x, *l1 = group(o, m0x, *l1)
    m0 = jnp.concatenate([m0, m0x])
    l1 = jnp.stack(l1)
    m0 = (m0, swap(tie(m0, l1), 1))
    l1x = swap(l1, 2)
    layer_one, act, der, xm, rs = run_fm(tokens, o, vec, m0, per)
    layer_one, l1x = group(layer_one, l1x)
    l1 = jnp.concatenate([l1, l1x])
    l1 = (l1, swap(l1, 1))
    layer_two, grad, kp, sn = run_top(layer_one, cotangent, vec, l1, per)

    class Sum:
        def __init__(self, keep, send):
            self.keep, self.got, self.send = keep, [], send
            self.bits = [1, 2] + upper[::-1]

        def start(self):
            self.flight = swap(self.send, self.bits[len(self.got)])
            return self

        def done(self):
            self.got.append(self.flight)
            size = self.flight.shape[0]
            if len(self.got) < len(self.bits):
                self.send = self.total(size // 2, size).astype(BF)
            else:
                self.send = self.total(0, 1)[0].astype(BF)
            return self

        def scatter(self):
            self.rest = self.total(0, 1)[0]
            masks = [0]
            for b in upper:
                masks = masks + [m ^ b for m in masks]
            sends = [self.total(z, z + 1)[0].astype(BF) for z in range(1, len(masks))]
            self.send = sends
            self.flight = [swap(s, m) for s, m in zip(sends, masks[1:])]
            return self

        def collect(self):
            total = self.rest
            for f in self.flight:
                total = total + f.astype(F32)
            self.send = total.astype(BF)
            return self

        def total(self, lo, hi):
            t = self.keep[lo:hi].astype(F32)
            for g in self.got:
                t = t + g[lo:hi].astype(F32)
            return t

        def replicas(self):
            mine, b = self.send, 1
            while True:
                other = lax.ppermute(mine, "replica", xor_pairs(reps, b))
                b *= 2
                if b >= reps:
                    return (mine, other)
                mine = (mine.astype(F32) + other.astype(F32)).astype(BF)

    def meet(value, *sums):
        value, *got = group(value, *[s.flight for s in sums])
        for s, g in zip(sums, got):
            s.flight = g
            s.done()
        return value

    def sent(value, *sums):
        return tie(value, *[s.send for s in sums])

    g1 = Sum(kp, sn).start().done().start()
    dx1, do, kp, sn, v2, db1 = run_bm(sent(grad, g1), act, der, xm, rs, o, vec, m0, per)
    do, sn, g1.flight = group(do, sn, g1.flight)
    gm0 = Sum(kp, sn).start()
    g1.got.append(g1.flight)
    g1.scatter()
    gm0.done().start()
    dm, kp, sn = run_ba(seq, mix, tie(do, *g1.send, gm0.send), xa, aux, vec, v2, db1, a0, per)
    sn, gm0.flight, *g1.flight = group(sn, gm0.flight, *g1.flight)
    ga0 = Sum(kp, sn).start()
    gm0.done().start()
    g1.collect()
    ga0.flight = tie(ga0.flight, gm0.send)
    ga0.done().start()
    first = images // (2 * per) * per
    part_grad = run_bx(seq, dx1, tie(dm, ga0.send, gm0.send), xa, aux, vec, a0, per, 0, first)
    part_grad, ga0.flight, gm0.flight, g1.send = group(part_grad, ga0.flight, gm0.flight, g1.send)
    ga0.done().start()
    gm0.done().start()
    fin_1 = g1.replicas()
    tokens_grad = run_bx(seq, dx1, dm, xa, aux, vec, a0, per, first, images - first, tie(part_grad, ga0.send, gm0.send))
    tokens_grad, ga0.flight, gm0.flight = group(tokens_grad, ga0.flight, gm0.flight)
    ga0.done().start()
    gm0.done()
    fin_m0 = gm0.replicas()
    ga0.done()
    fin_a0 = ga0.replicas()

    g_qkv, g_proj, g_up, g_down, g_bup, *s = run_finish(fin_a0, fin_m0, fin_1, ff)
    return (layer_one, layer_two, tokens_grad, s[0], s[1], g_qkv, s[2], s[3], g_proj, s[4], s[5], s[6],
            g_up, g_bup, g_down, s[7])
def solution(mesh):
    n = mesh.shape["shard"]
    reps = mesh.shape["replica"]
    batch = P(("replica", "shard"), None, None)
    row2 = P(None, "shard")
    row3 = P(None, "shard", None)
    in_specs = (batch, row2, row2, row3, row2, row2, row3, row2, row2, row2, row3, row2, row3, row2, batch)
    out_specs = (batch, batch, batch, row2, row2, row3, row2, row2, row3, row2, row2, row2, row3, row2, row3, row2)
    return jax.shard_map(
        functools.partial(body, n, reps), mesh=mesh, in_specs=in_specs, out_specs=out_specs, check_vma=False
    )
```

```python
import functools
import jax
import jax.numpy as jnp
from jax import lax
from jax.sharding import PartitionSpec as P
from jax.experimental import pallas as pl
from jax.experimental.pallas import tpu as pltpu

BF = jnp.bfloat16
F32 = jnp.float32
HEADS = 6
EPS = 1e-06
NEG = -1e30
VMEM_LIMIT = 54 * 2**20


def dot(a, b):
    return jnp.dot(a, b, preferred_element_type=F32)


def dot_nt(a, b):
    return lax.dot_general(a, b, (((1,), (1,)), ((), ())), preferred_element_type=F32)


def dot_tn(a, b):
    return lax.dot_general(a, b, (((0,), (0,)), ((), ())), preferred_element_type=F32)


def pad_rows(seq):
    return (seq + 15) // 16 * 16


def colsum(x):
    return jnp.sum(x, 0, keepdims=True)


def slot_masks(n):
    masks = [0]
    b = n // 2
    while b > 1:
        masks = masks + [m ^ b for m in masks]
        b //= 2
    return masks


def start_weights(own, other, dst, sems):
    idx = lax.axis_index("shard")
    for s, mask in enumerate(slot_masks(dst.shape[0])):
        pltpu.make_async_copy(own.at[s], dst.at[jnp.bitwise_xor(idx, mask)], sems.at[2 * s]).start()
        pltpu.make_async_copy(other.at[s], dst.at[jnp.bitwise_xor(idx, mask + 1)], sems.at[2 * s + 1]).start()


def wait_weights(own, other, dst, sems):
    idx = lax.axis_index("shard")
    for s, mask in enumerate(slot_masks(dst.shape[0])):
        pltpu.make_async_copy(own.at[s], dst.at[jnp.bitwise_xor(idx, mask)], sems.at[2 * s]).wait()
        pltpu.make_async_copy(other.at[s], dst.at[jnp.bitwise_xor(idx, mask + 1)], sems.at[2 * s + 1]).wait()


def first_step(*fs):
    @pl.when(pl.program_id(0) == 0)
    def _():
        for f in fs:
            f()


def flat(v):
    return v.reshape(v.shape[0] * v.shape[1], v.shape[2])


def slabs(w, first, count):
    return jnp.concatenate([flat(w[:, k]) for k in range(first, first + count)], 1) if count > 1 else flat(w[:, first])


def tall(w, first, count):
    v = w[:, first : first + count]
    return v.reshape(v.shape[0] * v.shape[1] * v.shape[2], v.shape[3])


def store_slots(keep, send, pieces):
    half = keep.shape[0]
    idx = lax.axis_index("shard")
    for s, mask in enumerate(slot_masks(2 * half)):
        for dst, extra in ((keep, 0), (send, 1)):
            owner = jnp.bitwise_xor(idx, mask + extra)
            for k, piece in enumerate(pieces):
                dst[s, k] = piece(owner).astype(dst.dtype)


def rows_of(ref, part, col, width):
    return lambda owner: ref[pl.ds(pl.multiple_of(owner * part, 8), part), col * width : (col + 1) * width]


def tall_rows_of(ref, part, q, count):
    return lambda owner: ref[pl.ds(pl.multiple_of((owner * count + q) * part, 8), part), :]


def normalise(x):
    mean = jnp.mean(x, -1, keepdims=True)
    cen = x - mean
    rstd = lax.rsqrt(jnp.mean(cen * cen, -1, keepdims=True) + EPS)
    return cen * rstd, rstd


def norm_back(dxhat, xhat, rstd):
    return rstd * (
        dxhat
        - jnp.mean(dxhat, -1, keepdims=True)
        - xhat * jnp.mean(dxhat * xhat, -1, keepdims=True)
    )


def gelu_both(h):
    phi = 0.5 + 0.5 * lax.erf(h * 0.7071067811865476)
    return h * phi, phi + h * (jnp.exp(h * h * -0.5) * 0.3989422804014327)


def to_rows(cols):
    return cols.T[0:8]


def to_column(rows8, r):
    full = jnp.concatenate([rows8, jnp.zeros((120, rows8.shape[1]), F32)], 0)
    return full.T[:, r : r + 1]


def load_padded(dst, src, seq, rows, images):
    for g in range(images):
        dst[g * rows : g * rows + seq] = src[g].astype(F32)
        dst[g * rows + seq : (g + 1) * rows] = jnp.zeros((rows - seq, dst.shape[1]), F32)


def pack_kernel(*refs):
    smalls, (bias_up, w_qkv, w_proj, w_up, w_down) = refs[:8], refs[8:13]
    out_a0, out_l1, sq = refs[13:]
    part, width = out_a0.shape[1:]
    sq[...] = jnp.zeros_like(sq)
    for p, ref in enumerate(smalls):
        sq[2 * p : 2 * p + 2, 0:part] = ref[...].astype(F32)
    hid = bias_up.shape[1]
    out_a0[3] = jnp.zeros((part, width), BF)
    out_a0[3, :, 0:128] = sq[...].T[0:part].astype(BF)
    out_a0[3, 0:2, width - hid :] = bias_up[...]
    quart = w_up.shape[2] // width
    for layer in range(2):
        attn = out_a0 if layer == 0 else out_l1
        rest, base = (out_a0, 4) if layer == 0 else (out_l1, 3)
        for k in range(3):
            attn[k] = w_qkv[layer, :, k * width : (k + 1) * width]
        rest[base] = w_proj[layer]
        for q in range(quart):
            rest[base + 1 + q] = w_up[layer, :, q * width : (q + 1) * width]
            rest[base + 1 + quart + q] = w_down[layer, q * part : (q + 1) * part]


def unpack_small(w, vec, tmp):
    shards, _, part, width = w.shape
    hid = tmp.shape[1] // shards
    rows = flat(w[:, 3, :, 0:128]).astype(F32).T
    for j in range(shards):
        tmp[:, j * hid : (j + 1) * hid] = w[j, 3, 0:2, width - hid :].astype(F32)
    quart = tmp.shape[1] // width
    for layer in range(2):
        for p in range(8):
            vec[layer, p : p + 1] = rows[2 * p + layer : 2 * p + layer + 1]
        for q in range(quart):
            vec[layer, 8 + q : 9 + q] = tmp[layer : layer + 1, q * width : (q + 1) * width]
        vec[layer, 8 + quart :] = jnp.zeros((8 - quart, width), F32)


def attn_forward(seq, xs, vec, w, m_ref, o_ref, aux_ref, xh_ref):
    images, rows, width = o_ref.shape
    xhat, rstd = normalise(xs[...])
    xh_ref[...] = xhat.astype(BF).reshape(images, rows, width)
    n1 = (xhat * vec[0:1, :] + vec[1:2, :]).astype(BF)
    for c in range(3):
        cs = slice(c * width, (c + 1) * width)
        mc = dot(n1, slabs(w, c, 1))
        if c != 1:
            mc = mc + (vec[2:3, :] if c == 0 else vec[3:4, :])
        m_ref[:, :, cs] = mc.astype(BF).reshape(images, rows, width)
    lane = lax.broadcasted_iota(jnp.int32, (rows, 128), 1)
    row = lax.broadcasted_iota(jnp.int32, (rows, 128), 0)
    low = lane < 64
    kpad = jnp.where(row >= seq, NEG, 0.0).astype(BF)
    ones = jnp.where(row >= seq, 0.0, 1.0).astype(BF)
    first = lax.broadcasted_iota(jnp.int32, (1, 128), 1)
    mine = [jnp.where(first < 64, 1.0, 0.0).astype(BF), jnp.where(first < 64, 0.0, 1.0).astype(BF)]
    mark = [jnp.where(first == 64, 1.0, 0.0).astype(BF), jnp.where(first == 0, 1.0, 0.0).astype(BF)]
    kpads = [kpad * mark[0], kpad * mark[1]]
    for g in range(images):
        aux = jnp.broadcast_to(rstd[g * rows : (g + 1) * rows], (rows, 128))
        for p in range(width // 128):
            q2 = m_ref[g, :, p * 128 : (p + 1) * 128] * jnp.asarray(0.125, BF)
            k2 = m_ref[g, :, width + p * 128 : width + (p + 1) * 128]
            v2 = m_ref[g, :, 2 * width + p * 128 : 2 * width + (p + 1) * 128]
            vext = jnp.concatenate([v2 * ones, ones], 1)
            parts = []
            for half in range(2):
                s = dot_nt(q2 * mine[half] + mark[half], k2 * mine[half] + kpads[half])
                mx = jnp.max(s, -1, keepdims=True)
                pr = jnp.exp(s - mx).astype(BF)
                oe = dot(pr, vext)
                tot = oe[:, 128:]
                parts.append(oe[:, :128] / tot)
                aux = jnp.where(lane == 2 * p + half, mx + jnp.log(tot), aux)
            o_ref[g, :, p * 128 : (p + 1) * 128] = jnp.where(low, parts[0], parts[1]).astype(BF)
        aux_ref[g] = to_rows(aux)


def mlp_forward(seq, xs, o_ref, vec, w, base, out_ref, a_ref, d_ref, xh_ref, rs_ref):
    images, rows, width = o_ref.shape
    x1 = xs[...] + dot(flat(o_ref[...]), slabs(w, base, 1)) + vec[4:5, :]
    xhat, rstd = normalise(x1)
    xh_ref[...] = xhat.astype(BF).reshape(images, rows, width)
    for g in range(images):
        rs_ref[g] = to_rows(jnp.broadcast_to(rstd[g * rows : (g + 1) * rows], (rows, 128)))
    n2 = (xhat * vec[5:6, :] + vec[6:7, :]).astype(BF)
    acc = x1 + vec[7:8, :]
    quart = a_ref.shape[2] // width
    w2 = tall(w, base + 1 + quart, quart)
    for c in range(quart // 2):
        cs = slice(2 * c * width, 2 * (c + 1) * width)
        bias = jnp.concatenate([vec[8 + 2 * c : 9 + 2 * c, :], vec[9 + 2 * c : 10 + 2 * c, :]], 1)
        h = dot(n2, slabs(w, base + 1 + 2 * c, 2)) + bias
        a, d = gelu_both(h)
        a = a.astype(BF)
        a_ref[:, :, cs] = a.reshape(images, rows, 2 * width)
        d_ref[:, :, cs] = d.astype(BF).reshape(images, rows, 2 * width)
        acc = acc + dot(a, w2[cs, :])
    acc = acc.reshape(images, rows, width)
    for g in range(images):
        out_ref[g] = acc[g, :seq]


def zero(*refs):
    for r in refs:
        r[...] = jnp.zeros_like(r)


def mlp_backward(gs, a_ref, d_ref, xh_ref, rs_ref, o_ref, vec, w, base, dx1_ref, do_ref, dwp, dw1, dw2, vec_o, db1_o):
    images, rows, width = xh_ref.shape
    n = images * rows
    dz = gs[...].astype(BF)
    xhat = flat(xh_ref[...]).astype(F32)
    n2 = (xhat * vec[5:6, :] + vec[6:7, :]).astype(BF)
    dn2 = jnp.zeros((n, width), F32)
    quart = a_ref.shape[2] // width
    w2 = tall(w, base + 1 + quart, quart)
    for c in range(quart // 2):
        cs = slice(2 * c * width, 2 * (c + 1) * width)
        a = flat(a_ref[:, :, cs])
        d = flat(d_ref[:, :, cs])
        da = dot_nt(dz, w2[cs, :])
        dh = (d.astype(F32) * da).astype(BF)
        db1_o[:, cs] += colsum(dh.astype(F32))
        dw2[cs, :] += dot_tn(a, dz)
        dw1[:, cs] += dot_tn(n2, dh)
        dn2 = dn2 + dot_nt(dh, slabs(w, base + 1 + 2 * c, 2))
    rstd = jnp.concatenate([to_column(rs_ref[g], 0) for g in range(images)], 0)
    dx1 = gs[...] + norm_back(dn2 * vec[5:6, :], xhat, rstd)
    dx1_ref[...] = dx1.reshape(images, rows, width).astype(dx1_ref.dtype)
    dy = dx1.astype(BF)
    dwp[...] += dot_tn(flat(o_ref[...]), dy)
    do_ref[...] = dot_nt(dy, slabs(w, base, 1)).astype(BF).reshape(images, rows, width)
    vec_o[0:1, :] += colsum(dz.astype(F32))
    vec_o[1:2, :] += colsum(dn2 * xhat)
    vec_o[2:3, :] += colsum(dn2)
    vec_o[3:4, :] += colsum(dy.astype(F32))


def attn_backward(seq, m_ref, do_ref, aux_ref, dm_ref):
    images, rows, width = do_ref.shape
    lane = lax.broadcasted_iota(jnp.int32, (rows, 128), 1)
    low = lane < 64
    last = rows - 16
    valid = lax.broadcasted_iota(jnp.int32, (16, rows), 0) < seq - last
    first = lax.broadcasted_iota(jnp.int32, (1, 128), 1)
    mine = [jnp.where(first < 64, 1.0, 0.0).astype(BF), jnp.where(first < 64, 0.0, 1.0).astype(BF)]
    def scores(g, p):
        q2 = m_ref[g, :, p * 128 : (p + 1) * 128] * jnp.asarray(0.125, BF)
        k2 = m_ref[g, :, width + p * 128 : width + (p + 1) * 128]
        v2 = m_ref[g, :, 2 * width + p * 128 : 2 * width + (p + 1) * 128]
        do2 = do_ref[g, :, p * 128 : (p + 1) * 128]
        st = [dot_nt(k2 * mine[half], q2) for half in range(2)]
        dp = [dot_nt(v2 * mine[half], do2) for half in range(2)]
        return q2, k2, do2, st, dp

    def weigh(g, p, got):
        q2, k2, do2, st, dp = got
        pts, dsts = [], []
        for half in range(2):
            h = 2 * p + half
            sh = st[half] - aux_ref[g, h : h + 1, :]
            pt = jnp.exp(jnp.concatenate([sh[:last], jnp.where(valid, sh[last:], NEG)], 0))
            pd = pt * dp[half]
            dsts.append((pd - pt * colsum(pd)).astype(BF))
            pts.append(pt.astype(BF))
        return q2, k2, do2, pts, dsts

    def finish(g, p, got):
        q2, k2, do2, pts, dsts = got
        kt = (k2 * jnp.asarray(0.125, BF)).T
        dvs = [dot(pts[half], do2) for half in range(2)]
        dks = [dot(dsts[half], q2) for half in range(2)]
        dqs = [dot(kt[half * 64 : half * 64 + 64], dsts[half]) for half in range(2)]
        dm_ref[g, :, p * 128 : (p + 1) * 128] = jnp.concatenate(dqs, 0).T.astype(BF)
        dm_ref[g, :, width + p * 128 : width + (p + 1) * 128] = jnp.where(low, dks[0], dks[1]).astype(BF)
        dm_ref[g, :, 2 * width + p * 128 : 2 * width + (p + 1) * 128] = jnp.where(low, dvs[0], dvs[1]).astype(BF)

    items = [(g, p) for g in range(images) for p in range(width // 128)]
    ahead = scores(*items[0])
    for t, item in enumerate(items):
        got = weigh(*item, ahead)
        if t + 1 < len(items):
            ahead = scores(*items[t + 1])
        finish(*item, got)


def qkv_backward(seq, dx1_ref, dm_ref, xh_ref, aux_ref, vec, w, dx_ref, dwqkv, vec_s, dbm_s):
    images, rows, width = xh_ref.shape
    dm = flat(dm_ref[...])
    dbm_s[...] += colsum(dm.astype(F32))
    xhat = flat(xh_ref[...]).astype(F32)
    n1 = (xhat * vec[0:1, :] + vec[1:2, :]).astype(BF)
    dwqkv[...] += dot_tn(n1, dm)
    dn1 = dot_nt(dm, slabs(w, 0, 3))
    vec_s[0:1, :] += colsum(dn1 * xhat)
    vec_s[1:2, :] += colsum(dn1)
    rstd = jnp.concatenate([to_column(aux_ref[g], 7) for g in range(images)], 0)
    dx = flat(dx1_ref[...]).astype(F32) + norm_back(dn1 * vec[0:1, :], xhat, rstd)
    dx = dx.reshape(images, rows, width)
    for g in range(images):
        dx_ref[g] = dx[g, :seq].astype(dx_ref.dtype)


def small_slab(sm, vec_s, dbm_s, vec2, db1, part):
    width = sm.shape[0]
    small = jnp.concatenate(
        [vec_s[0:2, :], dbm_s[:, :width], dbm_s[:, 2 * width :], vec2[3:4, :], vec2[1:3, :], vec2[0:1, :],
         jnp.zeros((120, width), F32)], 0)
    sm[...] = jnp.zeros_like(sm)
    sm[:, 0:128] = small.T
    shards = width // part
    hid = db1.shape[1] // shards
    for j in range(shards):
        sm[j * part : j * part + 1, width - hid :] = db1[:, j * hid : (j + 1) * hid]


def attn_pieces(dwqkv, sm, part):
    width = sm.shape[0]
    return [rows_of(dwqkv, part, c, width) for c in range(3)] + [rows_of(sm, part, 0, width)]


def mlp_pieces(dwp, dw1, dw2, part):
    width = dwp.shape[0]
    quart = dw1.shape[1] // width
    return ([rows_of(dwp, part, 0, width)] + [rows_of(dw1, part, q, width) for q in range(quart)]
            + [tall_rows_of(dw2, part, q, quart) for q in range(quart)])


def last_step(f):
    pl.when(pl.program_id(0) == pl.num_programs(0) - 1)(f)


def fa_kernel(seq, x_ref, own, other, m_ref, o_ref, aux_ref, xh_ref, vec_ref, xs, w, sems, tmp):
    first_step(lambda: start_weights(own, other, w, sems))
    images, rows, _ = o_ref.shape
    load_padded(xs, x_ref, seq, rows, images)
    first_step(lambda: wait_weights(own, other, w, sems), lambda: unpack_small(w, vec_ref, tmp))
    attn_forward(seq, xs, vec_ref.at[0], w, m_ref, o_ref, aux_ref, xh_ref)


def fm_kernel(seq, x_ref, o_ref, vec_ref, own, other, out_ref, a_ref, d_ref, xh_ref, rs_ref, xs, w, sems):
    first_step(lambda: start_weights(own, other, w, sems))
    images, rows, _ = o_ref.shape
    load_padded(xs, x_ref, seq, rows, images)
    first_step(lambda: wait_weights(own, other, w, sems))
    mlp_forward(seq, xs, o_ref, vec_ref.at[0], w, 0, out_ref, a_ref, d_ref, xh_ref, rs_ref)


def bm_kernel(seq, gr_ref, a_ref, d_ref, xh_ref, rs_ref, o_ref, vec_ref, own, other,
              dx1_ref, do_ref, keep, send, vec_o, db1_o, gs, dwp, dw1, dw2, w, sems):
    images, rows, width = xh_ref.shape
    first_step(lambda: start_weights(own, other, w, sems), lambda: zero(dwp, dw1, dw2, vec_o, db1_o))
    load_padded(gs, gr_ref, seq, rows, images)
    first_step(lambda: wait_weights(own, other, w, sems))
    mlp_backward(gs, a_ref, d_ref, xh_ref, rs_ref, o_ref, vec_ref.at[0], w, 0, dx1_ref, do_ref, dwp, dw1, dw2, vec_o, db1_o)

    @last_step
    def _():
        store_slots(keep, send, mlp_pieces(dwp, dw1, dw2, w.shape[2]))


def ba_kernel(seq, m_ref, do_ref, xh_ref, aux_ref, vec_ref, vec2, db1, own, other,
              dm_ref, keep, send, dwqkv, dbm_s, w, sems, sm):
    first_step(lambda: start_weights(own, other, w, sems), lambda: zero(dwqkv, dbm_s))
    attn_backward(seq, m_ref, do_ref, aux_ref, dm_ref)
    dm = flat(dm_ref[...])
    dbm_s[...] += colsum(dm.astype(F32))
    dwqkv[...] += dot_tn(flat(xh_ref[...]), dm)
    first_step(lambda: wait_weights(own, other, w, sems))

    @last_step
    def _():
        part = w.shape[2]
        width = sm.shape[0]
        prod = dwqkv[...]
        full = slabs(w, 0, 3).astype(F32)
        gain = jnp.sum(full * prod, 1, keepdims=True)
        shift = jnp.sum(full * dbm_s[...], 1, keepdims=True)
        params = vec_ref[0, 0:8, :]
        dwqkv[...] = to_column(params, 0) * prod + to_column(params, 1) * dbm_s[...]
        small_slab(sm, jnp.zeros((8, width), F32), dbm_s, vec2, db1, part)
        sm[:, 0:1] = gain
        sm[:, 1:2] = shift
        store_slots(keep, send, attn_pieces(dwqkv, sm, part))


def bx_kernel(seq, dx1_ref, dm_ref, xh_ref, aux_ref, vec_ref, own, other, *rest):
    dx_ref, w, sems = rest[-3:]
    vec = vec_ref.at[0]
    images, rows, width = xh_ref.shape
    first_step(lambda: start_weights(own, other, w, sems), lambda: wait_weights(own, other, w, sems))
    dn1 = dot_nt(flat(dm_ref[...]), slabs(w, 0, 3))
    rstd = jnp.concatenate([to_column(aux_ref[g], 7) for g in range(images)], 0)
    dx = flat(dx1_ref[...]).astype(F32) + norm_back(dn1 * vec[0:1, :], flat(xh_ref[...]).astype(F32), rstd)
    dx = dx.reshape(images, rows, width)
    for g in range(images):
        dx_ref[g] = dx[g, :seq]


def top_kernel(seq, x_ref, cot_ref, vec_ref, own, other, out_ref, dx_ref, keep, send,
               xs, gs, m_s, o_s, aux_s, xa_s, xm_s, rs_s, a_s, d_s, dx1_s, do_s, dm_s,
               dwqkv, dwp, dw1, dw2, vec_a, vec_m, dbm_s, db1_s, sm, w, sems):
    images, rows, width = o_s.shape
    vec = vec_ref.at[1]
    first_step(lambda: start_weights(own, other, w, sems),
               lambda: zero(dwqkv, dwp, dw1, dw2, vec_a, vec_m, dbm_s, db1_s))
    load_padded(xs, x_ref, seq, rows, images)
    load_padded(gs, cot_ref, seq, rows, images)
    first_step(lambda: wait_weights(own, other, w, sems))
    attn_forward(seq, xs, vec, w, m_s, o_s, aux_s, xa_s)
    mlp_forward(seq, xs, o_s, vec, w, 3, out_ref, a_s, d_s, xm_s, rs_s)
    mlp_backward(gs, a_s, d_s, xm_s, rs_s, o_s, vec, w, 3, dx1_s, do_s, dwp, dw1, dw2, vec_m, db1_s)
    attn_backward(seq, m_s, do_s, aux_s, dm_s)
    qkv_backward(seq, dx1_s, dm_s, xa_s, aux_s, vec, w, dx_ref, dwqkv, vec_a, dbm_s)

    @last_step
    def _():
        part = w.shape[2]
        small_slab(sm, vec_a, dbm_s, vec_m, db1_s, part)
        store_slots(keep, send, attn_pieces(dwqkv, sm, part) + mlp_pieces(dwp, dw1, dw2, part))


def finish_kernel(*refs):
    ins, outs = refs[:6], refs[6:]
    o_qkv, o_proj, o_up, o_down, o_bup = outs[:5]
    smalls = outs[5:]
    part, width = ins[0].shape[1:]
    hid = o_bup.shape[1]
    quart = o_up.shape[2] // width
    for layer in range(2):
        a1, a2 = ins[4:6] if layer == 1 else ins[0:2]
        m1, m2, base = (*ins[4:6], 4) if layer == 1 else (*ins[2:4], 0)
        for k in range(3):
            o_qkv[layer, :, k * width : (k + 1) * width] = a1[k].astype(F32) + a2[k].astype(F32)
        small = a1[3].astype(F32) + a2[3].astype(F32)
        o_bup[layer : layer + 1, :] = small[0:1, width - hid :]
        pad = jnp.concatenate([small[:, 0:128], jnp.zeros((128 - part, 128), F32)], 0).T
        for p, ref in enumerate(smalls):
            ref[layer : layer + 1, :] = pad[p : p + 1, 0:part]

        def both(k):
            return m1[base + k].astype(F32) + m2[base + k].astype(F32)

        o_proj[layer] = both(0)
        for q in range(quart):
            o_up[layer, :, q * width : (q + 1) * width] = both(1 + q)
            o_down[layer, q * part : (q + 1) * part] = both(1 + quart + q)


def blk(shape):
    nd = len(shape)
    return pl.BlockSpec(shape, lambda i: (i,) + (0,) * (nd - 1))


def whole(arr):
    nd = len(arr.shape)
    return pl.BlockSpec(arr.shape, lambda i: (0,) * nd)


def anyspec():
    return pl.BlockSpec(memory_space=pl.ANY)


def sds(shape, dt):
    return jax.ShapeDtypeStruct(shape, dt)


COST = {"fa": 13, "fm": 18, "bm": 26, "ba": 20, "top": 70}


def call(kern, name, per, blocked_in, whole_in, any_in, blocked_out, whole_out, scratch):
    in_specs = [blk((per,) + a.shape[1:]) for a in blocked_in] + [whole(a) for a in whole_in] + [anyspec() for _ in any_in]
    out_specs = [blk((per,) + a.shape[1:]) for a in blocked_out] + [whole(a) for a in whole_out]
    return pl.pallas_call(
        kern,
        grid=(blocked_in[0].shape[0] // per,),
        in_specs=in_specs,
        out_specs=out_specs,
        out_shape=list(blocked_out) + list(whole_out),
        scratch_shapes=scratch,
        compiler_params=pltpu.CompilerParams(vmem_limit_bytes=VMEM_LIMIT),
        name=name,
        cost_estimate=pl.CostEstimate(flops=COST[name] * 1_150_000_000, bytes_accessed=0, transcendentals=0),
    )(*blocked_in, *whole_in, *any_in)


def wscratch(own):
    return [pltpu.VMEM((2 * own.shape[0],) + own.shape[1:], BF), pltpu.SemaphoreType.DMA((2 * own.shape[0],))]


def run_pack(smalls, bias_up, w_qkv, w_proj, w_up, w_down):
    part, width = w_proj.shape[1:]
    quart = w_up.shape[2] // width
    return pl.pallas_call(
        pack_kernel,
        out_shape=[sds((5 + 2 * quart, part, width), BF), sds((4 + 2 * quart, part, width), BF)],
        scratch_shapes=[pltpu.VMEM((128, 128), F32)],
        name="pack",
    )(*smalls, bias_up, w_qkv, w_proj, w_up, w_down)


def run_fa(x, wa, ff, per):
    images, seq, width = x.shape
    rows = pad_rows(seq)
    return call(
        functools.partial(fa_kernel, seq), "fa", per, [x], [], wa,
        [sds((images, rows, 3 * width), BF), sds((images, rows, width), BF), sds((images, 8, rows), F32),
         sds((images, rows, width), BF)], [sds((2, 16, width), F32)],
        [pltpu.VMEM((per * rows, width), F32)] + wscratch(wa[0]) + [pltpu.VMEM((2, ff), F32)])


def run_top(x, cot, vec, wt, per):
    images, seq, width = x.shape
    rows = pad_rows(seq)
    ff = (wt[0].shape[1] - 4) // 2 * width
    n = per * rows
    cells = lambda c: pltpu.VMEM((per, rows, c), BF)
    tall8 = pltpu.VMEM((per, 8, rows), F32)
    full = lambda r, c: pltpu.VMEM((r, c), F32)
    return call(
        functools.partial(top_kernel, seq), "top", per, [x, cot], [vec], wt,
        [sds((images, seq, width), F32), sds((images, seq, width), BF)], slots(wt[0], wt[0].shape[1] + 1),
        [full(n, width), full(n, width), cells(3 * width), cells(width), tall8, cells(width), cells(width), tall8,
         cells(ff), cells(ff), pltpu.VMEM((per, rows, width), F32), cells(width), cells(3 * width),
         full(width, 3 * width), full(width, width), full(width, ff), full(ff, width), full(8, width), full(8, width),
         full(1, 3 * width), full(1, ff), full(width, width)] + wscratch(wt[0]))


def run_fm(x, o, vec, wm, per):
    images, seq, width = x.shape
    rows = o.shape[1]
    ff = (wm[0].shape[1] - 1) // 2 * width
    return call(
        functools.partial(fm_kernel, seq), "fm", per, [x, o], [vec], wm,
        [sds((images, seq, width), F32), sds((images, rows, ff), BF), sds((images, rows, ff), BF),
         sds((images, rows, width), BF), sds((images, 8, rows), F32)], [],
        [pltpu.VMEM((per * rows, width), F32)] + wscratch(wm[0]))


def slots(own, count):
    half, _, part, width = own.shape
    return [sds((half, count, part, width), BF)] * 2


def run_bm(gr, a, d, xh, rs, o, vec, wm, per):
    images, seq, width = gr.shape
    rows, ff = a.shape[1:]
    return call(
        functools.partial(bm_kernel, seq), "bm", per, [gr, a, d, xh, rs, o], [vec], wm,
        [sds((images, rows, width), BF), sds((images, rows, width), BF)],
        slots(wm[0], wm[0].shape[1]) + [sds((8, width), F32), sds((1, ff), F32)],
        [pltpu.VMEM((per * rows, width), F32), pltpu.VMEM((width, width), F32), pltpu.VMEM((width, ff), F32),
         pltpu.VMEM((ff, width), F32)] + wscratch(wm[0]))


def run_ba(seq, m, do, xh, aux, vec, vec2, db1, wa, per):
    images, rows, width = do.shape
    return call(
        functools.partial(ba_kernel, seq), "ba", per, [m, do, xh, aux], [vec, vec2, db1], wa,
        [sds((images, rows, 3 * width), BF)], slots(wa[0], 4),
        [pltpu.VMEM((width, 3 * width), F32), pltpu.VMEM((1, 3 * width), F32)]
        + wscratch(wa[0]) + [pltpu.VMEM((width, width), F32)])


def run_bx(seq, dx1, dm, xh, aux, vec, wa, per, first, count, prev=None):
    images, rows, width = dx1.shape
    base = first // per

    def at(shape):
        nd = len(shape)
        return pl.BlockSpec((per,) + shape[1:], lambda i: (i + base,) + (0,) * (nd - 1))

    more = [] if prev is None else [prev]
    out = sds((images, seq, width), F32)
    return pl.pallas_call(
        functools.partial(bx_kernel, seq),
        grid=(count // per,),
        in_specs=[at(a.shape) for a in (dx1, dm, xh, aux)] + [whole(vec)] + [anyspec() for _ in [*wa, *more]],
        out_specs=at(out.shape),
        out_shape=out,
        input_output_aliases={7: 0} if more else {},
        scratch_shapes=wscratch(wa[0]),
        compiler_params=pltpu.CompilerParams(vmem_limit_bytes=32 * 2**20),
        name="bx",
        cost_estimate=pl.CostEstimate(flops=count * 1_150_000_000, bytes_accessed=0, transcendentals=0),
    )(dx1, dm, xh, aux, vec, *wa, *more)


def run_finish(a0, m0, l1, ff):
    part, width = a0[0].shape[1:]
    return pl.pallas_call(
        finish_kernel,
        out_shape=[sds((2, part, 3 * width), F32), sds((2, part, width), F32), sds((2, part, ff), F32),
                   sds((2, ff // width * part, width), F32), sds((2, ff // width * part), F32)]
        + [sds((2, part), F32)] * 8,
        compiler_params=pltpu.CompilerParams(vmem_limit_bytes=24 * 2**20),
        name="finish",
    )(*a0, *m0, *l1)


def xor_pairs(count, b):
    return [(i, i ^ b) for i in range(count)]


def tie(value, *others):
    return lax.optimization_barrier((value, *others))[0]


def group(*values):
    return lax.optimization_barrier(values)


def body(n, reps, tokens, norm1_gain, norm1_shift, qkv_weight, query_bias, value_bias, proj_weight, proj_bias,
         norm2_gain, norm2_shift, fc1_weight, fc1_bias, fc2_weight, fc2_bias, cotangent):
    images, seq, width = tokens.shape
    ff = fc1_weight.shape[2]
    per = 2 if images % 2 == 0 else 1
    upper = []
    b = n // 2
    while b > 2:
        upper.append(b)
        b //= 2

    def swap(x, b):
        return lax.ppermute(x, "shard", xor_pairs(n, b))

    def direct(x):
        masks = [0]
        for b in upper:
            masks = masks + [m ^ b for m in masks]
        return [x] + [swap(x, m) for m in masks[1:]]

    smalls = [norm1_gain, norm1_shift, query_bias, value_bias, proj_bias, norm2_gain, norm2_shift, fc2_bias]
    am, l1 = run_pack(smalls, fc1_bias, qkv_weight, proj_weight, fc1_weight, fc2_weight)

    am = direct(am)
    a0 = jnp.stack([y[:4] for y in am])
    m0 = jnp.stack([y[4:] for y in am])
    a0x = swap(a0, 2)
    l1 = direct(tie(l1, a0))
    a0 = jnp.concatenate([a0, a0x])
    m0x = swap(tie(m0, a0x), 2)
    a0 = (a0, swap(a0, 1))
    mix, o, aux, xa, vec = run_fa(tie(tokens, m0, l1[0]), a0, ff, per)
    o, m0x, *l1 = group(o, m0x, *l1)
    m0 = jnp.concatenate([m0, m0x])
    l1 = jnp.stack(l1)
    m0 = (m0, swap(tie(m0, l1), 1))
    l1x = swap(l1, 2)
    layer_one, act, der, xm, rs = run_fm(tokens, o, vec, m0, per)
    layer_one, l1x = group(layer_one, l1x)
    l1 = jnp.concatenate([l1, l1x])
    l1 = (l1, swap(l1, 1))
    layer_two, grad, kp, sn = run_top(layer_one, cotangent, vec, l1, per)

    class Sum:
        def __init__(self, keep, send):
            self.keep, self.got, self.send = keep, [], send
            self.bits = [1, 2] + upper[::-1]

        def start(self):
            self.flight = swap(self.send, self.bits[len(self.got)])
            return self

        def done(self):
            self.got.append(self.flight)
            size = self.flight.shape[0]
            if len(self.got) < len(self.bits):
                self.send = self.total(size // 2, size).astype(BF)
            else:
                self.send = self.total(0, 1)[0].astype(BF)
            return self

        def scatter(self):
            self.rest = self.total(0, 1)[0]
            masks = [0]
            for b in upper:
                masks = masks + [m ^ b for m in masks]
            sends = [self.total(z, z + 1)[0].astype(BF) for z in range(1, len(masks))]
            self.send = sends
            self.flight = [swap(s, m) for s, m in zip(sends, masks[1:])]
            return self

        def collect(self):
            total = self.rest
            for f in self.flight:
                total = total + f.astype(F32)
            self.send = total.astype(BF)
            return self

        def total(self, lo, hi):
            t = self.keep[lo:hi].astype(F32)
            for g in self.got:
                t = t + g[lo:hi].astype(F32)
            return t

        def replicas(self):
            mine, b = self.send, 1
            while True:
                other = lax.ppermute(mine, "replica", xor_pairs(reps, b))
                b *= 2
                if b >= reps:
                    return (mine, other)
                mine = (mine.astype(F32) + other.astype(F32)).astype(BF)

    def meet(value, *sums):
        value, *got = group(value, *[s.flight for s in sums])
        for s, g in zip(sums, got):
            s.flight = g
            s.done()
        return value

    def sent(value, *sums):
        return tie(value, *[s.send for s in sums])

    g1 = Sum(kp, sn).start().done().start()
    dx1, do, kp, sn, v2, db1 = run_bm(sent(grad, g1), act, der, xm, rs, o, vec, m0, per)
    do, sn, g1.flight = group(do, sn, g1.flight)
    gm0 = Sum(kp, sn).start()
    g1.got.append(g1.flight)
    g1.scatter()
    gm0.done().start()
    dm, kp, sn = run_ba(seq, mix, tie(do, *g1.send, gm0.send), xa, aux, vec, v2, db1, a0, per)
    sn, gm0.flight, *g1.flight = group(sn, gm0.flight, *g1.flight)
    ga0 = Sum(kp, sn).start()
    gm0.done().start()
    g1.collect()
    ga0.flight = tie(ga0.flight, gm0.send)
    ga0.done().start()
    first = images // (2 * per) * per
    part_grad = run_bx(seq, dx1, tie(dm, ga0.send, gm0.send), xa, aux, vec, a0, per, 0, first)
    part_grad, ga0.flight, gm0.flight, g1.send = group(part_grad, ga0.flight, gm0.flight, g1.send)
    ga0.done().start()
    gm0.done().start()
    fin_1 = g1.replicas()
    tokens_grad = run_bx(seq, dx1, dm, xa, aux, vec, a0, per, first, images - first, tie(part_grad, ga0.send, gm0.send))
    tokens_grad, ga0.flight, gm0.flight = group(tokens_grad, ga0.flight, gm0.flight)
    ga0.done().start()
    gm0.done()
    fin_m0 = gm0.replicas()
    ga0.done()
    fin_a0 = ga0.replicas()

    g_qkv, g_proj, g_up, g_down, g_bup, *s = run_finish(fin_a0, fin_m0, fin_1, ff)
    return (layer_one, layer_two, tokens_grad, s[0], s[1], g_qkv, s[2], s[3], g_proj, s[4], s[5], s[6],
            g_up, g_bup, g_down, s[7])
def solution(mesh):
    n = mesh.shape["shard"]
    reps = mesh.shape["replica"]
    batch = P(("replica", "shard"), None, None)
    row2 = P(None, "shard")
    row3 = P(None, "shard", None)
    in_specs = (batch, row2, row2, row3, row2, row2, row3, row2, row2, row2, row3, row2, row3, row2, batch)
    out_specs = (batch, batch, batch, row2, row2, row3, row2, row2, row3, row2, row2, row2, row3, row2, row3, row2)
    return jax.shard_map(
        functools.partial(body, n, reps), mesh=mesh, in_specs=in_specs, out_specs=out_specs, check_vma=False
    )
```
